32 devices in a mesh: dom: 8 (over z, core), repl: 4 (over y, x).
Axes of the slice: x: 2, y: 2, z: 4, core: 2. Of those that a mesh axis runs over, the one named last changes fastest.
Arguments:
- features: bfloat16 [8192, 512], P(('dom', 'repl')), may hold values from -6 to 6
- cotangent: bfloat16 [8192, 512], P(('dom', 'repl')), may hold values from -6 to 6
- weight: bfloat16 [512, 512], replicated, may hold values from -0.25 to 0.25
- tiles: bfloat16 [8, 4, 8, 16, 128, 128], P('dom', 'repl'), may hold values from -0.09375 to 0.09375
- tile_rows: int32 [8, 4, 8, 16], P('dom', 'repl'), may hold values from 0 to 7
- tile_cols: int32 [8, 4, 8, 16], P('dom', 'repl'), may hold values from 0 to 1
- tile_counts: int32 [8, 4, 8], P('dom', 'repl'), may hold values from 1 to 16, as said below
Outputs:
- activated: bfloat16 [8192, 512], P(('dom', 'repl'))
- feature_grad: bfloat16 [8192, 512], P(('dom', 'repl'))
- weight_grad: float32 [512, 512], replicated
The draws below stay inside these ranges and needn't reach their ends.
Inputs may be any that keep to these rules, and one draw needn't show every extreme that they name: `tile_counts`: live tiles of each row block, column group and column block; some entry equals 16 in every draw.
All inputs are finite; a program needn't handle non-finite values.
Results may differ from the reference program's by a relative error of at most 0.006.
Values may be sent and summed in bfloat16 or wider, within the bound.
No kernel may reach another device: no remote copies, remote signals or barrier semaphores. Data moves between devices by JAX's collectives and lax.ppermute only.
A program may use at most 64 MiB of HBM per device.

```python
import jax
import jax.numpy as jnp
from jax import lax

F = 512
TILE = 128
ROWS_DEV = 256
MAXT = 16
BLOCKS = 8
SUBS = 4
COLTILES = 2
ROWTILES = 8
VERTS = 8192


def draw_tile_counts(key, part):
    keys = jax.random.split(jax.random.fold_in(key, 17), 5)
    base = jax.random.randint(keys[0], (BLOCKS, SUBS, BLOCKS), 1, MAXT + 1)
    heavy = jax.random.randint(keys[1], (BLOCKS, 1, 1), 0, 4) == 0
    counts = jnp.where(heavy, MAXT, base)
    first = jax.random.randint(keys[2], (), 0, BLOCKS)
    second = jax.random.randint(keys[3], (), 0, SUBS)
    third = jax.random.randint(keys[4], (), 0, BLOCKS)
    counts = counts.at[first, second, third].set(MAXT)
    return counts.astype(jnp.int32)


def touch_ends(result, own_key, smallest, largest):
    longest = result.shape.index(max(result.shape))
    spots = []
    for shift in (0, 1):
        where = [jax.random.randint(jax.random.fold_in(own_key, axis), (), 0, length) for axis, length in enumerate(result.shape)]
        where[longest] = (where[longest] + shift) % result.shape[longest]
        spots.append(tuple(where))
    return result.at[spots[0]].set(smallest).at[spots[1]].set(largest)


def levels(key, dims, cuts, smallest, top_value):
    level = 1.0
    for position, parts in cuts:
        heights = jax.random.uniform(jax.random.fold_in(jax.random.fold_in(key, 6), position), (parts,), jnp.float32, smallest / len(cuts), top_value / len(cuts))
        level = level * jnp.repeat(jnp.exp(heights), dims[position] // parts).reshape((-1,) + (1,) * (len(dims) - 1 - position))
    return level


def scatter_about(stream_key, dims, scale, most, shards=(), held_as=jnp.bfloat16):
    entries = scale * jax.random.normal(stream_key, dims, jnp.float32)
    if shards:
        entries = entries * levels(stream_key, dims, shards, -0.22, 0.18)
    return jnp.clip(entries, -most, most).astype(held_as)


def setup_inputs(seed: int = 0) -> dict:
    streams_of = jax.random.split(jax.random.key(seed), 8)
    return {
        "features": scatter_about(streams_of[0], (VERTS, F), 1.0, 6.0, ((0, 32),)),
        "cotangent": scatter_about(streams_of[1], (VERTS, F), 1.0, 6.0, ((0, 32),)),
        "weight": scatter_about(streams_of[2], (F, F), F ** -0.5, 0.25),
        "tiles": scatter_about(streams_of[3], (BLOCKS, SUBS, BLOCKS, MAXT, TILE, TILE), (BLOCKS * MAXT * TILE * TILE // (2 * ROWS_DEV)) ** -0.5, 0.09375, ((0, 8), (1, 4))),
        "tile_rows": touch_ends(jax.random.randint(streams_of[4], (BLOCKS, SUBS, BLOCKS, MAXT), 0, ROWTILES), jax.random.fold_in(streams_of[4], 1), 0, ROWTILES - 1).astype(jnp.int32),
        "tile_cols": touch_ends(jax.random.randint(streams_of[5], (BLOCKS, SUBS, BLOCKS, MAXT), 0, COLTILES), jax.random.fold_in(streams_of[5], 1), 0, COLTILES - 1).astype(jnp.int32),
        "tile_counts": draw_tile_counts(jax.random.fold_in(streams_of[7], 71), 0),
    }


def silu_slope(preact):
    sig = jax.nn.sigmoid(preact)
    return sig * (1.0 + preact * (1.0 - sig))


def reference(features, cotangent, weight, tiles, tile_rows, tile_cols, tile_counts):
    nblk = BLOCKS
    ngrp = SUBS
    owners = features.reshape(nblk * ngrp, COLTILES, TILE, F)

    def live_slab(row_block, member, column):
        slab = tiles[row_block, member, column].astype(jnp.float32)
        alive = (jnp.arange(MAXT) < tile_counts[row_block, member, column]).astype(jnp.float32)
        return slab * alive[:, None, None]

    def forward_block(row_block):
        def visit(totals, pair):
            member = pair // nblk
            column = pair % nblk
            slab = live_slab(row_block, member, column)
            source = owners[column * ngrp + member]
            picked = source[tile_cols[row_block, member, column]].astype(jnp.float32)
            prod = jnp.einsum("tab,tbf->taf", slab, picked)
            return totals.at[tile_rows[row_block, member, column]].add(prod), None

        start = jnp.zeros((ROWTILES, TILE, F), jnp.float32)
        totals, _ = lax.scan(visit, start, jnp.arange(nblk * ngrp))
        return totals.reshape(ngrp * ROWS_DEV, F)

    aggregated = lax.map(forward_block, jnp.arange(nblk)).reshape(VERTS, F)
    agg_rounded = aggregated.astype(jnp.bfloat16)
    preact = jnp.dot(agg_rounded, weight, preferred_element_type=jnp.float32)
    activated = jax.nn.silu(preact).astype(jnp.bfloat16)
    pre_grad = (cotangent.astype(jnp.float32) * silu_slope(preact)).astype(jnp.bfloat16)
    weight_grad = jnp.dot(agg_rounded.T, pre_grad, preferred_element_type=jnp.float32) * (float(VERTS) ** -0.5)
    agg_grad = jnp.dot(pre_grad, weight.T, preferred_element_type=jnp.float32).astype(jnp.bfloat16)
    grad_tiles = agg_grad.reshape(nblk, ROWTILES, TILE, F)

    def backward_owner(owner):
        column = owner // ngrp
        member = owner % ngrp

        def visit(totals, row_block):
            slab = live_slab(row_block, member, column)
            picked = grad_tiles[row_block][tile_rows[row_block, member, column]].astype(jnp.float32)
            prod = jnp.einsum("tab,taf->tbf", slab, picked)
            return totals.at[tile_cols[row_block, member, column]].add(prod), None

        start = jnp.zeros((COLTILES, TILE, F), jnp.float32)
        totals, _ = lax.scan(visit, start, jnp.arange(nblk))
        return totals.reshape(ROWS_DEV, F)

    feature_grad = lax.map(backward_owner, jnp.arange(nblk * ngrp)).reshape(VERTS, F).astype(jnp.bfloat16)
    return (activated, feature_grad, weight_grad)
```

```python
import functools

import jax
import jax.numpy as jnp
from jax import lax
from jax.experimental import pallas as pl
from jax.experimental.pallas import tpu as pltpu
from jax.sharding import PartitionSpec as P

VMEM_LIMIT = 48 * 1024 * 1024


def exchange(x, axis, mask):
    return lax.ppermute(x, axis, [(i, i ^ mask) for i in range(lax.axis_size(axis))])


def params():
    return pltpu.CompilerParams(vmem_limit_bytes=VMEM_LIMIT)


def densify_kernel(rows_ref, cols_ref, counts_ref, place_ref, tiles_ref, a_ref, acc_ref, *, col_tiles, slots):
    step = pl.program_id(0)
    column = step ^ place_ref[0]
    member = place_ref[1]
    size = tiles_ref.shape[-1]
    acc_ref[...] = jnp.zeros_like(acc_ref)

    def add(slot, carry):
        row = rows_ref[column * slots + slot]
        row = ((row // col_tiles) ^ member) * col_tiles + lax.rem(row, col_tiles)
        spot = row * col_tiles + cols_ref[column * slots + slot]
        acc_ref[spot] += tiles_ref[0, slot].astype(jnp.float32)
        return carry

    lax.fori_loop(0, counts_ref[column], add, 0)
    for spot in range(acc_ref.shape[0]):
        row, col = spot // col_tiles, spot % col_tiles
        a_ref[0, row * size:(row + 1) * size, col * size:(col + 1) * size] = acc_ref[spot].astype(a_ref.dtype)


def densify(tiles, tile_rows, tile_cols, tile_counts, place, group_count, rows_local):
    columns, slots, size, _ = tiles.shape
    col_tiles = rows_local // size
    rows = group_count * rows_local
    return pl.pallas_call(
        functools.partial(densify_kernel, col_tiles=col_tiles, slots=slots),
        out_shape=jax.ShapeDtypeStruct((columns // 2, rows, 2 * rows_local), jnp.bfloat16),
        grid_spec=pltpu.PrefetchScalarGridSpec(
            num_scalar_prefetch=4,
            grid=(columns,),
            in_specs=[pl.BlockSpec((1, slots, size, size), lambda j, r, c, n, p: (j ^ p[0], 0, 0, 0))],
            out_specs=pl.BlockSpec((1, rows, rows_local), lambda j, r, c, n, p: (j // 2, 0, lax.rem(j, 2))),
            scratch_shapes=[pltpu.VMEM((group_count * col_tiles * col_tiles, size, size), jnp.float32)],
        ),
        compiler_params=params(),
        cost_estimate=pl.CostEstimate(flops=columns * slots * size * size, bytes_accessed=8 * rows * columns * rows_local, transcendentals=0),
        name="densify",
    )(tile_rows.reshape(-1), tile_cols.reshape(-1), tile_counts.reshape(-1), place, tiles)


def transpose_kernel(a_ref, out_ref):
    out_ref[0] = a_ref[0].T


def transposed(dense, rows_local):
    pairs, rows, _ = dense.shape
    return pl.pallas_call(
        transpose_kernel,
        out_shape=jax.ShapeDtypeStruct((2 * pairs, rows_local, rows), jnp.bfloat16),
        grid=(2 * pairs,),
        in_specs=[pl.BlockSpec((1, rows, rows_local), lambda j: (j // 2, 0, lax.rem(j, 2)))],
        out_specs=pl.BlockSpec((1, rows_local, rows), lambda j: (j, 0, 0)),
        compiler_params=params(),
        cost_estimate=pl.CostEstimate(flops=0, bytes_accessed=8 * pairs * rows * rows_local, transcendentals=0),
        name="transposed",
    )(dense)


def forward_kernel(*refs, pairs, has_prev):
    dense, sources = refs[:pairs], refs[pairs:3 * pairs]
    prev, out_ref = refs[3 * pairs:-1], refs[-1]
    half = sources[0].shape[0]
    total = prev[0][...] if has_prev else None
    for pair in range(pairs):
        for side in range(2):
            part = jnp.dot(
                dense[pair][0, :, side * half:(side + 1) * half], sources[2 * pair + side][...],
                preferred_element_type=jnp.float32,
            )
            total = part if total is None else total + part
    out_ref[...] = total.astype(out_ref.dtype)


def forward(dense, which, sources, prev, dtype):
    _, rows, depth = dense.shape
    half, width = sources[0].shape

    def block(pair):
        return pl.BlockSpec((1, half, depth), lambda k: (pair, k, 0))

    in_specs = [block(pair) for pair in which]
    in_specs += [pl.BlockSpec((half, width), lambda k: (0, 0)) for _ in sources]
    args = [dense] * len(which) + list(sources)
    if prev is not None:
        in_specs.append(pl.BlockSpec((half, width), lambda k: (k, 0)))
        args.append(prev)
    return pl.pallas_call(
        functools.partial(forward_kernel, pairs=len(which), has_prev=prev is not None),
        out_shape=jax.ShapeDtypeStruct((rows, width), dtype),
        grid=(rows // half,),
        in_specs=in_specs,
        out_specs=pl.BlockSpec((half, width), lambda k: (k, 0)),
        compiler_params=params(),
        cost_estimate=pl.CostEstimate(
            flops=2 * len(which) * rows * depth * width, bytes_accessed=2 * len(which) * rows * depth + 4 * rows * width,
            transcendentals=0),
        name="forward",
    )(*args)


def middle_kernel(place_ref, *refs, groups, part_rows):
    aggs, cots = refs[:groups], refs[groups:2 * groups]
    weight_ref = refs[2 * groups]
    act_ref = refs[2 * groups + 1]
    grads = refs[2 * groups + 2:3 * groups + 2]
    keep_ref, send_ref, part_ref = refs[3 * groups + 2:]
    member, core = place_ref[1], lax.rem(place_ref[0], 2)
    weight = weight_ref[...]
    total = None
    for k in range(groups):
        agg = aggs[k][...]
        preact = jnp.dot(agg, weight, preferred_element_type=jnp.float32)
        sigma = jax.nn.sigmoid(preact)
        if k == 0:
            act_ref[...] = (preact * sigma).astype(act_ref.dtype)
        slope = sigma * (1.0 + preact * (1.0 - sigma))
        pre_grad = (cots[k][...].astype(jnp.float32) * slope).astype(jnp.bfloat16)
        grads[k][...] = lax.dot_general(
            pre_grad, weight, (((1,), (1,)), ((), ())), preferred_element_type=jnp.float32
        ).astype(grads[k].dtype)
        if part_ref.shape[0] == part_rows:
            agg = aggs[k][:, pl.ds(pl.multiple_of(member * part_rows, part_rows), part_rows)]
        part = lax.dot_general(agg, pre_grad, (((0,), (0,)), ((), ())), preferred_element_type=jnp.float32)
        total = part if total is None else total + part
    part_ref[...] = total
    start = 0 if part_ref.shape[0] == part_rows else member * part_rows
    half = part_rows // 2
    keep_ref[...] = part_ref[pl.ds(pl.multiple_of(start + core * half, half), half), :]
    send_ref[...] = part_ref[pl.ds(pl.multiple_of(start + (1 - core) * half, half), half), :]


def middle(aggs, cots, weight, place):
    groups = len(aggs)
    rows, width = aggs[0].shape
    part_rows = width // groups
    whole = pl.BlockSpec(memory_space=pltpu.VMEM)
    scratch_rows = part_rows if part_rows % 128 == 0 else width
    out = pl.pallas_call(
        functools.partial(middle_kernel, groups=groups, part_rows=part_rows),
        out_shape=[jax.ShapeDtypeStruct((rows, width), jnp.bfloat16)] * (1 + groups)
        + [jax.ShapeDtypeStruct((part_rows // 2, width), jnp.float32)] * 2,
        in_specs=[pl.BlockSpec(memory_space=pltpu.SMEM)] + [whole] * (2 * groups + 1),
        out_specs=[whole] * (3 + groups),
        scratch_shapes=[pltpu.VMEM((scratch_rows, width), jnp.float32)],
        compiler_params=params(),
        cost_estimate=pl.CostEstimate(
            flops=2 * groups * rows * width * (2 * width + scratch_rows), bytes_accessed=6 * groups * rows * width,
            transcendentals=groups * rows * width),
        name="middle",
    )(place, *aggs, *cots, weight)
    return out[0], out[1:1 + groups], out[-2], out[-1]


def backward_kernel(*refs, groups):
    at_ref, grads, (own_ref, other_ref) = refs[0], refs[1:1 + groups], refs[1 + groups:]
    rows = grads[0].shape[0]
    for side, out_ref in ((1, other_ref), (0, own_ref)):
        total = None
        for k in range(groups):
            part = jnp.dot(
                at_ref[side, :, k * rows:(k + 1) * rows], grads[k][...], preferred_element_type=jnp.float32
            )
            total = part if total is None else total + part
        out_ref[...] = total.astype(out_ref.dtype)


def backward(dense_t, pair, grads):
    _, cols, rows = dense_t.shape
    groups = len(grads)
    rows_local, width = grads[0].shape
    return pl.pallas_call(
        functools.partial(backward_kernel, groups=groups),
        out_shape=[jax.ShapeDtypeStruct((cols, width), jnp.float32), jax.ShapeDtypeStruct((cols, width), jnp.bfloat16)],
        grid=(1,),
        in_specs=[pl.BlockSpec((2, cols, rows), lambda i: (pair, 0, 0))]
        + [pl.BlockSpec((rows_local, width), lambda i: (0, 0))] * groups,
        out_specs=[pl.BlockSpec((cols, width), lambda i: (0, 0))] * 2,
        compiler_params=params(),
        cost_estimate=pl.CostEstimate(
            flops=4 * cols * rows * width, bytes_accessed=4 * cols * rows + 2 * rows * width + 6 * cols * width,
            transcendentals=0),
        name="backward",
    )(dense_t, *grads)


def local(features, cotangent, weight, tiles, tile_rows, tile_cols, tile_counts):
    blocks = lax.axis_size("dom")
    groups = lax.axis_size("repl")
    pairs = blocks // 2
    rows_local, width = features.shape
    scale = float(rows_local * blocks * groups) ** (-0.5)
    position, member = lax.axis_index("dom"), lax.axis_index("repl")
    place = jnp.stack([position, member]).astype(jnp.int32)

    sources = {0: features}
    bit = blocks // 2
    while bit > 1:
        for j in list(sources):
            sources[j + bit] = exchange(sources[j], "dom", bit)
        bit //= 2
    for j in list(sources):
        sources[j + 1] = exchange(sources[j], "dom", 1)
    cots = [cotangent] + [exchange(cotangent, "repl", k) for k in range(1, groups)]

    dense = densify(tiles[0, 0], tile_rows, tile_cols, tile_counts, place, groups, rows_local)
    dense_t = transposed(dense, rows_local)

    early = list(range(pairs - 1))
    totals = forward(dense, early, [sources[j] for p in early for j in (2 * p, 2 * p + 1)], None, jnp.float32)
    last = pairs - 1
    partial = forward(dense, [last], [sources[2 * last], sources[2 * last + 1]], totals, jnp.bfloat16)

    def piece(k):
        return partial[k * rows_local:(k + 1) * rows_local]

    agg = piece(0).astype(jnp.float32)
    for k in range(1, groups):
        agg = agg + exchange(piece(k), "repl", k).astype(jnp.float32)
    agg_rounded = agg.astype(jnp.bfloat16)
    aggs = [agg_rounded] + [exchange(agg_rounded, "repl", k) for k in range(1, groups)]

    activated, grads, keep, send = middle(aggs, cots, weight, place)

    part = keep + exchange(send, "dom", 1)
    bit = 2
    while bit < blocks:
        part = part + exchange(part, "dom", bit)
        bit *= 2
    part = part * scale
    mine = jnp.stack([part] + [exchange(part, "repl", k) for k in range(1, groups)])
    both = jnp.concatenate([mine, exchange(mine, "dom", 1)])
    core = position % 2
    order = ((jnp.arange(2)[None, :] ^ core) * groups + (jnp.arange(groups)[:, None] ^ member)).reshape(-1)
    weight_grad = both[order].reshape(weight.shape)

    sums = {}
    for pair in reversed(range(pairs)):
        own, other = backward(dense_t, pair, grads)
        sums[pair] = own + exchange(other, "dom", 1).astype(jnp.float32)
    bit = 1
    while bit < pairs:
        for pair in sorted(sums, reverse=True):
            if pair & bit:
                arrived = exchange(sums.pop(pair).astype(jnp.bfloat16), "dom", 2 * bit)
                sums[pair ^ bit] = sums[pair ^ bit] + arrived.astype(jnp.float32)
        bit *= 2
    feature_grad = sums[0].astype(jnp.bfloat16)
    return (activated, feature_grad, weight_grad)


def solution(mesh):
    in_specs = (
        P(("dom", "repl"), None),
        P(("dom", "repl"), None),
        P(),
        P("dom", "repl", None, None, None, None),
        P("dom", "repl", None, None),
        P("dom", "repl", None, None),
        P("dom", "repl", None),
    )
    out_specs = (P(("dom", "repl"), None), P(("dom", "repl"), None), P())
    return jax.shard_map(local, mesh=mesh, in_specs=in_specs, out_specs=out_specs, check_vma=False)
```

```python
import functools

import jax
import jax.numpy as jnp
from jax import lax
from jax.experimental import pallas as pl
from jax.experimental.pallas import tpu as pltpu
from jax.sharding import PartitionSpec as P

WHOLE = pl.BlockSpec(memory_space=pltpu.VMEM)
SCALARS = pl.BlockSpec(memory_space=pltpu.SMEM)


def exchange(x, axis, mask):
    return lax.ppermute(x, axis, [(i, i ^ mask) for i in range(lax.axis_size(axis))])


def after(x, *others):
    return lax.optimization_barrier((x, *others))[0]


def params(mib):
    return pltpu.CompilerParams(vmem_limit_bytes=mib * 1024 * 1024)


def like(shape, dtype):
    return jax.ShapeDtypeStruct(shape, dtype)


def bf16_dot(a, b):
    return jnp.dot(a, b, preferred_element_type=jnp.float32)


def densify_kernel(rows_ref, cols_ref, counts_ref, place_ref, tiles_ref, a_ref, acc_ref, *, col_tiles, slots):
    step = pl.program_id(0)
    column = step ^ place_ref[0]
    member = place_ref[1]
    size = tiles_ref.shape[-1]
    acc_ref[...] = jnp.zeros_like(acc_ref)

    def add(slot, carry):
        row = rows_ref[column * slots + slot]
        row = ((row // col_tiles) ^ member) * col_tiles + lax.rem(row, col_tiles)
        spot = row * col_tiles + cols_ref[column * slots + slot]
        acc_ref[spot] += tiles_ref[0, slot].astype(jnp.float32)
        return carry

    lax.fori_loop(0, counts_ref[column], add, 0)
    for spot in range(acc_ref.shape[0]):
        row, col = spot // col_tiles, spot % col_tiles
        a_ref[0, row * size:(row + 1) * size, col * size:(col + 1) * size] = acc_ref[spot].astype(a_ref.dtype)


def densify(tiles, tile_rows, tile_cols, tile_counts, place, group_count, rows_local):
    columns, slots, size, _ = tiles.shape
    col_tiles = rows_local // size
    rows = group_count * rows_local
    return pl.pallas_call(
        functools.partial(densify_kernel, col_tiles=col_tiles, slots=slots),
        out_shape=like((columns, rows, rows_local), jnp.bfloat16),
        grid_spec=pltpu.PrefetchScalarGridSpec(
            num_scalar_prefetch=4,
            grid=(columns,),
            in_specs=[pl.BlockSpec((1, slots, size, size), lambda j, r, c, n, p: (j ^ p[0], 0, 0, 0))],
            out_specs=pl.BlockSpec((1, rows, rows_local), lambda j, r, c, n, p: (j, 0, 0)),
            scratch_shapes=[pltpu.VMEM((group_count * col_tiles * col_tiles, size, size), jnp.float32)],
        ),
        compiler_params=params(12),
        cost_estimate=pl.CostEstimate(
            flops=columns * slots * size * size, bytes_accessed=8 * rows * columns * rows_local, transcendentals=0),
        name="densify",
    )(tile_rows.reshape(-1), tile_cols.reshape(-1), tile_counts.reshape(-1), place, tiles)


def transpose_kernel(a_ref, out_ref):
    out_ref[0] = a_ref[0].T


def transposed(dense):
    columns, rows, cols = dense.shape
    return pl.pallas_call(
        transpose_kernel,
        out_shape=like((columns, cols, rows), jnp.bfloat16),
        grid=(columns,),
        in_specs=[pl.BlockSpec((1, rows, cols), lambda j: (j, 0, 0))],
        out_specs=pl.BlockSpec((1, cols, rows), lambda j: (j, 0, 0)),
        compiler_params=params(12),
        cost_estimate=pl.CostEstimate(flops=0, bytes_accessed=8 * columns * rows * cols, transcendentals=0),
        name="transposed",
    )(dense)


def forward_kernel(*refs, which, groups, has_prev):
    dense_ref, sources, rest = refs[0], refs[1:1 + len(which)], refs[1 + len(which):]
    prev = rest[:groups] if has_prev else None
    outs = rest[groups if has_prev else 0:]
    rows = sources[0].shape[0]
    for k in range(groups):
        total = prev[k][...] if has_prev else None
        for j, source in zip(which, sources):
            part = bf16_dot(dense_ref[j, k * rows:(k + 1) * rows, :], source[...])
            total = part if total is None else total + part
        outs[k][...] = total.astype(outs[k].dtype)


def forward(dense, which, sources, prev, dtypes):
    groups = len(dtypes)
    rows, width = sources[0].shape
    return pl.pallas_call(
        functools.partial(forward_kernel, which=which, groups=groups, has_prev=prev is not None),
        out_shape=[like((rows, width), dtype) for dtype in dtypes],
        in_specs=[WHOLE] * (1 + len(which) + (groups if prev is not None else 0)),
        out_specs=[WHOLE] * groups,
        compiler_params=params(8),
        cost_estimate=pl.CostEstimate(
            flops=2 * len(which) * groups * rows * rows * width,
            bytes_accessed=2 * len(which) * groups * rows * rows + 4 * groups * rows * width, transcendentals=0),
        name="forward",
    )(dense, *sources, *(prev or []))


def middle_kernel(*refs, groups):
    pieces, cot_ref, weight_ref = refs[:groups], refs[groups], refs[groups + 1]
    act_ref, agg_ref, pre_grad_ref, grad_ref = refs[groups + 2:]
    agg = pieces[0][...]
    for piece in pieces[1:]:
        agg = agg + piece[...].astype(jnp.float32)
    agg = agg.astype(jnp.bfloat16)
    agg_ref[...] = agg
    weight = weight_ref[...]
    preact = bf16_dot(agg, weight)
    sigma = jax.nn.sigmoid(preact)
    act_ref[...] = (preact * sigma).astype(act_ref.dtype)
    slope = sigma * (1.0 + preact * (1.0 - sigma))
    pre_grad = (cot_ref[...].astype(jnp.float32) * slope).astype(jnp.bfloat16)
    pre_grad_ref[...] = pre_grad
    grad_ref[...] = lax.dot_general(
        pre_grad, weight, (((1,), (1,)), ((), ())), preferred_element_type=jnp.float32
    ).astype(grad_ref.dtype)


def middle(pieces, cotangent, weight):
    rows, width = cotangent.shape
    return pl.pallas_call(
        functools.partial(middle_kernel, groups=len(pieces)),
        out_shape=[like((rows, width), jnp.bfloat16)] * 4,
        in_specs=[WHOLE] * (2 + len(pieces)),
        out_specs=[WHOLE] * 4,
        compiler_params=params(8),
        cost_estimate=pl.CostEstimate(
            flops=4 * rows * width * width, bytes_accessed=10 * rows * width, transcendentals=rows * width),
        name="middle",
    )(*pieces, cotangent, weight)


def weight_kernel(place_ref, agg_ref, pre_grad_ref, own_ref, *rest, groups):
    sends, part_ref = rest[:-1], rest[-1]
    member = place_ref[1]
    rows = own_ref.shape[0]
    part_ref[...] = lax.dot_general(
        agg_ref[...], pre_grad_ref[...], (((0,), (0,)), ((), ())), preferred_element_type=jnp.float32
    )
    for k in range(groups):
        out = own_ref if k == 0 else sends[k - 1]
        out[...] = part_ref[pl.ds(pl.multiple_of((member ^ k) * rows, rows), rows), :].astype(out.dtype)


def weight_part(agg, pre_grad, place, groups):
    rows, width = agg.shape
    part = (width // groups, width)
    return pl.pallas_call(
        functools.partial(weight_kernel, groups=groups),
        out_shape=[like(part, jnp.float32)] + [like(part, jnp.bfloat16)] * (groups - 1),
        in_specs=[SCALARS, WHOLE, WHOLE],
        out_specs=[WHOLE] * groups,
        scratch_shapes=[pltpu.VMEM((width, width), jnp.float32)],
        compiler_params=params(8),
        cost_estimate=pl.CostEstimate(
            flops=2 * rows * width * width, bytes_accessed=4 * rows * width + 4 * width * width, transcendentals=0),
        name="weight_part",
    )(place, agg, pre_grad)


def backward_kernel(*refs, pair, groups):
    at_ref, grads, (own_ref, other_ref) = refs[0], refs[1:1 + groups], refs[1 + groups:]
    rows = grads[0].shape[0]
    for side, out_ref in ((1, other_ref), (0, own_ref)):
        total = None
        for k in range(groups):
            part = bf16_dot(at_ref[2 * pair + side, :, k * rows:(k + 1) * rows], grads[k][...])
            total = part if total is None else total + part
        out_ref[...] = total.astype(out_ref.dtype)


def backward(dense_t, pair, grads):
    _, cols, rows = dense_t.shape
    width = grads[0].shape[1]
    return pl.pallas_call(
        functools.partial(backward_kernel, pair=pair, groups=len(grads)),
        out_shape=[like((cols, width), jnp.float32), like((cols, width), jnp.bfloat16)],
        in_specs=[WHOLE] * (1 + len(grads)),
        out_specs=[WHOLE] * 2,
        compiler_params=params(8),
        cost_estimate=pl.CostEstimate(
            flops=4 * cols * rows * width, bytes_accessed=4 * cols * rows + 2 * rows * width + 6 * cols * width,
            transcendentals=0),
        name="backward",
    )(dense_t, *grads)


def local(features, cotangent, weight, tiles, tile_rows, tile_cols, tile_counts):
    blocks = lax.axis_size("dom")
    groups = lax.axis_size("repl")
    pairs = blocks // 2
    rows_local, width = features.shape
    scale = float(rows_local * blocks * groups) ** (-0.5)
    position, member = lax.axis_index("dom"), lax.axis_index("repl")
    place = jnp.stack([position, member]).astype(jnp.int32)

    dense = densify(tiles[0, 0], tile_rows, tile_cols, tile_counts, place, groups, rows_local)

    sources = {0: features}
    bit = pairs // 2
    while bit:
        for j in list(sources):
            given = sources[j] if j == 0 else after(sources[j], dense)
            sources[j + 2 * bit] = exchange(given, "dom", 2 * bit)
        bit //= 2
    for j in list(sources):
        sources[j + 1] = exchange(sources[j], "dom", 1)

    early, late = list(range(blocks - 2)), [blocks - 2, blocks - 1]
    totals = forward(dense, early, [sources[j] for j in early], None, [jnp.float32] * groups)
    pieces = forward(
        dense, late, [sources[j] for j in late], totals, [jnp.float32] + [jnp.bfloat16] * (groups - 1))

    arrived = [exchange(pieces[k], "repl", k) for k in range(1, groups)]
    dense_t = transposed(after(dense, *pieces))
    arrived[-1] = after(arrived[-1], dense_t)
    activated, agg, pre_grad, grad = middle([pieces[0]] + arrived, cotangent, weight)
    grads = [grad] + [exchange(grad, "repl", k) for k in range(1, groups)]
    shares = weight_part(agg, pre_grad, place, groups)
    grads[-1] = after(grads[-1], *shares)

    partials = {pair: backward(dense_t, pair, grads) for pair in reversed(range(pairs))}
    swapped = {}
    last = None
    for pair in reversed(range(pairs)):
        own, other = partials[pair]
        swapped[pair] = exchange(other, "dom", 1)
    sums = {pair: partials[pair][0] + swapped[pair].astype(jnp.float32) for pair in swapped}
    bit = 1
    while bit < pairs:
        for pair in sorted(sums, reverse=True):
            if pair & bit:
                given = sums.pop(pair).astype(jnp.bfloat16)
                if last is not None:
                    given = after(given, last)
                last = exchange(given, "dom", 2 * bit)
                sums[pair ^ bit] = sums[pair ^ bit] + last.astype(jnp.float32)
                if bit == 1 and pair == pairs - 1:
                    first_sum, first_received = given, last
        bit *= 2
    feature_grad = sums[0].astype(jnp.bfloat16)

    part = shares[0]
    for k in range(1, groups):
        part = part + exchange(after(shares[k], first_sum), "repl", k).astype(jnp.float32)
    part = after(part, first_received)
    core = position % 2
    part = part.reshape(2, -1, width)
    part = lax.dynamic_index_in_dim(part, core, 0, False) + exchange(
        lax.dynamic_index_in_dim(part, 1 - core, 0, False).astype(jnp.bfloat16), "dom", 1).astype(jnp.float32)
    part = part.astype(jnp.bfloat16)
    terms = [part.astype(jnp.float32)]
    terms += [exchange(part, "dom", 2 * k).astype(jnp.float32) for k in range(1, pairs)]
    while len(terms) > 1:
        terms = [terms[i] + terms[i + 1] for i in range(0, len(terms), 2)]
    part = terms[0] * scale
    mine = jnp.stack([part] + [exchange(part, "repl", k) for k in range(1, groups)])
    both = jnp.concatenate([mine, exchange(mine, "dom", 1)])
    order = ((jnp.arange(2)[None, :] ^ core) * groups + (jnp.arange(groups)[:, None] ^ member)).reshape(-1)
    weight_grad = both[order].reshape(weight.shape)
    return (activated, feature_grad, weight_grad)


def solution(mesh):
    in_specs = (
        P(("dom", "repl"), None),
        P(("dom", "repl"), None),
        P(),
        P("dom", "repl", None, None, None, None),
        P("dom", "repl", None, None),
        P("dom", "repl", None, None),
        P("dom", "repl", None),
    )
    out_specs = (P(("dom", "repl"), None), P(("dom", "repl"), None), P())
    return jax.shard_map(local, mesh=mesh, in_specs=in_specs, out_specs=out_specs, check_vma=False)
```

```python
import functools

import jax
import jax.numpy as jnp
from jax import lax
from jax.experimental import pallas as pl
from jax.experimental.pallas import tpu as pltpu
from jax.sharding import PartitionSpec as P

WHOLE = pl.BlockSpec(memory_space=pltpu.VMEM)
SCALARS = pl.BlockSpec(memory_space=pltpu.SMEM)
CHUNKS = 2


def exchange(x, axis, mask):
    return lax.ppermute(x, axis, [(i, i ^ mask) for i in range(lax.axis_size(axis))])


def after(x, *others):
    return lax.optimization_barrier((x, *others))[0]


def params(mib):
    return pltpu.CompilerParams(vmem_limit_bytes=mib * 1024 * 1024)


def like(shape, dtype):
    return jax.ShapeDtypeStruct(shape, dtype)


def bf16_dot(a, b):
    return jnp.dot(a, b, preferred_element_type=jnp.float32)


def densify_kernel(rows_ref, cols_ref, counts_ref, place_ref, tiles_ref, a_ref, acc_ref, *, col_tiles, slots):
    step = pl.program_id(0)
    column = step ^ place_ref[0]
    member = place_ref[1]
    size = tiles_ref.shape[-1]
    acc_ref[...] = jnp.zeros_like(acc_ref)

    def add(slot, carry):
        row = rows_ref[column * slots + slot]
        row = ((row // col_tiles) ^ member) * col_tiles + lax.rem(row, col_tiles)
        spot = row * col_tiles + cols_ref[column * slots + slot]
        acc_ref[spot] += tiles_ref[0, slot].astype(jnp.float32)
        return carry

    lax.fori_loop(0, counts_ref[column], add, 0)
    for spot in range(acc_ref.shape[0]):
        row, col = spot // col_tiles, spot % col_tiles
        a_ref[0, row * size:(row + 1) * size, col * size:(col + 1) * size] = acc_ref[spot].astype(a_ref.dtype)


def densify(tiles, tile_rows, tile_cols, tile_counts, place, group_count, rows_local):
    columns, slots, size, _ = tiles.shape
    col_tiles = rows_local // size
    rows = group_count * rows_local
    return pl.pallas_call(
        functools.partial(densify_kernel, col_tiles=col_tiles, slots=slots),
        out_shape=like((columns, rows, rows_local), jnp.bfloat16),
        grid_spec=pltpu.PrefetchScalarGridSpec(
            num_scalar_prefetch=4,
            grid=(columns,),
            in_specs=[pl.BlockSpec((1, slots, size, size), lambda j, r, c, n, p: (j ^ p[0], 0, 0, 0))],
            out_specs=pl.BlockSpec((1, rows, rows_local), lambda j, r, c, n, p: (j, 0, 0)),
            scratch_shapes=[pltpu.VMEM((group_count * col_tiles * col_tiles, size, size), jnp.float32)],
        ),
        compiler_params=params(12),
        cost_estimate=pl.CostEstimate(
            flops=columns * slots * size * size, bytes_accessed=8 * rows * columns * rows_local, transcendentals=0),
        name="densify",
    )(tile_rows.reshape(-1), tile_cols.reshape(-1), tile_counts.reshape(-1), place, tiles)


def transpose_kernel(a_ref, *outs):
    for pair, out_ref in enumerate(outs):
        for side in range(2):
            out_ref[side] = a_ref[2 * pair + side].T


def transposed(dense):
    columns, rows, cols = dense.shape
    return pl.pallas_call(
        transpose_kernel,
        out_shape=[like((2, cols, rows), jnp.bfloat16)] * (columns // 2),
        in_specs=[WHOLE],
        out_specs=[WHOLE] * (columns // 2),
        compiler_params=params(8),
        cost_estimate=pl.CostEstimate(flops=0, bytes_accessed=4 * columns * rows * cols, transcendentals=0),
        name="transposed",
    )(dense)


def forward_kernel(*refs, which, starts, groups, has_prev):
    dense_ref, sources, rest = refs[0], refs[1:1 + len(which)], refs[1 + len(which):]
    prev = rest[:groups] if has_prev else None
    outs = rest[groups if has_prev else 0:]
    rows, width = outs[0].shape
    for k in range(groups):
        total = prev[k][...] if has_prev else None
        for j, start, source in zip(which, starts, sources):
            part = bf16_dot(dense_ref[j, k * rows:(k + 1) * rows, :], source[:, start:start + width])
            total = part if total is None else total + part
        outs[k][...] = total.astype(outs[k].dtype)


def forward(dense, which, sources, start, width, prev, dtypes):
    groups = len(dtypes)
    rows = sources[0].shape[0]
    starts = [0 if source.shape[1] == width else start for source in sources]
    return pl.pallas_call(
        functools.partial(forward_kernel, which=which, starts=starts, groups=groups, has_prev=prev is not None),
        out_shape=[like((rows, width), dtype) for dtype in dtypes],
        in_specs=[WHOLE] * (1 + len(which) + (groups if prev is not None else 0)),
        out_specs=[WHOLE] * groups,
        compiler_params=params(8),
        cost_estimate=pl.CostEstimate(
            flops=2 * len(which) * groups * rows * rows * width,
            bytes_accessed=2 * len(which) * groups * rows * rows + 4 * groups * rows * width, transcendentals=0),
        name="forward",
    )(dense, *sources, *(prev or []))


def middle_kernel(*refs, chunks, groups):
    pieces = refs[:chunks * groups]
    cot_ref, weight_ref = refs[chunks * groups:chunks * groups + 2]
    act_ref, agg_ref, pre_grad_ref = refs[chunks * groups + 2:chunks * groups + 5]
    grads = refs[chunks * groups + 5:]
    part = grads[0].shape[1]
    for c in range(chunks):
        agg = pieces[c * groups][...]
        for k in range(1, groups):
            agg = agg + pieces[c * groups + k][...].astype(jnp.float32)
        agg_ref[:, c * part:(c + 1) * part] = agg.astype(jnp.bfloat16)
    weight = weight_ref[...]
    preact = bf16_dot(agg_ref[...], weight)
    sigma = jax.nn.sigmoid(preact)
    act_ref[...] = (preact * sigma).astype(act_ref.dtype)
    slope = sigma * (1.0 + preact * (1.0 - sigma))
    pre_grad = (cot_ref[...].astype(jnp.float32) * slope).astype(jnp.bfloat16)
    pre_grad_ref[...] = pre_grad
    for c in range(chunks):
        grads[c][...] = lax.dot_general(
            pre_grad, weight_ref[c * part:(c + 1) * part, :], (((1,), (1,)), ((), ())),
            preferred_element_type=jnp.float32,
        ).astype(jnp.bfloat16)


def middle(pieces, cotangent, weight):
    rows, width = cotangent.shape
    chunks = len(pieces)
    whole = like((rows, width), jnp.bfloat16)
    return pl.pallas_call(
        functools.partial(middle_kernel, chunks=chunks, groups=len(pieces[0])),
        out_shape=[whole] * 3 + [like((rows, width // chunks), jnp.bfloat16)] * chunks,
        in_specs=[WHOLE] * (2 + chunks * len(pieces[0])),
        out_specs=[WHOLE] * (3 + chunks),
        compiler_params=params(8),
        cost_estimate=pl.CostEstimate(
            flops=4 * rows * width * width, bytes_accessed=10 * rows * width, transcendentals=rows * width),
        name="middle",
    )(*[piece for chunk in pieces for piece in chunk], cotangent, weight)


def weight_kernel(place_ref, agg_ref, pre_grad_ref, own_ref, send_ref, part_ref):
    core, member = lax.rem(place_ref[0], 2), place_ref[1]
    groups, rows, _ = own_ref.shape
    part_ref[...] = lax.dot_general(
        agg_ref[...], pre_grad_ref[...], (((0,), (0,)), ((), ())), preferred_element_type=jnp.float32
    )
    for k in range(groups):
        for side, out_ref in ((core, own_ref), (1 - core, send_ref)):
            start = ((member ^ k) * 2 + side) * rows
            out_ref[k] = part_ref[pl.ds(pl.multiple_of(start, rows), rows), :].astype(out_ref.dtype)


def weight_part(agg, pre_grad, place, groups):
    rows, width = agg.shape
    part = (groups, width // (2 * groups), width)
    return pl.pallas_call(
        weight_kernel,
        out_shape=[like(part, jnp.float32), like(part, jnp.bfloat16)],
        in_specs=[SCALARS, WHOLE, WHOLE],
        out_specs=[WHOLE] * 2,
        scratch_shapes=[pltpu.VMEM((width, width), jnp.float32)],
        compiler_params=params(8),
        cost_estimate=pl.CostEstimate(
            flops=2 * rows * width * width, bytes_accessed=4 * rows * width + 4 * width * width, transcendentals=0),
        name="weight_part",
    )(place, agg, pre_grad)


def place_kernel(place_ref, *refs, groups):
    mine, other_ref, out_ref = refs[:groups], refs[groups], refs[groups + 1]
    core, member = lax.rem(place_ref[0], 2), place_ref[1]
    rows = mine[0].shape[0]
    for k in range(groups):
        for side, value in ((core, mine[k][...]), (1 - core, other_ref[k * rows:(k + 1) * rows, :])):
            start = ((member ^ k) * 2 + side) * rows
            out_ref[pl.ds(pl.multiple_of(start, rows), rows), :] = value


def place_slices(mine, other, place):
    groups = len(mine)
    rows, width = mine[0].shape
    return pl.pallas_call(
        functools.partial(place_kernel, groups=groups),
        out_shape=like((2 * groups * rows, width), jnp.float32),
        in_specs=[SCALARS] + [WHOLE] * (groups + 1),
        out_specs=WHOLE,
        compiler_params=params(8),
        cost_estimate=pl.CostEstimate(flops=0, bytes_accessed=16 * groups * rows * width, transcendentals=0),
        name="place_slices",
    )(place, *mine, other)


def backward_kernel(*refs, count, groups):
    blocks, grads = refs[:count], refs[count:count + groups]
    owns, other_ref = refs[count + groups:-1], refs[-1]
    rows = grads[0].shape[0]
    for pair in range(count):
        for side in (1, 0):
            total = None
            for k in range(groups):
                part = bf16_dot(blocks[pair][side, :, k * rows:(k + 1) * rows], grads[k][...])
                total = part if total is None else total + part
            if side == 0:
                owns[pair][...] = total
            else:
                size = total.shape[0]
                other_ref[pair * size:(pair + 1) * size, :] = total.astype(other_ref.dtype)


def backward(blocks, grads):
    _, cols, rows = blocks[0].shape
    width = grads[0].shape[1]
    count = len(blocks)
    out = pl.pallas_call(
        functools.partial(backward_kernel, count=count, groups=len(grads)),
        out_shape=[like((cols, width), jnp.float32)] * count + [like((count * cols, width), jnp.bfloat16)],
        in_specs=[WHOLE] * (count + len(grads)),
        out_specs=[WHOLE] * (count + 1),
        compiler_params=params(8),
        cost_estimate=pl.CostEstimate(
            flops=4 * count * cols * rows * width,
            bytes_accessed=4 * count * cols * rows + 2 * rows * width + 6 * count * cols * width, transcendentals=0),
        name="backward",
    )(*blocks, *grads)
    return out[:-1], out[-1]


def local(features, cotangent, weight, tiles, tile_rows, tile_cols, tile_counts):
    blocks = lax.axis_size("dom")
    groups = lax.axis_size("repl")
    pairs = blocks // 2
    rows_local, width = features.shape
    part_width = width // CHUNKS
    scale = float(rows_local * blocks * groups) ** (-0.5)
    position, member = lax.axis_index("dom"), lax.axis_index("repl")
    place = jnp.stack([position, member]).astype(jnp.int32)

    dense = densify(tiles[0, 0], tile_rows, tile_cols, tile_counts, place, groups, rows_local)

    top = pairs // 2
    near = {0: features}
    bit = top // 2
    while bit:
        for pair in list(near):
            near[pair + bit] = exchange(near[pair], "dom", 2 * bit)
        bit //= 2
    near = {pair: (near[pair], exchange(near[pair], "dom", 1)) for pair in near}
    fronts = []
    for c in range(CHUNKS):
        given = features[:, c * part_width:(c + 1) * part_width]
        fronts.append(exchange(given, "dom", 2 * top))
    pieces, arrived = [], []
    for c in range(CHUNKS):
        ready = [far[pairs - 1][0]] if c else [dense]
        far = {top: fronts[c]}
        bit = top // 2
        while bit:
            for pair in list(far):
                far[pair + bit] = exchange(after(far[pair], *ready), "dom", 2 * bit)
            bit //= 2
        if c:
            far[pairs - 1] = after(far[pairs - 1], *pieces[-1])
        far = {pair: (far[pair], exchange(far[pair], "dom", 1)) for pair in far}
        sources = {**near, **far}
        order = list(range(pairs - 1))
        totals = forward(
            dense, [2 * pair + side for pair in order for side in range(2)],
            [sources[pair][side] for pair in order for side in range(2)],
            c * part_width, part_width, None, [jnp.float32] * groups)
        out = forward(
            dense, [2 * pairs - 2, 2 * pairs - 1], list(sources[pairs - 1]), c * part_width, part_width, totals,
            [jnp.float32] + [jnp.bfloat16] * (groups - 1))
        pieces.append(out)
        arrived.append([exchange(out[k], "repl", k) for k in range(1, groups)])
    dense_t = transposed(after(dense, *pieces[-1], *arrived[0]))
    arrived[-1][-1] = after(arrived[-1][-1], *dense_t)

    out = middle([[out[0]] + got for out, got in zip(pieces, arrived)], cotangent, weight)
    activated, agg, pre_grad = out[:3]
    share, share_send = weight_part(agg, pre_grad, place, groups)
    share = share + exchange(share_send, "dom", 1).astype(jnp.float32)

    columns, mark = [], None
    for c in range(CHUNKS):
        grad = out[3 + c] if mark is None else after(out[3 + c], mark)
        grads = [grad] + [exchange(grad, "repl", k) for k in range(1, groups)]
        if c == 0:
            share = after(share, grads[-1])
            part = share[0]
            for k in range(1, groups):
                part = part + exchange(share[k].astype(jnp.bfloat16), "repl", k).astype(jnp.float32)
            part = part.astype(jnp.bfloat16)
        else:
            grads[-1] = after(grads[-1], follow)
        owns, others = {}, {}
        (owns[pairs - 1],), other_top = backward(dense_t[-1:], grads)
        mark = other_top
        rest, other = backward(dense_t[:-1], grads)
        others[pairs - 1] = exchange(other_top, "dom", 1)
        other = exchange(other, "dom", 1)
        for pair in range(pairs - 1):
            owns[pair] = rest[pair]
            others[pair] = other[pair * rows_local:(pair + 1) * rows_local]
        sums = {pair: owns[pair] + others[pair].astype(jnp.float32) for pair in owns}
        bit, last = 1, None
        while bit < pairs:
            for pair in sorted(sums, reverse=True):
                if not pair & bit:
                    continue
                given = sums.pop(pair).astype(jnp.bfloat16)
                first = pair == max([pair, *sums])
                if c == 0 and first:
                    given = jnp.concatenate([given] + [part[:, i * part_width:(i + 1) * part_width] for i in range(CHUNKS)])
                if c and first and bit == 1:
                    given = after(given, second)
                if c == 0:
                    if bit == 1 and first:
                        follow = given
                    elif bit > 1 and first:
                        second = given
                if last is not None and not first:
                    given = after(given, last)
                got = exchange(given, "dom", 2 * bit)
                if c == 0 and first:
                    high = part.shape[0]
                    got, slices = got[:rows_local], got[rows_local:]
                    slices = jnp.concatenate([slices[i * high:(i + 1) * high] for i in range(CHUNKS)], axis=1)
                    part = part.astype(jnp.float32) + slices.astype(jnp.float32)
                    if 2 * bit < pairs:
                        part = part.astype(jnp.bfloat16)
                last = got
                sums[pair ^ bit] = sums[pair ^ bit] + got.astype(jnp.float32)
            bit *= 2
        columns.append(sums[0].astype(jnp.bfloat16))
    feature_grad = jnp.concatenate(columns, axis=1)

    part = part * scale
    mine = [part] + [exchange(part, "repl", k) for k in range(1, groups)]
    other = exchange(jnp.concatenate(mine), "dom", 1)
    weight_grad = place_slices(mine, other, place)
    return (activated, feature_grad, weight_grad)


def solution(mesh):
    in_specs = (
        P(("dom", "repl"), None),
        P(("dom", "repl"), None),
        P(),
        P("dom", "repl", None, None, None, None),
        P("dom", "repl", None, None),
        P("dom", "repl", None, None),
        P("dom", "repl", None),
    )
    out_specs = (P(("dom", "repl"), None), P(("dom", "repl"), None), P())
    return jax.shard_map(local, mesh=mesh, in_specs=in_specs, out_specs=out_specs, check_vma=False)
```

```python
import functools

import jax
import jax.numpy as jnp
import numpy as np
from jax import lax
from jax.experimental import pallas as pl
from jax.experimental.pallas import tpu as pltpu
from jax.sharding import PartitionSpec as P

WHOLE = pl.BlockSpec(memory_space=pltpu.VMEM)
SCALARS = pl.BlockSpec(memory_space=pltpu.SMEM)
CHUNKS = 1


def bit_count(n):
    return n.bit_length() - 1


def bit_order(core, bits):
    return list(range(bits))[::-1] if core else list(range(bits))


def slot_mask(slot, core, bits):
    mask = 0
    for i, bit in enumerate(bit_order(core, bits)):
        mask |= ((slot >> (bits - 1 - i)) & 1) << bit
    return mask


def swap_cores(x):
    return lax.ppermute(x, "dom", [(i, i ^ 1) for i in range(lax.axis_size("dom"))])


def swap_chips(x, held):
    blocks = lax.axis_size("dom")
    bits = bit_count(blocks // 2)
    return lax.ppermute(x, "dom", [(i, i ^ (2 * slot_mask(held, i % 2, bits))) for i in range(blocks)])


def swap_members(x, held):
    blocks, groups = lax.axis_size("dom"), lax.axis_size("repl")
    bits = bit_count(groups)
    pairs = []
    for i in range(blocks):
        for j in range(groups):
            pairs.append((i * groups + j, i * groups + (j ^ slot_mask(held, i % 2, bits))))
    return lax.ppermute(x, ("dom", "repl"), pairs)


def after(x, *others):
    return lax.optimization_barrier((x, *others))[0]


def params(mib):
    return pltpu.CompilerParams(vmem_limit_bytes=mib * 1024 * 1024)


def like(shape, dtype):
    return jax.ShapeDtypeStruct(shape, dtype)


def bf16_dot(a, b):
    return jnp.dot(a, b, preferred_element_type=jnp.float32)


def tables(blocks, groups):
    bits = bit_count(blocks // 2)
    column = np.zeros((blocks, blocks), np.int32)
    for position in range(blocks):
        for j in range(blocks):
            core = (position % 2) ^ (j % 2)
            column[position, j] = ((position // 2) ^ slot_mask(j // 2, core, bits)) * 2 + core
    bits = bit_count(groups)
    slot = np.zeros((2, groups, groups), np.int32)
    for core in range(2):
        for member in range(groups):
            for k in range(groups):
                slot[core, member, member ^ slot_mask(k, core, bits)] = k
    return jnp.asarray(column), jnp.asarray(slot.reshape(2, -1))


def densify_kernel(rows_ref, cols_ref, counts_ref, column_ref, slot_ref, place_ref, tiles_ref, a_ref, acc_ref, *, col_tiles):
    position, member = place_ref[0], place_ref[1]
    column = column_ref[position, pl.program_id(0)]
    core = lax.rem(position, 2)
    size = tiles_ref.shape[-1]
    groups = acc_ref.shape[0] // (col_tiles * col_tiles)
    acc_ref[...] = jnp.zeros_like(acc_ref)

    def add(tile, carry):
        row = rows_ref[0, 0, column, tile]
        row = slot_ref[core, member * groups + row // col_tiles] * col_tiles + lax.rem(row, col_tiles)
        spot = row * col_tiles + cols_ref[0, 0, column, tile]
        acc_ref[spot] += tiles_ref[0, tile].astype(jnp.float32)
        return carry

    lax.fori_loop(0, counts_ref[0, 0, column], add, 0)
    for spot in range(acc_ref.shape[0]):
        row, col = spot // col_tiles, spot % col_tiles
        a_ref[0, row * size:(row + 1) * size, col * size:(col + 1) * size] = acc_ref[spot].astype(a_ref.dtype)


def densify(tiles, tile_rows, tile_cols, tile_counts, column, slot, place, group_count, rows_local):
    columns, count, size, _ = tiles.shape
    col_tiles = rows_local // size
    rows = group_count * rows_local
    return pl.pallas_call(
        functools.partial(densify_kernel, col_tiles=col_tiles),
        out_shape=like((columns, rows, rows_local), jnp.bfloat16),
        grid_spec=pltpu.PrefetchScalarGridSpec(
            num_scalar_prefetch=6,
            grid=(columns,),
            in_specs=[pl.BlockSpec((1, count, size, size), lambda j, r, c, n, column, slot, p: (column[p[0], j], 0, 0, 0))],
            out_specs=pl.BlockSpec((1, rows, rows_local), lambda j, *_: (j, 0, 0)),
            scratch_shapes=[pltpu.VMEM((group_count * col_tiles * col_tiles, size, size), jnp.float32)],
        ),
        compiler_params=params(12),
        cost_estimate=pl.CostEstimate(
            flops=columns * count * size * size, bytes_accessed=8 * rows * columns * rows_local, transcendentals=0),
        name="densify",
    )(tile_rows, tile_cols, tile_counts, column, slot, place, tiles)


def transpose_kernel(a_ref, *outs):
    part = outs[0].shape[0]
    for i, out_ref in enumerate(outs):
        for j in range(part):
            out_ref[j] = a_ref[i * part + j].T


def transposed(dense):
    columns, rows, cols = dense.shape
    return pl.pallas_call(
        transpose_kernel,
        out_shape=[like((columns // 2, cols, rows), jnp.bfloat16)] * 2,
        in_specs=[WHOLE],
        out_specs=[WHOLE] * 2,
        compiler_params=params(8),
        cost_estimate=pl.CostEstimate(flops=0, bytes_accessed=4 * columns * rows * cols, transcendentals=0),
        name="transposed",
    )(dense)


def forward_kernel(*refs, first, pieces, has_prev):
    dense_ref, sources = refs[0], refs[1:1 + len(pieces)]
    rest = refs[1 + len(pieces):]
    prev, outs = (rest[:2], rest[2:]) if has_prev else (None, rest)
    half, width = outs[0].shape
    rows = dense_ref.shape[2]
    for i, out_ref in enumerate(outs):
        for k in range(half // rows):
            total = prev[i][k * rows:(k + 1) * rows, :] if has_prev else None
            start = i * half + k * rows
            for j, (row, col) in enumerate(pieces):
                part = bf16_dot(
                    dense_ref[first + j, start:start + rows, :], sources[j][row:row + rows, col:col + width])
                total = part if total is None else total + part
            out_ref[k * rows:(k + 1) * rows, :] = total.astype(out_ref.dtype)


def forward(dense, first, sources, width, prev, dtypes):
    _, rows, _ = dense.shape
    arrays = [source[0] for source in sources]
    return pl.pallas_call(
        functools.partial(
            forward_kernel, first=first, pieces=[source[1:] for source in sources], has_prev=prev is not None),
        out_shape=[like((rows // 2, width), dtype) for dtype in dtypes],
        in_specs=[WHOLE] * (1 + len(arrays) + (2 if prev is not None else 0)),
        out_specs=[WHOLE] * 2,
        compiler_params=params(8),
        cost_estimate=pl.CostEstimate(
            flops=2 * len(arrays) * rows * dense.shape[2] * width,
            bytes_accessed=2 * len(arrays) * rows * dense.shape[2] + 4 * rows * width, transcendentals=0),
        name="forward",
    )(dense, *arrays, *(prev or []))


def middle_kernel(*refs, chunks):
    pieces = refs[:2 * chunks]
    cot_ref, weight_ref = refs[2 * chunks:2 * chunks + 2]
    act_ref, agg_ref, pre_grad_ref = refs[2 * chunks + 2:2 * chunks + 5]
    grads = refs[2 * chunks + 5:]
    part = grads[0].shape[1]
    for c in range(chunks):
        agg = pieces[2 * c][...] + pieces[2 * c + 1][...].astype(jnp.float32)
        agg_ref[:, c * part:(c + 1) * part] = agg.astype(jnp.bfloat16)
    preact = bf16_dot(agg_ref[...], weight_ref[...])
    sigma = jax.nn.sigmoid(preact)
    act_ref[...] = (preact * sigma).astype(act_ref.dtype)
    slope = sigma * (1.0 + preact * (1.0 - sigma))
    pre_grad = (cot_ref[...].astype(jnp.float32) * slope).astype(jnp.bfloat16)
    pre_grad_ref[...] = pre_grad
    for c in range(chunks):
        grads[c][...] = lax.dot_general(
            pre_grad, weight_ref[c * part:(c + 1) * part, :], (((1,), (1,)), ((), ())),
            preferred_element_type=jnp.float32,
        ).astype(jnp.bfloat16)


def middle(pieces, cotangent, weight):
    rows, width = cotangent.shape
    chunks = len(pieces)
    whole = like((rows, width), jnp.bfloat16)
    return pl.pallas_call(
        functools.partial(middle_kernel, chunks=chunks),
        out_shape=[whole] * 3 + [like((rows, width // chunks), jnp.bfloat16)] * chunks,
        in_specs=[WHOLE] * (2 + 2 * chunks),
        out_specs=[WHOLE] * (3 + chunks),
        compiler_params=params(8),
        cost_estimate=pl.CostEstimate(
            flops=4 * rows * width * width, bytes_accessed=10 * rows * width, transcendentals=rows * width),
        name="middle",
    )(*[piece for chunk in pieces for piece in chunk], cotangent, weight)


def weight_kernel(place_ref, slot_ref, agg_ref, pre_grad_ref, own_ref, send_ref, part_ref):
    core, member = lax.rem(place_ref[0], 2), place_ref[1]
    groups, rows, _ = own_ref.shape
    part_ref[...] = lax.dot_general(
        agg_ref[...], pre_grad_ref[...], (((0,), (0,)), ((), ())), preferred_element_type=jnp.float32
    )
    for k in range(groups):
        for side, out_ref in ((core, own_ref), (1 - core, send_ref)):
            out_ref[slot_ref[side, member * groups + k]] = part_ref[
                pl.ds(pl.multiple_of((2 * k + side) * rows, rows), rows), :].astype(out_ref.dtype)


def weight_part(agg, pre_grad, slot, place, groups):
    rows, width = agg.shape
    part = (groups, width // (2 * groups), width)
    return pl.pallas_call(
        weight_kernel,
        out_shape=[like(part, jnp.float32), like(part, jnp.bfloat16)],
        in_specs=[SCALARS, SCALARS, WHOLE, WHOLE],
        out_specs=[WHOLE] * 2,
        scratch_shapes=[pltpu.VMEM((width, width), jnp.float32)],
        compiler_params=params(8),
        cost_estimate=pl.CostEstimate(
            flops=2 * rows * width * width, bytes_accessed=4 * rows * width + 4 * width * width, transcendentals=0),
        name="weight_part",
    )(place, slot, agg, pre_grad)


def place_kernel(place_ref, slot_ref, own_ref, other_ref, out_ref):
    core, member = lax.rem(place_ref[0], 2), place_ref[1]
    groups, rows, _ = own_ref.shape
    for k in range(groups):
        for side, ref in ((core, own_ref), (1 - core, other_ref)):
            out_ref[pl.ds(pl.multiple_of((2 * k + side) * rows, rows), rows), :] = ref[slot_ref[side, member * groups + k]]


def place_slices(own, other, slot, place):
    groups, rows, width = own.shape
    return pl.pallas_call(
        place_kernel,
        out_shape=like((2 * groups * rows, width), jnp.float32),
        in_specs=[SCALARS, SCALARS, WHOLE, WHOLE],
        out_specs=WHOLE,
        compiler_params=params(8),
        cost_estimate=pl.CostEstimate(flops=0, bytes_accessed=16 * groups * rows * width, transcendentals=0),
        name="place_slices",
    )(place, slot, own, other)


def backward_kernel(at_ref, *refs):
    grads, (own_ref, other_ref) = refs[:-2], refs[-2:]
    columns, size, _ = at_ref.shape
    for i in list(range(1, columns, 2)) + list(range(0, columns, 2)):
        total, start = None, 0
        for grad in grads:
            stop = start + grad.shape[0]
            part = bf16_dot(at_ref[i, :, start:stop], grad[...])
            total, start = part if total is None else total + part, stop
        out_ref = other_ref if i % 2 else own_ref
        out_ref[(i // 2) * size:(i // 2 + 1) * size, :] = total.astype(out_ref.dtype)


def backward(dense_t, grads):
    columns, cols, rows = dense_t.shape
    width = grads[0].shape[1]
    half = columns // 2 * cols
    return pl.pallas_call(
        backward_kernel,
        out_shape=[like((half, width), jnp.float32), like((half, width), jnp.bfloat16)],
        in_specs=[WHOLE] * (1 + len(grads)),
        out_specs=[WHOLE] * 2,
        compiler_params=params(8),
        cost_estimate=pl.CostEstimate(
            flops=4 * half * rows * width, bytes_accessed=4 * half * rows + 2 * rows * width + 6 * half * width,
            transcendentals=0),
        name="backward",
    )(dense_t, *grads)


def finish_kernel(*refs):
    out_ref = refs[-1]
    width = refs[0].shape[1]
    for c in range(len(refs) // 2):
        total = refs[2 * c][...] + refs[2 * c + 1][...].astype(jnp.float32)
        out_ref[:, c * width:(c + 1) * width] = total.astype(out_ref.dtype)


def finish(parts):
    rows, width = parts[0].shape
    width *= len(parts) // 2
    return pl.pallas_call(
        finish_kernel,
        out_shape=like((rows, width), jnp.bfloat16),
        in_specs=[WHOLE] * len(parts),
        out_specs=WHOLE,
        compiler_params=params(8),
        cost_estimate=pl.CostEstimate(flops=rows * width, bytes_accessed=8 * rows * width, transcendentals=0),
        name="finish",
    )(*parts)


def halve(total, swap, bits):
    for bit in reversed(range(bits)):
        half = total.shape[0] // 2
        arrived = swap(total[half:].astype(jnp.bfloat16), 1 << bit)
        total = total[:half]
        if bit:
            total = total + arrived.astype(jnp.float32)
    return total, arrived


def local(features, cotangent, weight, tiles, tile_rows, tile_cols, tile_counts):
    blocks = lax.axis_size("dom")
    groups = lax.axis_size("repl")
    chips = blocks // 2
    chip_bits, member_bits = bit_count(chips), bit_count(groups)
    rows_local, width = features.shape
    part_width = width // CHUNKS
    scale = float(rows_local * blocks * groups) ** (-0.5)
    place = jnp.stack([lax.axis_index("dom"), lax.axis_index("repl")]).astype(jnp.int32)
    column, slot = tables(blocks, groups)

    near, near_other = [(features, 0)], [(swap_cores(features), 0)]
    for bit in range(chip_bits - 1):
        held = [array[row:row + rows_local] for array, row in near]
        got = swap_chips(jnp.concatenate(held) if bit else held[0], 1 << bit)
        got_other = swap_cores(got)
        near += [(got, k * rows_local) for k in range(1 << bit)]
        near_other += [(got_other, k * rows_local) for k in range(1 << bit)]
    dense = densify(tiles[0, 0], tile_rows, tile_cols, tile_counts, column, slot, place, groups, rows_local)

    pieces = []
    for c in range(CHUNKS):
        cut = slice(c * part_width, (c + 1) * part_width)
        held = jnp.concatenate([array[row:row + rows_local, cut] for array, row in near])
        got = swap_chips(held, chips // 2)
        early = [(*pair[side], c * part_width) for pair in zip(near, near_other) for side in range(2)]
        totals = forward(dense, 0, early, part_width, None, [jnp.float32] * 2)
        got = after(got, *totals)
        got_other = swap_cores(got)
        late = [(array, k * rows_local, 0) for k in range(chips // 2) for array in (got, got_other)]
        low, high = forward(dense, len(early), late, part_width, totals, [jnp.float32, jnp.bfloat16])
        arrived = swap_members(high, groups // 2)
        pieces.append(halve(low + arrived.astype(jnp.float32), swap_members, member_bits - 1))
    dense_t = transposed(after(dense, high))
    pieces[-1] = (pieces[-1][0], after(pieces[-1][1], *dense_t))

    activated, agg, pre_grad, *grad_chunks = middle(pieces, cotangent, weight)

    share, share_send = weight_part(agg, pre_grad, slot, place, groups)
    share = share + swap_cores(share_send).astype(jnp.float32)

    columns = []
    for c in range(CHUNKS):
        grads = [grad_chunks[c]]
        for bit in range(member_bits):
            grads.append(swap_members(jnp.concatenate(grads) if bit else grads[0], 1 << bit))
            if c == 0 and bit == 0:
                total, arrived = halve(after(share, grads[-1]).reshape(-1, width), swap_members, member_bits)
                part = (total + arrived.astype(jnp.float32)).astype(jnp.bfloat16)
        grads[-1] = after(grads[-1], part)
        own, other = backward(dense_t[1], grads)
        high_sum = (own + swap_cores(other).astype(jnp.float32)).astype(jnp.bfloat16)
        own, other = backward(after(dense_t[0], high_sum), grads)
        low_sum = own + swap_cores(other).astype(jnp.float32)
        low_sum = low_sum + swap_chips(high_sum, chips // 2).astype(jnp.float32)
        columns += halve(low_sum, swap_chips, chip_bits - 1)
    feature_grad = finish(columns)

    for bit in range(chip_bits):
        part = part.astype(jnp.float32) + swap_chips(part, 1 << bit).astype(jnp.float32)
        part = part.astype(jnp.bfloat16) if bit < chip_bits - 1 else part * scale
    parts = jnp.concatenate([part] + [swap_members(part, k) for k in range(1, groups)])
    other = swap_cores(parts)
    shape = (groups, -1, width)
    weight_grad = place_slices(parts.reshape(shape), other.reshape(shape), slot, place)
    return (activated, feature_grad, weight_grad)


def solution(mesh):
    in_specs = (
        P(("dom", "repl"), None),
        P(("dom", "repl"), None),
        P(),
        P("dom", "repl", None, None, None, None),
        P("dom", "repl", None, None),
        P("dom", "repl", None, None),
        P("dom", "repl", None),
    )
    out_specs = (P(("dom", "repl"), None), P(("dom", "repl"), None), P())
    return jax.shard_map(local, mesh=mesh, in_specs=in_specs, out_specs=out_specs, check_vma=False)
```

```python
import functools

import jax
import jax.numpy as jnp
from jax import lax
from jax.experimental import pallas as pl
from jax.experimental.pallas import tpu as pltpu
from jax.sharding import PartitionSpec as P

WHOLE = pl.BlockSpec(memory_space=pltpu.VMEM)
SCALARS = pl.BlockSpec(memory_space=pltpu.SMEM)


def bit_count(n):
    return n.bit_length() - 1


def between(index, core, bits):
    reverse = 0
    for i in range(bits):
        reverse = reverse | (((index >> i) & 1) << (bits - 1 - i))
    return core * index + (1 - core) * reverse


def swap_cores(x):
    return lax.ppermute(x, "dom", [(i, i ^ 1) for i in range(lax.axis_size("dom"))])


def swap_chips(x, held):
    blocks = lax.axis_size("dom")
    bits = bit_count(blocks // 2)
    return lax.ppermute(x, "dom", [(i, i ^ (2 * between(held, i % 2, bits))) for i in range(blocks)])


def swap_members(x, held, turn=0):
    blocks, groups = lax.axis_size("dom"), lax.axis_size("repl")
    bits = bit_count(groups)
    pairs = []
    for i in range(blocks):
        for j in range(groups):
            pairs.append((i * groups + j, i * groups + (j ^ between(held, (i % 2) ^ turn, bits))))
    return lax.ppermute(x, ("dom", "repl"), pairs)


def after(x, *others):
    return lax.optimization_barrier((x, *others))[0]


def params(mib):
    return pltpu.CompilerParams(vmem_limit_bytes=mib * 1024 * 1024)


def like(shape, dtype):
    return jax.ShapeDtypeStruct(shape, dtype)


def bf16_dot(a, b):
    return jnp.dot(a, b, preferred_element_type=jnp.float32)


def column_of(position, j, blocks):
    core = (position & 1) ^ (j & 1)
    return (((position >> 1) ^ between(j >> 1, core, bit_count(blocks // 2))) << 1) | core


def densify_kernel(spots_ref, place_ref, tiles_ref, a_ref, acc_ref, *, col_tiles):
    column = column_of(place_ref[0], pl.program_id(0), pl.num_programs(0))
    size = tiles_ref.shape[-1]
    count = tiles_ref.shape[1]
    acc_ref[...] = jnp.zeros_like(acc_ref)

    def add(tile, carry):
        acc_ref[spots_ref[column, tile]] += tiles_ref[0, tile].astype(jnp.float32)
        return carry

    lax.fori_loop(0, spots_ref[column, count], add, 0)
    for spot in range(acc_ref.shape[0]):
        row, col = spot // col_tiles, spot % col_tiles
        a_ref[0, row * size:(row + 1) * size, col * size:(col + 1) * size] = acc_ref[spot].astype(a_ref.dtype)


def densify(tiles, spots, place, group_count, rows_local):
    columns, count, size, _ = tiles.shape
    col_tiles = rows_local // size
    rows = group_count * rows_local
    return pl.pallas_call(
        functools.partial(densify_kernel, col_tiles=col_tiles),
        out_shape=like((columns, rows, rows_local), jnp.bfloat16),
        grid_spec=pltpu.PrefetchScalarGridSpec(
            num_scalar_prefetch=2,
            grid=(columns,),
            in_specs=[pl.BlockSpec((1, count, size, size), lambda j, s, p: (column_of(p[0], j, columns), 0, 0, 0))],
            out_specs=pl.BlockSpec((1, rows, rows_local), lambda j, *_: (j, 0, 0)),
            scratch_shapes=[pltpu.VMEM((group_count * col_tiles * col_tiles, size, size), jnp.float32)],
        ),
        compiler_params=params(12),
        cost_estimate=pl.CostEstimate(
            flops=columns * count * size * size, bytes_accessed=8 * rows * columns * rows_local, transcendentals=0),
        name="densify",
    )(spots, place, tiles)


def transpose_kernel(a_ref, *outs):
    for i, out_ref in enumerate(outs):
        for side in range(2):
            out_ref[side] = a_ref[2 * i + side].T


def transposed(dense):
    columns, rows, cols = dense.shape
    return pl.pallas_call(
        transpose_kernel,
        out_shape=[like((2, cols, rows), jnp.bfloat16)] * (columns // 2),
        in_specs=[WHOLE],
        out_specs=[WHOLE] * (columns // 2),
        compiler_params=params(8),
        cost_estimate=pl.CostEstimate(flops=0, bytes_accessed=4 * columns * rows * cols, transcendentals=0),
        name="transposed",
    )(dense)


def forward_kernel(*refs, first, count, slots, has_prev):
    dense_ref, sources = refs[0], refs[1:1 + count]
    rest = refs[1 + count:]
    prev, outs = (rest[:slots], rest[slots:]) if has_prev else (None, rest)
    rows = outs[0].shape[0]
    for k, out_ref in reversed(list(enumerate(outs))):
        total = prev[k][...] if has_prev else None
        for j, source in enumerate(sources):
            part = bf16_dot(dense_ref[first + j, k * rows:(k + 1) * rows, :], source[...])
            total = part if total is None else total + part
        out_ref[...] = total.astype(out_ref.dtype)


def forward(dense, first, sources, prev, dtypes):
    slots = len(dtypes)
    _, rows, depth = dense.shape
    width = sources[0].shape[1]
    return pl.pallas_call(
        functools.partial(
            forward_kernel, first=first, count=len(sources), slots=slots, has_prev=prev is not None),
        out_shape=[like((rows // slots, width), dtype) for dtype in dtypes],
        in_specs=[WHOLE] * (1 + len(sources) + (slots if prev is not None else 0)),
        out_specs=[WHOLE] * slots,
        compiler_params=params(8),
        cost_estimate=pl.CostEstimate(
            flops=2 * len(sources) * rows * depth * width,
            bytes_accessed=2 * len(sources) * rows * depth + 4 * rows * width, transcendentals=0),
        name="forward",
    )(dense, *sources, *(prev or []))


def middle_kernel(*refs):
    pieces, (cot_ref, weight_ref, act_ref, agg_ref, pre_grad_ref, grad_ref) = refs[:-6], refs[-6:]
    agg = pieces[0][...]
    for piece in pieces[1:]:
        agg = agg + piece[...].astype(jnp.float32)
    agg = agg.astype(jnp.bfloat16)
    agg_ref[...] = agg
    weight = weight_ref[...]
    preact = bf16_dot(agg, weight)
    sigma = jax.nn.sigmoid(preact)
    act_ref[...] = (preact * sigma).astype(act_ref.dtype)
    slope = sigma * (1.0 + preact * (1.0 - sigma))
    pre_grad = (cot_ref[...].astype(jnp.float32) * slope).astype(jnp.bfloat16)
    pre_grad_ref[...] = pre_grad
    grad_ref[...] = lax.dot_general(
        pre_grad, weight, (((1,), (1,)), ((), ())), preferred_element_type=jnp.float32
    ).astype(jnp.bfloat16)


def middle(pieces, cotangent, weight):
    rows, width = cotangent.shape
    return pl.pallas_call(
        middle_kernel,
        out_shape=[like((rows, width), jnp.bfloat16)] * 4,
        in_specs=[WHOLE] * (2 + len(pieces)),
        out_specs=[WHOLE] * 4,
        compiler_params=params(8),
        cost_estimate=pl.CostEstimate(
            flops=4 * rows * width * width, bytes_accessed=10 * rows * width, transcendentals=rows * width),
        name="middle",
    )(*pieces, cotangent, weight)


def weight_kernel(place_ref, agg_ref, pre_grad_ref, *refs, groups):
    owns, send_ref, part_ref = refs[:groups], refs[groups], refs[groups + 1]
    core, member = place_ref[0] & 1, place_ref[1]
    rows = owns[0].shape[0]
    bits = bit_count(groups)
    part_ref[...] = lax.dot_general(
        agg_ref[...], pre_grad_ref[...], (((0,), (0,)), ((), ())), preferred_element_type=jnp.float32
    )

    def piece(k, side):
        start = (2 * (member ^ between(k, 1 - side, bits)) + side) * rows
        return part_ref[pl.ds(pl.multiple_of(start, rows), rows), :]

    for k in range(groups):
        owns[k][...] = piece(k, core)
        send_ref[k * rows:(k + 1) * rows, :] = piece(k, 1 - core).astype(send_ref.dtype)


def weight_part(agg, pre_grad, place, groups):
    rows, width = agg.shape
    part = width // (2 * groups)
    out = pl.pallas_call(
        functools.partial(weight_kernel, groups=groups),
        out_shape=[like((part, width), jnp.float32)] * groups + [like((groups * part, width), jnp.bfloat16)],
        in_specs=[SCALARS, WHOLE, WHOLE],
        out_specs=[WHOLE] * (groups + 1),
        scratch_shapes=[pltpu.VMEM((width, width), jnp.float32)],
        compiler_params=params(8),
        cost_estimate=pl.CostEstimate(
            flops=2 * rows * width * width, bytes_accessed=4 * rows * width + 4 * width * width, transcendentals=0),
        name="weight_part",
    )(place, agg, pre_grad)
    return out[:-1], out[-1]


def place_kernel(place_ref, *refs, groups):
    owns, other_ref, out_ref = refs[:groups], refs[groups], refs[groups + 1]
    core, member = place_ref[0] & 1, place_ref[1]
    rows = owns[0].shape[0]
    bits = bit_count(groups)
    for k in range(groups):
        for side, value in ((core, owns[k][...]), (1 - core, other_ref[k * rows:(k + 1) * rows, :])):
            start = (2 * (member ^ between(k, 1 - side, bits)) + side) * rows
            out_ref[pl.ds(pl.multiple_of(start, rows), rows), :] = value


def place_slices(owns, other, place):
    groups = len(owns)
    rows, width = owns[0].shape
    return pl.pallas_call(
        functools.partial(place_kernel, groups=groups),
        out_shape=like((2 * groups * rows, width), jnp.float32),
        in_specs=[SCALARS] + [WHOLE] * (groups + 1),
        out_specs=WHOLE,
        compiler_params=params(8),
        cost_estimate=pl.CostEstimate(flops=0, bytes_accessed=16 * groups * rows * width, transcendentals=0),
        name="place_slices",
    )(place, *owns, other)


def backward_kernel(*refs, count, slots):
    blocks, grads = refs[:count], refs[count:count + slots]
    owns, other_ref = refs[count + slots:-1], refs[-1]
    rows = owns[0].shape[0]
    for side in (1, 0):
        for i, block in enumerate(blocks):
            total, start = None, 0
            for grad in grads:
                stop = start + grad.shape[0]
                part = bf16_dot(block[side, :, start:stop], grad[...])
                total, start = part if total is None else total + part, stop
            if side:
                other_ref[i * rows:(i + 1) * rows, :] = total.astype(other_ref.dtype)
            else:
                owns[i][...] = total


def backward(blocks, grads):
    _, cols, rows = blocks[0].shape
    width = grads[0].shape[1]
    count = len(blocks)
    out = pl.pallas_call(
        functools.partial(backward_kernel, count=count, slots=len(grads)),
        out_shape=[like((cols, width), jnp.float32)] * count + [like((count * cols, width), jnp.bfloat16)],
        in_specs=[WHOLE] * (count + len(grads)),
        out_specs=[WHOLE] * (count + 1),
        compiler_params=params(8),
        cost_estimate=pl.CostEstimate(
            flops=4 * count * cols * rows * width,
            bytes_accessed=4 * count * cols * rows + 2 * rows * width + 6 * count * cols * width, transcendentals=0),
        name="backward",
    )(*blocks, *grads)
    return out[:-1], out[-1]


def finish_kernel(*refs):
    total = refs[0][...]
    for ref in refs[1:-1]:
        total = total + ref[...].astype(jnp.float32)
    refs[-1][...] = total.astype(refs[-1].dtype)


def finish(parts):
    rows, width = parts[0].shape
    return pl.pallas_call(
        finish_kernel,
        out_shape=like((rows, width), jnp.bfloat16),
        in_specs=[WHOLE] * len(parts),
        out_specs=WHOLE,
        compiler_params=params(8),
        cost_estimate=pl.CostEstimate(flops=rows * width, bytes_accessed=8 * rows * width, transcendentals=0),
        name="finish",
    )(*parts)


def top_bit(slot):
    return 1 << (slot.bit_length() - 1)


def halve(totals, swap):
    while True:
        half = len(totals) // 2
        send = [total.astype(jnp.bfloat16) for total in totals[half:]]
        got = swap(jnp.concatenate(send) if half > 1 else send[0], half)
        if half == 1:
            return [totals[0], got]
        totals = add_slots(totals[:half], got)


def add_slots(totals, got):
    rows = totals[0].shape[0]
    return [total + got[k * rows:(k + 1) * rows].astype(jnp.float32) for k, total in enumerate(totals)]


def collect(totals, swap):
    totals = list(totals)
    arrived = []
    for k in reversed(range(1, len(totals))):
        got = swap(totals[k].astype(jnp.bfloat16), top_bit(k))
        if k == top_bit(k):
            arrived.append(got)
        else:
            totals[k - top_bit(k)] = totals[k - top_bit(k)].astype(jnp.float32) + got.astype(jnp.float32)
    return [totals[0], *arrived]


def local(features, cotangent, weight, tiles, tile_rows, tile_cols, tile_counts):
    blocks = lax.axis_size("dom")
    groups = lax.axis_size("repl")
    chips = blocks // 2
    rows_local, width = features.shape
    scale = float(rows_local * blocks * groups) ** (-0.5)
    position, member = lax.axis_index("dom"), lax.axis_index("repl")
    place = jnp.stack([position, member]).astype(jnp.int32)

    col_tiles = rows_local // tiles.shape[-1]
    row = tile_rows[0, 0]
    row = between((row // col_tiles) ^ member, position & 1, bit_count(groups)) * col_tiles + row % col_tiles
    spots = jnp.concatenate([row * col_tiles + tile_cols[0, 0], tile_counts[0, 0][:, None]], axis=1)
    dense = densify(tiles[0, 0], spots, place, groups, rows_local)

    held = [features]
    for k in range(1, chips):
        held.append(swap_chips(held[k - top_bit(k)], top_bit(k)))
    totals = None
    for first, stop in ((0, chips // 2), (chips // 2, chips)):
        sources = []
        for k in range(first, stop):
            own = held[k] if totals is None else after(held[k], held[-1], *totals)
            sources += [own, swap_cores(own)]
        dtypes = [jnp.float32] * groups
        if stop == chips:
            dtypes = [jnp.float32 if k < groups // 2 else jnp.bfloat16 for k in range(groups)]
        totals = forward(dense, 2 * first, sources, totals, dtypes)

    pieces = collect(totals, swap_members)
    dense_t = transposed(after(dense, *totals))
    pieces[-1] = after(pieces[-1], *dense_t)
    activated, agg, pre_grad, grad = middle(pieces, cotangent, weight)
    owns, send = weight_part(agg, pre_grad, place, groups)
    parts = add_slots(owns, swap_cores(send))

    grads = [grad]
    while sum(x.shape[0] for x in grads) < groups * rows_local:
        slots = sum(x.shape[0] for x in grads) // rows_local
        grads.append(swap_members(jnp.concatenate(grads) if slots > 1 else grad, slots))
        if slots == 1:
            parts[-1] = after(parts[-1], grads[-1])
            kept, got = halve(parts, functools.partial(swap_members, turn=1))
            part = (kept + got.astype(jnp.float32)).astype(jnp.bfloat16)
    grads[-1] = after(grads[-1], part)

    half = chips // 2
    own, other = backward(dense_t[half:], grads)
    high = jnp.concatenate(add_slots(own, swap_cores(other))).astype(jnp.bfloat16)
    own, other = backward([after(dense_t[0], high), *dense_t[1:half]], grads)
    low = add_slots(own, swap_cores(other))
    feature_grad = finish(halve(add_slots(low, swap_chips(high, half)), swap_chips))

    bit = 1
    while bit < chips:
        part = part.astype(jnp.float32) + swap_chips(part, bit).astype(jnp.float32)
        bit *= 2
        part = part.astype(jnp.bfloat16) if bit < chips else part * scale
    parts = [part] + [swap_members(part, k, turn=1) for k in range(1, groups)]
    weight_grad = place_slices(parts, swap_cores(jnp.concatenate(parts)), place)
    return (activated, feature_grad, weight_grad)


def solution(mesh):
    in_specs = (
        P(("dom", "repl"), None),
        P(("dom", "repl"), None),
        P(),
        P("dom", "repl", None, None, None, None),
        P("dom", "repl", None, None),
        P("dom", "repl", None, None),
        P("dom", "repl", None),
    )
    out_specs = (P(("dom", "repl"), None), P(("dom", "repl"), None), P())
    return jax.shard_map(local, mesh=mesh, in_specs=in_specs, out_specs=out_specs, check_vma=False)
```

```python
import functools

import jax
import jax.numpy as jnp
from jax import lax
from jax.experimental import pallas as pl
from jax.experimental.pallas import tpu as pltpu
from jax.sharding import PartitionSpec as P

WHOLE = pl.BlockSpec(memory_space=pltpu.VMEM)
SCALARS = pl.BlockSpec(memory_space=pltpu.SMEM)


def bit_count(n):
    return n.bit_length() - 1


def between(index, core, bits):
    reverse = 0
    for i in range(bits):
        reverse = reverse | (((index >> i) & 1) << (bits - 1 - i))
    return core * index + (1 - core) * reverse


def swap_cores(x):
    return lax.ppermute(x, "dom", [(i, i ^ 1) for i in range(lax.axis_size("dom"))])


def swap_chips(x, held):
    blocks = lax.axis_size("dom")
    bits = bit_count(blocks // 2)
    return lax.ppermute(x, "dom", [(i, i ^ (2 * between(held, i % 2, bits))) for i in range(blocks)])


def swap_members(x, held, turn=0):
    blocks, groups = lax.axis_size("dom"), lax.axis_size("repl")
    bits = bit_count(groups)
    pairs = []
    for i in range(blocks):
        for j in range(groups):
            pairs.append((i * groups + j, i * groups + (j ^ between(held, (i % 2) ^ turn, bits))))
    return lax.ppermute(x, ("dom", "repl"), pairs)


def after(x, *others):
    return lax.optimization_barrier((x, *others))[0]


def params(mib):
    return pltpu.CompilerParams(vmem_limit_bytes=mib * 1024 * 1024)


def like(shape, dtype):
    return jax.ShapeDtypeStruct(shape, dtype)


def bf16_dot(a, b):
    return jnp.dot(a, b, preferred_element_type=jnp.float32)


def column_of(position, j, blocks):
    core = (position & 1) ^ (j & 1)
    return (((position >> 1) ^ between(j >> 1, core, bit_count(blocks // 2))) << 1) | core


def densify_kernel(spots_ref, place_ref, tiles_ref, a_ref, acc_ref, *, col_tiles):
    column = column_of(place_ref[0], pl.program_id(0), pl.num_programs(0))
    size = tiles_ref.shape[-1]
    count = tiles_ref.shape[1]
    acc_ref[...] = jnp.zeros_like(acc_ref)

    def add(tile, carry):
        acc_ref[spots_ref[column, tile]] += tiles_ref[0, tile].astype(jnp.float32)
        return carry

    lax.fori_loop(0, spots_ref[column, count], add, 0)
    for spot in range(acc_ref.shape[0]):
        row, col = spot // col_tiles, spot % col_tiles
        a_ref[0, row * size:(row + 1) * size, col * size:(col + 1) * size] = acc_ref[spot].astype(a_ref.dtype)


def densify(tiles, spots, place, group_count, rows_local):
    columns, count, size, _ = tiles.shape
    col_tiles = rows_local // size
    rows = group_count * rows_local
    return pl.pallas_call(
        functools.partial(densify_kernel, col_tiles=col_tiles),
        out_shape=like((columns, rows, rows_local), jnp.bfloat16),
        grid_spec=pltpu.PrefetchScalarGridSpec(
            num_scalar_prefetch=2,
            grid=(columns,),
            in_specs=[pl.BlockSpec((1, count, size, size), lambda j, s, p: (column_of(p[0], j, columns), 0, 0, 0))],
            out_specs=pl.BlockSpec((1, rows, rows_local), lambda j, *_: (j, 0, 0)),
            scratch_shapes=[pltpu.VMEM((group_count * col_tiles * col_tiles, size, size), jnp.float32)],
        ),
        compiler_params=params(12),
        cost_estimate=pl.CostEstimate(
            flops=columns * count * size * size, bytes_accessed=8 * rows * columns * rows_local, transcendentals=0),
        name="densify",
    )(spots, place, tiles)


def transpose_kernel(a_ref, *outs):
    for i, out_ref in enumerate(outs):
        for side in range(2):
            out_ref[side] = a_ref[2 * i + side].T


def transposed(dense):
    columns, rows, cols = dense.shape
    return pl.pallas_call(
        transpose_kernel,
        out_shape=[like((2, cols, rows), jnp.bfloat16)] * (columns // 2),
        in_specs=[WHOLE],
        out_specs=[WHOLE] * (columns // 2),
        compiler_params=params(8),
        cost_estimate=pl.CostEstimate(flops=0, bytes_accessed=4 * columns * rows * cols, transcendentals=0),
        name="transposed",
    )(dense)


def forward_kernel(*refs, first, count, slots, has_prev):
    dense_ref, sources = refs[0], refs[1:1 + count]
    rest = refs[1 + count:]
    prev, outs = (rest[:slots], rest[slots:]) if has_prev else (None, rest)
    rows = outs[0].shape[0]
    for k, out_ref in reversed(list(enumerate(outs))):
        total = prev[k][...] if has_prev else None
        for j, source in enumerate(sources):
            part = bf16_dot(dense_ref[first + j, k * rows:(k + 1) * rows, :], source[...])
            total = part if total is None else total + part
        out_ref[...] = total.astype(out_ref.dtype)


def forward(dense, first, sources, prev, dtypes):
    slots = len(dtypes)
    _, rows, depth = dense.shape
    width = sources[0].shape[1]
    return pl.pallas_call(
        functools.partial(
            forward_kernel, first=first, count=len(sources), slots=slots, has_prev=prev is not None),
        out_shape=[like((rows // slots, width), dtype) for dtype in dtypes],
        in_specs=[WHOLE] * (1 + len(sources) + (slots if prev is not None else 0)),
        out_specs=[WHOLE] * slots,
        compiler_params=params(8),
        cost_estimate=pl.CostEstimate(
            flops=2 * len(sources) * rows * depth * width,
            bytes_accessed=2 * len(sources) * rows * depth + 4 * rows * width, transcendentals=0),
        name="forward",
    )(dense, *sources, *(prev or []))


def middle_kernel(*refs):
    pieces, (cot_ref, weight_ref, act_ref, agg_ref, pre_grad_ref, grad_ref) = refs[:-6], refs[-6:]
    agg = pieces[0][...]
    for piece in pieces[1:]:
        agg = agg + piece[...].astype(jnp.float32)
    agg = agg.astype(jnp.bfloat16)
    agg_ref[...] = agg
    weight = weight_ref[...]
    preact = bf16_dot(agg, weight)
    sigma = jax.nn.sigmoid(preact)
    act_ref[...] = (preact * sigma).astype(act_ref.dtype)
    slope = sigma * (1.0 + preact * (1.0 - sigma))
    pre_grad = (cot_ref[...].astype(jnp.float32) * slope).astype(jnp.bfloat16)
    pre_grad_ref[...] = pre_grad
    grad_ref[...] = lax.dot_general(
        pre_grad, weight, (((1,), (1,)), ((), ())), preferred_element_type=jnp.float32
    ).astype(jnp.bfloat16)


def middle(pieces, cotangent, weight):
    rows, width = cotangent.shape
    return pl.pallas_call(
        middle_kernel,
        out_shape=[like((rows, width), jnp.bfloat16)] * 4,
        in_specs=[WHOLE] * (2 + len(pieces)),
        out_specs=[WHOLE] * 4,
        compiler_params=params(8),
        cost_estimate=pl.CostEstimate(
            flops=4 * rows * width * width, bytes_accessed=10 * rows * width, transcendentals=rows * width),
        name="middle",
    )(*pieces, cotangent, weight)


def weight_kernel(place_ref, agg_ref, pre_grad_ref, *refs, groups):
    owns, send_ref, part_ref = refs[:groups], refs[groups], refs[groups + 1]
    core, member = place_ref[0] & 1, place_ref[1]
    rows = owns[0].shape[0]
    bits = bit_count(groups)
    part_ref[...] = lax.dot_general(
        agg_ref[...], pre_grad_ref[...], (((0,), (0,)), ((), ())), preferred_element_type=jnp.float32
    )

    def piece(k, side):
        start = (2 * (member ^ between(k, 1 - side, bits)) + side) * rows
        return part_ref[pl.ds(pl.multiple_of(start, rows), rows), :]

    for k in range(groups):
        owns[k][...] = piece(k, core)
        send_ref[k * rows:(k + 1) * rows, :] = piece(k, 1 - core).astype(send_ref.dtype)


def weight_part(agg, pre_grad, place, groups):
    rows, width = agg.shape
    part = width // (2 * groups)
    out = pl.pallas_call(
        functools.partial(weight_kernel, groups=groups),
        out_shape=[like((part, width), jnp.float32)] * groups + [like((groups * part, width), jnp.bfloat16)],
        in_specs=[SCALARS, WHOLE, WHOLE],
        out_specs=[WHOLE] * (groups + 1),
        scratch_shapes=[pltpu.VMEM((width, width), jnp.float32)],
        compiler_params=params(8),
        cost_estimate=pl.CostEstimate(
            flops=2 * rows * width * width, bytes_accessed=4 * rows * width + 4 * width * width, transcendentals=0),
        name="weight_part",
    )(place, agg, pre_grad)
    return out[:-1], out[-1]


def place_kernel(place_ref, *refs, groups):
    owns, other_ref, out_ref = refs[:groups], refs[groups], refs[groups + 1]
    core, member = place_ref[0] & 1, place_ref[1]
    rows = owns[0].shape[0]
    bits = bit_count(groups)
    for k in range(groups):
        for side, value in ((core, owns[k][...]), (1 - core, other_ref[k * rows:(k + 1) * rows, :])):
            start = (2 * (member ^ between(k, 1 - side, bits)) + side) * rows
            out_ref[pl.ds(pl.multiple_of(start, rows), rows), :] = value


def place_slices(owns, other, place):
    groups = len(owns)
    rows, width = owns[0].shape
    return pl.pallas_call(
        functools.partial(place_kernel, groups=groups),
        out_shape=like((2 * groups * rows, width), jnp.float32),
        in_specs=[SCALARS] + [WHOLE] * (groups + 1),
        out_specs=WHOLE,
        compiler_params=params(8),
        cost_estimate=pl.CostEstimate(flops=0, bytes_accessed=16 * groups * rows * width, transcendentals=0),
        name="place_slices",
    )(place, *owns, other)


def backward_kernel(*refs, side, count, slots):
    blocks, grads, outs = refs[:count], refs[count:count + slots], refs[count + slots:]
    rows = blocks[0].shape[1]
    for i, block in enumerate(blocks):
        total, start = None, 0
        for grad in grads:
            stop = start + grad.shape[0]
            part = bf16_dot(block[side, :, start:stop], grad[...])
            total, start = part if total is None else total + part, stop
        if side:
            outs[0][i * rows:(i + 1) * rows, :] = total.astype(outs[0].dtype)
        else:
            outs[i][...] = total


def backward(blocks, grads, side):
    _, cols, rows = blocks[0].shape
    width = grads[0].shape[1]
    count = len(blocks)
    own = [like((cols, width), jnp.float32)] * count
    return pl.pallas_call(
        functools.partial(backward_kernel, side=side, count=count, slots=len(grads)),
        out_shape=[like((count * cols, width), jnp.bfloat16)] if side else own,
        in_specs=[WHOLE] * (count + len(grads)),
        out_specs=[WHOLE] * (1 if side else count),
        compiler_params=params(8),
        cost_estimate=pl.CostEstimate(
            flops=2 * count * cols * rows * width,
            bytes_accessed=2 * count * cols * rows + 2 * rows * width + 4 * count * cols * width, transcendentals=0),
        name="backward",
    )(*blocks, *grads)


def settle_kernel(*refs, slots, count):
    totals, arrived, outs = refs[:slots], refs[slots:slots + count], refs[slots + count:]
    rows = totals[0].shape[0]
    for k in range(slots):
        total = totals[k][...]
        for ref in arrived:
            total = total + ref[k * rows:(k + 1) * rows, :].astype(jnp.float32)
        outs[k][...] = total.astype(outs[k].dtype)


def settle(totals, arrived, dtypes):
    rows, width = totals[0].shape
    return pl.pallas_call(
        functools.partial(settle_kernel, slots=len(totals), count=len(arrived)),
        out_shape=[like((rows, width), dtype) for dtype in dtypes],
        in_specs=[WHOLE] * (len(totals) + len(arrived)),
        out_specs=[WHOLE] * len(totals),
        compiler_params=params(8),
        cost_estimate=pl.CostEstimate(flops=rows * width, bytes_accessed=8 * rows * width, transcendentals=0),
        name="settle",
    )(*totals, *arrived)


def top_bit(slot):
    return 1 << (slot.bit_length() - 1)


def halve(totals, swap):
    while True:
        half = len(totals) // 2
        send = [total.astype(jnp.bfloat16) for total in totals[half:]]
        got = swap(jnp.concatenate(send) if half > 1 else send[0], half)
        if half == 1:
            return [totals[0], got]
        totals = add_slots(totals[:half], got)


def add_slots(totals, got):
    rows = totals[0].shape[0]
    return [total + got[k * rows:(k + 1) * rows].astype(jnp.float32) for k, total in enumerate(totals)]


def collect(totals, swap):
    totals = list(totals)
    arrived = []
    for k in reversed(range(1, len(totals))):
        got = swap(totals[k].astype(jnp.bfloat16), top_bit(k))
        if k == top_bit(k):
            arrived.append(got)
        else:
            totals[k - top_bit(k)] = totals[k - top_bit(k)].astype(jnp.float32) + got.astype(jnp.float32)
    return [totals[0], *arrived]


def local(features, cotangent, weight, tiles, tile_rows, tile_cols, tile_counts):
    blocks = lax.axis_size("dom")
    groups = lax.axis_size("repl")
    chips = blocks // 2
    rows_local, width = features.shape
    scale = float(rows_local * blocks * groups) ** (-0.5)
    position, member = lax.axis_index("dom"), lax.axis_index("repl")
    place = jnp.stack([position, member]).astype(jnp.int32)

    col_tiles = rows_local // tiles.shape[-1]
    row = tile_rows[0, 0]
    row = between((row // col_tiles) ^ member, position & 1, bit_count(groups)) * col_tiles + row % col_tiles
    spots = jnp.concatenate([row * col_tiles + tile_cols[0, 0], tile_counts[0, 0][:, None]], axis=1)
    dense = densify(tiles[0, 0], spots, place, groups, rows_local)

    held = [features]
    for k in range(1, chips):
        given = after(features, held[k - 1]) if k == top_bit(k) > 1 else held[k - top_bit(k)]
        held.append(swap_chips(given, top_bit(k)))
    totals = None
    for first, stop in ((0, chips // 2), (chips // 2, chips)):
        sources = []
        for k in range(first, stop):
            own = held[k] if totals is None else after(held[k], held[-1], *totals)
            sources += [own, swap_cores(own)]
        dtypes = [jnp.float32] * groups
        if stop == chips:
            dtypes = [jnp.float32 if k < groups // 2 else jnp.bfloat16 for k in range(groups)]
        totals = forward(dense, 2 * first, sources, totals, dtypes)

    pieces = collect(totals, swap_members)
    dense_t = transposed(after(dense, *totals))
    pieces[-1] = after(pieces[-1], *dense_t)
    activated, agg, pre_grad, grad = middle(pieces, cotangent, weight)
    owns, send = weight_part(agg, pre_grad, place, groups)
    parts = add_slots(owns, swap_cores(send))

    grads = [grad]
    while sum(x.shape[0] for x in grads) < groups * rows_local:
        slots = sum(x.shape[0] for x in grads) // rows_local
        grads.append(swap_members(jnp.concatenate(grads) if slots > 1 else grad, slots))
        if slots == 1:
            kept, got = halve(parts, functools.partial(swap_members, turn=1))
            part = (kept + got.astype(jnp.float32)).astype(jnp.bfloat16)
    part = after(part, grads[-1])

    half = chips // 2
    other = backward(dense_t[half:], grads, 1)
    own = backward([after(dense_t[half], *other), *dense_t[half + 1:]], grads, 0)
    high = jnp.concatenate(add_slots(own, swap_cores(other[0]))).astype(jnp.bfloat16)
    grads[0] = after(grads[0], high)
    other = backward(dense_t[:half], grads, 1)
    totals = backward(dense_t[:half], grads, 0)
    arrived = [swap_cores(other[0]), swap_chips(high, half)]
    while half > 1:
        half //= 2
        totals = settle(totals, arrived, [jnp.float32] * half + [jnp.bfloat16] * half)
        send = jnp.concatenate(totals[half:]) if half > 1 else totals[half]
        totals, arrived = totals[:half], [swap_chips(send, half)]
    (feature_grad,) = settle(totals, arrived, [jnp.bfloat16])

    bit = 1
    while bit < chips:
        part = part.astype(jnp.float32) + swap_chips(part, bit).astype(jnp.float32)
        bit *= 2
        part = part.astype(jnp.bfloat16) if bit < chips else part * scale
    parts = [part] + [swap_members(part, k, turn=1) for k in range(1, groups)]
    weight_grad = place_slices(parts, swap_cores(jnp.concatenate(parts)), place)
    return (activated, feature_grad, weight_grad)


def solution(mesh):
    in_specs = (
        P(("dom", "repl"), None),
        P(("dom", "repl"), None),
        P(),
        P("dom", "repl", None, None, None, None),
        P("dom", "repl", None, None),
        P("dom", "repl", None, None),
        P("dom", "repl", None),
    )
    out_specs = (P(("dom", "repl"), None), P(("dom", "repl"), None), P())
    return jax.shard_map(local, mesh=mesh, in_specs=in_specs, out_specs=out_specs, check_vma=False)
```

```python
import functools

import jax
import jax.numpy as jnp
from jax import lax
from jax.experimental import pallas as pl
from jax.experimental.pallas import tpu as pltpu
from jax.sharding import PartitionSpec as P

WHOLE = pl.BlockSpec(memory_space=pltpu.VMEM)
SCALARS = pl.BlockSpec(memory_space=pltpu.SMEM)


def bit_count(n):
    return n.bit_length() - 1


def between(index, core, bits):
    reverse = 0
    for i in range(bits):
        reverse = reverse | (((index >> i) & 1) << (bits - 1 - i))
    return core * index + (1 - core) * reverse


def swap_cores(x):
    return lax.ppermute(x, "dom", [(i, i ^ 1) for i in range(lax.axis_size("dom"))])


def swap_chips(x, held):
    blocks = lax.axis_size("dom")
    bits = bit_count(blocks // 2)
    return lax.ppermute(x, "dom", [(i, i ^ (2 * between(held, i % 2, bits))) for i in range(blocks)])


def swap_members(x, held, turn=0):
    blocks, groups = lax.axis_size("dom"), lax.axis_size("repl")
    bits = bit_count(groups)
    pairs = []
    for i in range(blocks):
        for j in range(groups):
            pairs.append((i * groups + j, i * groups + (j ^ between(held, (i % 2) ^ turn, bits))))
    return lax.ppermute(x, ("dom", "repl"), pairs)


def after(x, *others):
    return lax.optimization_barrier((x, *others))[0]


def params(mib):
    return pltpu.CompilerParams(vmem_limit_bytes=mib * 1024 * 1024)


def like(shape, dtype):
    return jax.ShapeDtypeStruct(shape, dtype)


def bf16_dot(a, b):
    return jnp.dot(a, b, preferred_element_type=jnp.float32)


def column_of(position, j, blocks):
    core = (position & 1) ^ (j & 1)
    return (((position >> 1) ^ between(j >> 1, core, bit_count(blocks // 2))) << 1) | core


def densify_kernel(spots_ref, place_ref, tiles_ref, a_ref, acc_ref, *, col_tiles):
    column = column_of(place_ref[0], pl.program_id(0), pl.num_programs(0))
    size = tiles_ref.shape[-1]
    count = tiles_ref.shape[1]
    acc_ref[...] = jnp.zeros_like(acc_ref)

    def add(tile, carry):
        acc_ref[spots_ref[column, tile]] += tiles_ref[0, tile].astype(jnp.float32)
        return carry

    lax.fori_loop(0, spots_ref[column, count], add, 0)
    for spot in range(acc_ref.shape[0]):
        row, col = spot // col_tiles, spot % col_tiles
        a_ref[0, row * size:(row + 1) * size, col * size:(col + 1) * size] = acc_ref[spot].astype(a_ref.dtype)


def densify(tiles, spots, place, group_count, rows_local):
    columns, count, size, _ = tiles.shape
    col_tiles = rows_local // size
    rows = group_count * rows_local
    return pl.pallas_call(
        functools.partial(densify_kernel, col_tiles=col_tiles),
        out_shape=like((columns, rows, rows_local), jnp.bfloat16),
        grid_spec=pltpu.PrefetchScalarGridSpec(
            num_scalar_prefetch=2,
            grid=(columns,),
            in_specs=[pl.BlockSpec((1, count, size, size), lambda j, s, p: (column_of(p[0], j, columns), 0, 0, 0))],
            out_specs=pl.BlockSpec((1, rows, rows_local), lambda j, *_: (j, 0, 0)),
            scratch_shapes=[pltpu.VMEM((group_count * col_tiles * col_tiles, size, size), jnp.float32)],
        ),
        compiler_params=params(12),
        cost_estimate=pl.CostEstimate(
            flops=columns * count * size * size, bytes_accessed=8 * rows * columns * rows_local, transcendentals=0),
        name="densify",
    )(spots, place, tiles)


def transpose_kernel(a_ref, *outs):
    for i, out_ref in enumerate(outs):
        for side in range(2):
            out_ref[side] = a_ref[2 * i + side].T


def transposed(dense):
    columns, rows, cols = dense.shape
    return pl.pallas_call(
        transpose_kernel,
        out_shape=[like((2, cols, rows), jnp.bfloat16)] * (columns // 2),
        in_specs=[WHOLE],
        out_specs=[WHOLE] * (columns // 2),
        compiler_params=params(8),
        cost_estimate=pl.CostEstimate(flops=0, bytes_accessed=4 * columns * rows * cols, transcendentals=0),
        name="transposed",
    )(dense)


def forward_kernel(*refs, first, count, slots, has_prev):
    dense_ref, sources = refs[0], refs[1:1 + count]
    rest = refs[1 + count:]
    prev, outs = (rest[:slots], rest[slots:]) if has_prev else (None, rest)
    rows = outs[0].shape[0]
    for k, out_ref in reversed(list(enumerate(outs))):
        total = prev[k][...] if has_prev else None
        for j, source in enumerate(sources):
            part = bf16_dot(dense_ref[first + j, k * rows:(k + 1) * rows, :], source[...])
            total = part if total is None else total + part
        out_ref[...] = total.astype(out_ref.dtype)


def forward(dense, first, sources, prev, dtypes):
    slots = len(dtypes)
    _, rows, depth = dense.shape
    width = sources[0].shape[1]
    return pl.pallas_call(
        functools.partial(
            forward_kernel, first=first, count=len(sources), slots=slots, has_prev=prev is not None),
        out_shape=[like((rows // slots, width), dtype) for dtype in dtypes],
        in_specs=[WHOLE] * (1 + len(sources) + (slots if prev is not None else 0)),
        out_specs=[WHOLE] * slots,
        compiler_params=params(8),
        cost_estimate=pl.CostEstimate(
            flops=2 * len(sources) * rows * depth * width,
            bytes_accessed=2 * len(sources) * rows * depth + 4 * rows * width, transcendentals=0),
        name="forward",
    )(dense, *sources, *(prev or []))


def middle_kernel(*refs):
    pieces, (cot_ref, weight_ref, act_ref, agg_ref, pre_grad_ref, grad_ref) = refs[:-6], refs[-6:]
    agg = pieces[0][...]
    for piece in pieces[1:]:
        agg = agg + piece[...].astype(jnp.float32)
    agg = agg.astype(jnp.bfloat16)
    agg_ref[...] = agg
    weight = weight_ref[...]
    preact = bf16_dot(agg, weight)
    sigma = jax.nn.sigmoid(preact)
    act_ref[...] = (preact * sigma).astype(act_ref.dtype)
    slope = sigma * (1.0 + preact * (1.0 - sigma))
    pre_grad = (cot_ref[...].astype(jnp.float32) * slope).astype(jnp.bfloat16)
    pre_grad_ref[...] = pre_grad
    grad_ref[...] = lax.dot_general(
        pre_grad, weight, (((1,), (1,)), ((), ())), preferred_element_type=jnp.float32
    ).astype(jnp.bfloat16)


def middle(pieces, cotangent, weight):
    rows, width = cotangent.shape
    return pl.pallas_call(
        middle_kernel,
        out_shape=[like((rows, width), jnp.bfloat16)] * 4,
        in_specs=[WHOLE] * (2 + len(pieces)),
        out_specs=[WHOLE] * 4,
        compiler_params=params(8),
        cost_estimate=pl.CostEstimate(
            flops=4 * rows * width * width, bytes_accessed=10 * rows * width, transcendentals=rows * width),
        name="middle",
    )(*pieces, cotangent, weight)


def weight_kernel(place_ref, agg_ref, pre_grad_ref, *refs, groups):
    owns, send_ref, part_ref = refs[:groups], refs[groups], refs[groups + 1]
    core, member = place_ref[0] & 1, place_ref[1]
    rows = owns[0].shape[0]
    bits = bit_count(groups)
    part_ref[...] = lax.dot_general(
        agg_ref[...], pre_grad_ref[...], (((0,), (0,)), ((), ())), preferred_element_type=jnp.float32
    )

    def piece(k, side):
        start = (2 * (member ^ between(k, 1 - side, bits)) + side) * rows
        return part_ref[pl.ds(pl.multiple_of(start, rows), rows), :]

    for k in range(groups):
        owns[k][...] = piece(k, core)
        send_ref[k * rows:(k + 1) * rows, :] = piece(k, 1 - core).astype(send_ref.dtype)


def weight_part(agg, pre_grad, place, groups):
    rows, width = agg.shape
    part = width // (2 * groups)
    out = pl.pallas_call(
        functools.partial(weight_kernel, groups=groups),
        out_shape=[like((part, width), jnp.float32)] * groups + [like((groups * part, width), jnp.bfloat16)],
        in_specs=[SCALARS, WHOLE, WHOLE],
        out_specs=[WHOLE] * (groups + 1),
        scratch_shapes=[pltpu.VMEM((width, width), jnp.float32)],
        compiler_params=params(8),
        cost_estimate=pl.CostEstimate(
            flops=2 * rows * width * width, bytes_accessed=4 * rows * width + 4 * width * width, transcendentals=0),
        name="weight_part",
    )(place, agg, pre_grad)
    return out[:-1], out[-1]


def place_kernel(place_ref, *refs, groups):
    owns, other_ref, out_ref = refs[:groups], refs[groups], refs[groups + 1]
    core, member = place_ref[0] & 1, place_ref[1]
    rows = owns[0].shape[0]
    bits = bit_count(groups)
    for k in range(groups):
        for side, value in ((core, owns[k][...]), (1 - core, other_ref[k * rows:(k + 1) * rows, :])):
            start = (2 * (member ^ between(k, 1 - side, bits)) + side) * rows
            out_ref[pl.ds(pl.multiple_of(start, rows), rows), :] = value


def place_slices(owns, other, place):
    groups = len(owns)
    rows, width = owns[0].shape
    return pl.pallas_call(
        functools.partial(place_kernel, groups=groups),
        out_shape=like((2 * groups * rows, width), jnp.float32),
        in_specs=[SCALARS] + [WHOLE] * (groups + 1),
        out_specs=WHOLE,
        compiler_params=params(8),
        cost_estimate=pl.CostEstimate(flops=0, bytes_accessed=16 * groups * rows * width, transcendentals=0),
        name="place_slices",
    )(place, *owns, other)


def backward_kernel(*refs, side, count, slots):
    blocks, grads, outs = refs[:count], refs[count:count + slots], refs[count + slots:]
    rows = blocks[0].shape[1]
    for i, block in enumerate(blocks):
        total, start = None, 0
        for grad in grads:
            stop = start + grad.shape[0]
            part = bf16_dot(block[side, :, start:stop], grad[...])
            total, start = part if total is None else total + part, stop
        if side:
            outs[0][i * rows:(i + 1) * rows, :] = total.astype(outs[0].dtype)
        else:
            outs[i][...] = total


def backward(blocks, grads, side):
    _, cols, rows = blocks[0].shape
    width = grads[0].shape[1]
    count = len(blocks)
    own = [like((cols, width), jnp.float32)] * count
    return pl.pallas_call(
        functools.partial(backward_kernel, side=side, count=count, slots=len(grads)),
        out_shape=[like((count * cols, width), jnp.bfloat16)] if side else own,
        in_specs=[WHOLE] * (count + len(grads)),
        out_specs=[WHOLE] * (1 if side else count),
        compiler_params=params(8),
        cost_estimate=pl.CostEstimate(
            flops=2 * count * cols * rows * width,
            bytes_accessed=2 * count * cols * rows + 2 * rows * width + 4 * count * cols * width, transcendentals=0),
        name="backward",
    )(*blocks, *grads)


def settle_kernel(*refs, slots, count):
    totals, arrived, outs = refs[:slots], refs[slots:slots + count], refs[slots + count:]
    rows = totals[0].shape[0]
    for k in range(slots):
        total = totals[k][...]
        for ref in arrived:
            total = total + ref[k * rows:(k + 1) * rows, :].astype(jnp.float32)
        outs[k][...] = total.astype(outs[k].dtype)


def settle(totals, arrived, dtypes):
    rows, width = totals[0].shape
    return pl.pallas_call(
        functools.partial(settle_kernel, slots=len(totals), count=len(arrived)),
        out_shape=[like((rows, width), dtype) for dtype in dtypes],
        in_specs=[WHOLE] * (len(totals) + len(arrived)),
        out_specs=[WHOLE] * len(totals),
        compiler_params=params(8),
        cost_estimate=pl.CostEstimate(flops=rows * width, bytes_accessed=8 * rows * width, transcendentals=0),
        name="settle",
    )(*totals, *arrived)


def top_bit(slot):
    return 1 << (slot.bit_length() - 1)


def halve(totals, swap):
    while True:
        half = len(totals) // 2
        send = [total.astype(jnp.bfloat16) for total in totals[half:]]
        got = swap(jnp.concatenate(send) if half > 1 else send[0], half)
        if half == 1:
            return [totals[0], got]
        totals = add_slots(totals[:half], got)


def add_slots(totals, got):
    rows = totals[0].shape[0]
    return [total + got[k * rows:(k + 1) * rows].astype(jnp.float32) for k, total in enumerate(totals)]


def collect(totals, swap):
    totals = list(totals)
    arrived = []
    for k in reversed(range(1, len(totals))):
        got = swap(totals[k].astype(jnp.bfloat16), top_bit(k))
        if k == top_bit(k):
            arrived.append(got)
        else:
            totals[k - top_bit(k)] = totals[k - top_bit(k)].astype(jnp.float32) + got.astype(jnp.float32)
    return [totals[0], *arrived]


def local(features, cotangent, weight, tiles, tile_rows, tile_cols, tile_counts):
    blocks = lax.axis_size("dom")
    groups = lax.axis_size("repl")
    chips = blocks // 2
    rows_local, width = features.shape
    scale = float(rows_local * blocks * groups) ** (-0.5)
    position, member = lax.axis_index("dom"), lax.axis_index("repl")
    place = jnp.stack([position, member]).astype(jnp.int32)

    col_tiles = rows_local // tiles.shape[-1]
    row = tile_rows[0, 0]
    row = between((row // col_tiles) ^ member, position & 1, bit_count(groups)) * col_tiles + row % col_tiles
    spots = jnp.concatenate([row * col_tiles + tile_cols[0, 0], tile_counts[0, 0][:, None]], axis=1)
    dense = densify(tiles[0, 0], spots, place, groups, rows_local)

    held = [features]
    for k in range(1, chips):
        given = after(features, held[k - 1]) if k == top_bit(k) > 1 else held[k - top_bit(k)]
        held.append(swap_chips(given, top_bit(k)))
        if k == 1:
            held[1] = after(held[1], spots)
    totals = None
    for first, stop in ((0, chips // 2), (chips // 2, chips)):
        sources = []
        for k in range(first, stop):
            own = held[k] if totals is None else after(held[k], held[-1], *totals)
            sources += [own, swap_cores(own)]
        dtypes = [jnp.float32] * groups
        if stop == chips:
            dtypes = [jnp.float32 if k < groups // 2 else jnp.bfloat16 for k in range(groups)]
        totals = forward(dense, 2 * first, sources, totals, dtypes)

    pieces = collect(totals, swap_members)
    dense_t = transposed(after(dense, *totals, pieces[1]))
    pieces[-1] = after(pieces[-1], *dense_t)
    activated, agg, pre_grad, grad = middle(pieces, cotangent, weight)
    owns, send = weight_part(agg, pre_grad, place, groups)
    parts = add_slots(owns, swap_cores(send))

    grads = [grad]
    while sum(x.shape[0] for x in grads) < groups * rows_local:
        slots = sum(x.shape[0] for x in grads) // rows_local
        grads.append(swap_members(jnp.concatenate(grads) if slots > 1 else grad, slots))
        if slots == 1:
            part = parts[0]
            for k in range(1, groups):
                part = part + swap_members(parts[k].astype(jnp.bfloat16), k, turn=1).astype(jnp.float32)
            part = part.astype(jnp.bfloat16)
            near = swap_chips(part, 1)
            part = part.astype(jnp.float32) + near.astype(jnp.float32)
    grads[-1] = after(grads[-1], near)

    half = chips // 2
    other = backward(dense_t[half:], grads, 1)
    own = backward([after(dense_t[half], *other), *dense_t[half + 1:]], grads, 0)
    high = jnp.concatenate(add_slots(own, swap_cores(other[0]))).astype(jnp.bfloat16)
    grads[0] = after(grads[0], high)
    other = backward(dense_t[:half], grads, 1)
    totals = backward(dense_t[:half], grads, 0)
    arrived = [swap_cores(other[0]), swap_chips(high, half)]
    while half > 1:
        half //= 2
        totals = settle(totals, arrived, [jnp.float32] * half + [jnp.bfloat16] * half)
        send = jnp.concatenate(totals[half:]) if half > 1 else totals[half]
        totals, arrived = totals[:half], [swap_chips(send, half)]
    (feature_grad,) = settle(totals, arrived, [jnp.bfloat16])

    bit = 2
    while bit < chips:
        part = part.astype(jnp.bfloat16)
        part = part.astype(jnp.float32) + swap_chips(part, bit).astype(jnp.float32)
        bit *= 2
    part = part * scale
    parts = [part] + [swap_members(part, k, turn=1) for k in range(1, groups)]
    weight_grad = place_slices(parts, swap_cores(jnp.concatenate(parts)), place)
    return (activated, feature_grad, weight_grad)


def solution(mesh):
    in_specs = (
        P(("dom", "repl"), None),
        P(("dom", "repl"), None),
        P(),
        P("dom", "repl", None, None, None, None),
        P("dom", "repl", None, None),
        P("dom", "repl", None, None),
        P("dom", "repl", None),
    )
    out_specs = (P(("dom", "repl"), None), P(("dom", "repl"), None), P())
    return jax.shard_map(local, mesh=mesh, in_specs=in_specs, out_specs=out_specs, check_vma=False)
```

```python
import functools

import jax
import jax.numpy as jnp
from jax import lax
from jax.experimental import pallas as pl
from jax.experimental.pallas import tpu as pltpu
from jax.sharding import PartitionSpec as P

WHOLE = pl.BlockSpec(memory_space=pltpu.VMEM)
SCALARS = pl.BlockSpec(memory_space=pltpu.SMEM)


def bit_count(n):
    return n.bit_length() - 1


def between(index, core, bits):
    reverse = 0
    for i in range(bits):
        reverse = reverse | (((index >> i) & 1) << (bits - 1 - i))
    return core * index + (1 - core) * reverse


def swap_cores(x):
    return lax.ppermute(x, "dom", [(i, i ^ 1) for i in range(lax.axis_size("dom"))])


def swap_chips(x, held):
    blocks = lax.axis_size("dom")
    bits = bit_count(blocks // 2)
    return lax.ppermute(x, "dom", [(i, i ^ (2 * between(held, i % 2, bits))) for i in range(blocks)])


def swap_members(x, held, turn=0):
    blocks, groups = lax.axis_size("dom"), lax.axis_size("repl")
    bits = bit_count(groups)
    pairs = []
    for i in range(blocks):
        for j in range(groups):
            pairs.append((i * groups + j, i * groups + (j ^ between(held, (i % 2) ^ turn, bits))))
    return lax.ppermute(x, ("dom", "repl"), pairs)


def after(x, *others):
    return lax.optimization_barrier((x, *others))[0]


def params(mib):
    return pltpu.CompilerParams(vmem_limit_bytes=mib * 1024 * 1024)


def like(shape, dtype):
    return jax.ShapeDtypeStruct(shape, dtype)


def bf16_dot(a, b):
    return jnp.dot(a, b, preferred_element_type=jnp.float32)


def column_of(position, j, blocks):
    core = (position & 1) ^ (j & 1)
    return (((position >> 1) ^ between(j >> 1, core, bit_count(blocks // 2))) << 1) | core


def densify_kernel(spots_ref, place_ref, tiles_ref, a_ref, acc_ref, *, col_tiles):
    column = column_of(place_ref[0], pl.program_id(0), pl.num_programs(0))
    size = tiles_ref.shape[-1]
    count = tiles_ref.shape[1]
    acc_ref[...] = jnp.zeros_like(acc_ref)

    def add(tile, carry):
        acc_ref[spots_ref[column, tile]] += tiles_ref[0, tile].astype(jnp.float32)
        return carry

    lax.fori_loop(0, spots_ref[column, count], add, 0)
    for spot in range(acc_ref.shape[0]):
        row, col = spot // col_tiles, spot % col_tiles
        a_ref[0, row * size:(row + 1) * size, col * size:(col + 1) * size] = acc_ref[spot].astype(a_ref.dtype)


def densify(tiles, spots, place, group_count, rows_local):
    columns, count, size, _ = tiles.shape
    col_tiles = rows_local // size
    rows = group_count * rows_local
    return pl.pallas_call(
        functools.partial(densify_kernel, col_tiles=col_tiles),
        out_shape=like((columns, rows, rows_local), jnp.bfloat16),
        grid_spec=pltpu.PrefetchScalarGridSpec(
            num_scalar_prefetch=2,
            grid=(columns,),
            in_specs=[pl.BlockSpec((1, count, size, size), lambda j, s, p: (column_of(p[0], j, columns), 0, 0, 0))],
            out_specs=pl.BlockSpec((1, rows, rows_local), lambda j, *_: (j, 0, 0)),
            scratch_shapes=[pltpu.VMEM((group_count * col_tiles * col_tiles, size, size), jnp.float32)],
        ),
        compiler_params=params(12),
        cost_estimate=pl.CostEstimate(
            flops=columns * count * size * size, bytes_accessed=8 * rows * columns * rows_local, transcendentals=0),
        name="densify",
    )(spots, place, tiles)


def transpose_kernel(a_ref, *outs):
    for i, out_ref in enumerate(outs):
        for side in range(2):
            out_ref[side] = a_ref[2 * i + side].T


def transposed(dense):
    columns, rows, cols = dense.shape
    return pl.pallas_call(
        transpose_kernel,
        out_shape=[like((2, cols, rows), jnp.bfloat16)] * (columns // 2),
        in_specs=[WHOLE],
        out_specs=[WHOLE] * (columns // 2),
        compiler_params=params(8),
        cost_estimate=pl.CostEstimate(flops=0, bytes_accessed=4 * columns * rows * cols, transcendentals=0),
        name="transposed",
    )(dense)


def forward_kernel(*refs, first, count, slots, has_prev):
    dense_ref, sources = refs[0], refs[1:1 + count]
    rest = refs[1 + count:]
    prev, outs = (rest[:slots], rest[slots:]) if has_prev else (None, rest)
    rows = outs[0].shape[0]
    for k, out_ref in reversed(list(enumerate(outs))):
        total = prev[k][...] if has_prev else None
        for j, source in enumerate(sources):
            part = bf16_dot(dense_ref[first + j, k * rows:(k + 1) * rows, :], source[...])
            total = part if total is None else total + part
        out_ref[...] = total.astype(out_ref.dtype)


def forward(dense, first, sources, prev, dtypes):
    slots = len(dtypes)
    _, rows, depth = dense.shape
    width = sources[0].shape[1]
    return pl.pallas_call(
        functools.partial(
            forward_kernel, first=first, count=len(sources), slots=slots, has_prev=prev is not None),
        out_shape=[like((rows // slots, width), dtype) for dtype in dtypes],
        in_specs=[WHOLE] * (1 + len(sources) + (slots if prev is not None else 0)),
        out_specs=[WHOLE] * slots,
        compiler_params=params(8),
        cost_estimate=pl.CostEstimate(
            flops=2 * len(sources) * rows * depth * width,
            bytes_accessed=2 * len(sources) * rows * depth + 4 * rows * width, transcendentals=0),
        name="forward",
    )(dense, *sources, *(prev or []))


def middle_kernel(*refs):
    pieces, (cot_ref, weight_ref, act_ref, agg_ref, pre_grad_ref, grad_ref) = refs[:-6], refs[-6:]
    agg = pieces[0][...]
    for piece in pieces[1:]:
        agg = agg + piece[...].astype(jnp.float32)
    agg = agg.astype(jnp.bfloat16)
    agg_ref[...] = agg
    weight = weight_ref[...]
    preact = bf16_dot(agg, weight)
    sigma = jax.nn.sigmoid(preact)
    act_ref[...] = (preact * sigma).astype(act_ref.dtype)
    slope = sigma * (1.0 + preact * (1.0 - sigma))
    pre_grad = (cot_ref[...].astype(jnp.float32) * slope).astype(jnp.bfloat16)
    pre_grad_ref[...] = pre_grad
    grad_ref[...] = lax.dot_general(
        pre_grad, weight, (((1,), (1,)), ((), ())), preferred_element_type=jnp.float32
    ).astype(jnp.bfloat16)


def middle(pieces, cotangent, weight):
    rows, width = cotangent.shape
    return pl.pallas_call(
        middle_kernel,
        out_shape=[like((rows, width), jnp.bfloat16)] * 4,
        in_specs=[WHOLE] * (2 + len(pieces)),
        out_specs=[WHOLE] * 4,
        compiler_params=params(8),
        cost_estimate=pl.CostEstimate(
            flops=4 * rows * width * width, bytes_accessed=10 * rows * width, transcendentals=rows * width),
        name="middle",
    )(*pieces, cotangent, weight)


def weight_kernel(place_ref, agg_ref, pre_grad_ref, *refs, groups):
    owns, send_ref, part_ref = refs[:groups], refs[groups], refs[groups + 1]
    core, member = place_ref[0] & 1, place_ref[1]
    rows = owns[0].shape[0]
    bits = bit_count(groups)
    part_ref[...] = lax.dot_general(
        agg_ref[...], pre_grad_ref[...], (((0,), (0,)), ((), ())), preferred_element_type=jnp.float32
    )

    def piece(k, side):
        start = (2 * (member ^ between(k, 1 - side, bits)) + side) * rows
        return part_ref[pl.ds(pl.multiple_of(start, rows), rows), :]

    for k in range(groups):
        owns[k][...] = piece(k, core)
        send_ref[k * rows:(k + 1) * rows, :] = piece(k, 1 - core).astype(send_ref.dtype)


def weight_part(agg, pre_grad, place, groups):
    rows, width = agg.shape
    part = width // (2 * groups)
    out = pl.pallas_call(
        functools.partial(weight_kernel, groups=groups),
        out_shape=[like((part, width), jnp.float32)] * groups + [like((groups * part, width), jnp.bfloat16)],
        in_specs=[SCALARS, WHOLE, WHOLE],
        out_specs=[WHOLE] * (groups + 1),
        scratch_shapes=[pltpu.VMEM((width, width), jnp.float32)],
        compiler_params=params(8),
        cost_estimate=pl.CostEstimate(
            flops=2 * rows * width * width, bytes_accessed=4 * rows * width + 4 * width * width, transcendentals=0),
        name="weight_part",
    )(place, agg, pre_grad)
    return out[:-1], out[-1]


def place_kernel(place_ref, *refs, groups):
    owns, other_ref, out_ref = refs[:groups], refs[groups], refs[groups + 1]
    core, member = place_ref[0] & 1, place_ref[1]
    rows = owns[0].shape[0]
    bits = bit_count(groups)
    for k in range(groups):
        for side, value in ((core, owns[k][...]), (1 - core, other_ref[k * rows:(k + 1) * rows, :])):
            start = (2 * (member ^ between(k, 1 - side, bits)) + side) * rows
            out_ref[pl.ds(pl.multiple_of(start, rows), rows), :] = value


def place_slices(owns, other, place):
    groups = len(owns)
    rows, width = owns[0].shape
    return pl.pallas_call(
        functools.partial(place_kernel, groups=groups),
        out_shape=like((2 * groups * rows, width), jnp.float32),
        in_specs=[SCALARS] + [WHOLE] * (groups + 1),
        out_specs=WHOLE,
        compiler_params=params(8),
        cost_estimate=pl.CostEstimate(flops=0, bytes_accessed=16 * groups * rows * width, transcendentals=0),
        name="place_slices",
    )(place, *owns, other)


def backward_kernel(*refs, side, count, slots):
    blocks, grads, outs = refs[:count], refs[count:count + slots], refs[count + slots:]
    rows = blocks[0].shape[1]
    for i, block in enumerate(blocks):
        total, start = None, 0
        for grad in grads:
            stop = start + grad.shape[0]
            part = bf16_dot(block[side, :, start:stop], grad[...])
            total, start = part if total is None else total + part, stop
        if side:
            outs[0][i * rows:(i + 1) * rows, :] = total.astype(outs[0].dtype)
        else:
            outs[i][...] = total


def backward(blocks, grads, side):
    _, cols, rows = blocks[0].shape
    width = grads[0].shape[1]
    count = len(blocks)
    own = [like((cols, width), jnp.float32)] * count
    return pl.pallas_call(
        functools.partial(backward_kernel, side=side, count=count, slots=len(grads)),
        out_shape=[like((count * cols, width), jnp.bfloat16)] if side else own,
        in_specs=[WHOLE] * (count + len(grads)),
        out_specs=[WHOLE] * (1 if side else count),
        compiler_params=params(8),
        cost_estimate=pl.CostEstimate(
            flops=2 * count * cols * rows * width,
            bytes_accessed=2 * count * cols * rows + 2 * rows * width + 4 * count * cols * width, transcendentals=0),
        name="backward",
    )(*blocks, *grads)


def settle_kernel(*refs, slots, count):
    totals, arrived, outs = refs[:slots], refs[slots:slots + count], refs[slots + count:]
    rows = totals[0].shape[0]
    for k in range(slots):
        total = totals[k][...]
        for ref in arrived:
            total = total + ref[k * rows:(k + 1) * rows, :].astype(jnp.float32)
        outs[k][...] = total.astype(outs[k].dtype)


def settle(totals, arrived, dtypes):
    rows, width = totals[0].shape
    return pl.pallas_call(
        functools.partial(settle_kernel, slots=len(totals), count=len(arrived)),
        out_shape=[like((rows, width), dtype) for dtype in dtypes],
        in_specs=[WHOLE] * (len(totals) + len(arrived)),
        out_specs=[WHOLE] * len(totals),
        compiler_params=params(8),
        cost_estimate=pl.CostEstimate(flops=rows * width, bytes_accessed=8 * rows * width, transcendentals=0),
        name="settle",
    )(*totals, *arrived)


def top_bit(slot):
    return 1 << (slot.bit_length() - 1)


def halve(totals, swap):
    while True:
        half = len(totals) // 2
        send = [total.astype(jnp.bfloat16) for total in totals[half:]]
        got = swap(jnp.concatenate(send) if half > 1 else send[0], half)
        if half == 1:
            return [totals[0], got]
        totals = add_slots(totals[:half], got)


def add_slots(totals, got):
    rows = totals[0].shape[0]
    return [total + got[k * rows:(k + 1) * rows].astype(jnp.float32) for k, total in enumerate(totals)]


def collect(totals, swap):
    totals = list(totals)
    arrived = []
    for k in reversed(range(1, len(totals))):
        got = swap(totals[k].astype(jnp.bfloat16), top_bit(k))
        if k == top_bit(k):
            arrived.append(got)
        else:
            totals[k - top_bit(k)] = totals[k - top_bit(k)].astype(jnp.float32) + got.astype(jnp.float32)
    return [totals[0], *arrived]


def local(features, cotangent, weight, tiles, tile_rows, tile_cols, tile_counts):
    blocks = lax.axis_size("dom")
    groups = lax.axis_size("repl")
    chips = blocks // 2
    rows_local, width = features.shape
    scale = float(rows_local * blocks * groups) ** (-0.5)
    position, member = lax.axis_index("dom"), lax.axis_index("repl")
    place = jnp.stack([position, member]).astype(jnp.int32)

    col_tiles = rows_local // tiles.shape[-1]
    row = tile_rows[0, 0]
    row = between((row // col_tiles) ^ member, position & 1, bit_count(groups)) * col_tiles + row % col_tiles
    spots = jnp.concatenate([row * col_tiles + tile_cols[0, 0], tile_counts[0, 0][:, None]], axis=1)
    dense = densify(tiles[0, 0], spots, place, groups, rows_local)

    held = [features]
    for k in range(1, chips):
        given = after(features, held[k - 1]) if k == top_bit(k) > 1 else held[k - top_bit(k)]
        held.append(swap_chips(given, top_bit(k)))
        if k == 1:
            held[1] = after(held[1], spots)
    totals = None
    for first, stop in ((0, chips // 2), (chips // 2, chips)):
        sources = []
        for k in range(first, stop):
            own = held[k] if totals is None else after(held[k], held[-1], *totals)
            sources += [own, swap_cores(own)]
        dtypes = [jnp.float32] * groups
        if stop == chips:
            dtypes = [jnp.float32 if k < groups // 2 else jnp.bfloat16 for k in range(groups)]
        totals = forward(dense, 2 * first, sources, totals, dtypes)

    pieces = collect(totals, swap_members)
    dense_t = transposed(after(dense, *totals, pieces[1]))
    pieces[-1] = after(pieces[-1], *dense_t)
    activated, agg, pre_grad, grad = middle(pieces, cotangent, weight)
    owns, send = weight_part(agg, pre_grad, place, groups)
    parts = add_slots(owns, swap_cores(send))

    grads = [grad]
    for k in range(1, groups):
        if k == top_bit(k):
            straight = grads[0]
        else:
            straight = after(grads[k - top_bit(k)], grads[top_bit(k)])
        grads.append(swap_members(straight, top_bit(k)))
    part = parts[0]
    for k in range(1, groups):
        part = part + swap_members(parts[k].astype(jnp.bfloat16), k, turn=1).astype(jnp.float32)
    part = part.astype(jnp.bfloat16)
    near = swap_chips(part, 1)
    part = part.astype(jnp.float32) + near.astype(jnp.float32)
    grads[-1] = after(grads[-1], near)

    half = chips // 2
    other = backward(dense_t[half:], grads, 1)
    own = backward([after(dense_t[half], *other), *dense_t[half + 1:]], grads, 0)
    high = jnp.concatenate(add_slots(own, swap_cores(other[0]))).astype(jnp.bfloat16)
    grads[0] = after(grads[0], high)
    other = backward(dense_t[:half], grads, 1)
    totals = backward(dense_t[:half], grads, 0)
    arrived = [swap_cores(other[0]), swap_chips(high, half)]
    while half > 1:
        half //= 2
        totals = settle(totals, arrived, [jnp.float32] * half + [jnp.bfloat16] * half)
        send = jnp.concatenate(totals[half:]) if half > 1 else totals[half]
        totals, arrived = totals[:half], [swap_chips(send, half)]
    (feature_grad,) = settle(totals, arrived, [jnp.bfloat16])

    bit = 2
    while bit < chips:
        part = part.astype(jnp.bfloat16)
        part = part.astype(jnp.float32) + swap_chips(part, bit).astype(jnp.float32)
        bit *= 2
    part = part * scale
    parts = [part] + [swap_members(part, k, turn=1) for k in range(1, groups)]
    weight_grad = place_slices(parts, swap_cores(jnp.concatenate(parts)), place)
    return (activated, feature_grad, weight_grad)


def solution(mesh):
    in_specs = (
        P(("dom", "repl"), None),
        P(("dom", "repl"), None),
        P(),
        P("dom", "repl", None, None, None, None),
        P("dom", "repl", None, None),
        P("dom", "repl", None, None),
        P("dom", "repl", None),
    )
    out_specs = (P(("dom", "repl"), None), P(("dom", "repl"), None), P())
    return jax.shard_map(local, mesh=mesh, in_specs=in_specs, out_specs=out_specs, check_vma=False)
```

```python
import functools

import jax
import jax.numpy as jnp
from jax import lax
from jax.experimental import pallas as pl
from jax.experimental.pallas import tpu as pltpu
from jax.sharding import PartitionSpec as P

WHOLE = pl.BlockSpec(memory_space=pltpu.VMEM)
SCALARS = pl.BlockSpec(memory_space=pltpu.SMEM)


def bit_count(n):
    return n.bit_length() - 1


def between(index, core, bits):
    reverse = 0
    for i in range(bits):
        reverse = reverse | (((index >> i) & 1) << (bits - 1 - i))
    return core * index + (1 - core) * reverse


def swap_cores(x):
    return lax.ppermute(x, "dom", [(i, i ^ 1) for i in range(lax.axis_size("dom"))])


def swap_chips(x, held):
    blocks = lax.axis_size("dom")
    bits = bit_count(blocks // 2)
    return lax.ppermute(x, "dom", [(i, i ^ (2 * between(held, i % 2, bits))) for i in range(blocks)])


def swap_members(x, held, turn=0):
    blocks, groups = lax.axis_size("dom"), lax.axis_size("repl")
    bits = bit_count(groups)
    pairs = []
    for i in range(blocks):
        for j in range(groups):
            pairs.append((i * groups + j, i * groups + (j ^ between(held, (i % 2) ^ turn, bits))))
    return lax.ppermute(x, ("dom", "repl"), pairs)


def after(x, *others):
    return lax.optimization_barrier((x, *others))[0]


def params(mib):
    return pltpu.CompilerParams(vmem_limit_bytes=mib * 1024 * 1024)


def like(shape, dtype):
    return jax.ShapeDtypeStruct(shape, dtype)


def bf16_dot(a, b):
    return jnp.dot(a, b, preferred_element_type=jnp.float32)


def column_of(position, j, blocks):
    core = (position & 1) ^ (j & 1)
    return (((position >> 1) ^ between(j >> 1, core, bit_count(blocks // 2))) << 1) | core


def densify_kernel(spots_ref, place_ref, tiles_ref, a_ref, acc_ref, *, col_tiles):
    column = column_of(place_ref[0], pl.program_id(0), pl.num_programs(0))
    size = tiles_ref.shape[-1]
    count = tiles_ref.shape[1]
    acc_ref[...] = jnp.zeros_like(acc_ref)

    def add(tile, carry):
        acc_ref[spots_ref[column, tile]] += tiles_ref[0, tile].astype(jnp.float32)
        return carry

    lax.fori_loop(0, spots_ref[column, count], add, 0)
    for spot in range(acc_ref.shape[0]):
        row, col = spot // col_tiles, spot % col_tiles
        a_ref[0, row * size:(row + 1) * size, col * size:(col + 1) * size] = acc_ref[spot].astype(a_ref.dtype)


def densify(tiles, spots, place, group_count, rows_local):
    columns, count, size, _ = tiles.shape
    col_tiles = rows_local // size
    rows = group_count * rows_local
    return pl.pallas_call(
        functools.partial(densify_kernel, col_tiles=col_tiles),
        out_shape=like((columns, rows, rows_local), jnp.bfloat16),
        grid_spec=pltpu.PrefetchScalarGridSpec(
            num_scalar_prefetch=2,
            grid=(columns,),
            in_specs=[pl.BlockSpec((1, count, size, size), lambda j, s, p: (column_of(p[0], j, columns), 0, 0, 0))],
            out_specs=pl.BlockSpec((1, rows, rows_local), lambda j, *_: (j, 0, 0)),
            scratch_shapes=[pltpu.VMEM((group_count * col_tiles * col_tiles, size, size), jnp.float32)],
        ),
        compiler_params=params(12),
        cost_estimate=pl.CostEstimate(
            flops=columns * count * size * size, bytes_accessed=8 * rows * columns * rows_local, transcendentals=0),
        name="densify",
    )(spots, place, tiles)


def transpose_kernel(a_ref, *outs):
    for i, out_ref in enumerate(outs):
        for side in range(2):
            out_ref[side] = a_ref[2 * i + side].T


def transposed(dense):
    columns, rows, cols = dense.shape
    return pl.pallas_call(
        transpose_kernel,
        out_shape=[like((2, cols, rows), jnp.bfloat16)] * (columns // 2),
        in_specs=[WHOLE],
        out_specs=[WHOLE] * (columns // 2),
        compiler_params=params(8),
        cost_estimate=pl.CostEstimate(flops=0, bytes_accessed=4 * columns * rows * cols, transcendentals=0),
        name="transposed",
    )(dense)


def forward_kernel(*refs, first, base, count, slots, has_prev):
    dense_ref, sources = refs[0], refs[1:1 + count]
    rest = refs[1 + count:]
    prev, outs = (rest[:slots], rest[slots:]) if has_prev else (None, rest)
    rows = outs[0].shape[0]
    for k, out_ref in reversed(list(enumerate(outs))):
        total = prev[k][...] if has_prev else None
        for j, source in enumerate(sources):
            part = bf16_dot(dense_ref[first + j, (base + k) * rows:(base + k + 1) * rows, :], source[...])
            total = part if total is None else total + part
        out_ref[...] = total.astype(out_ref.dtype)


def forward(dense, first, sources, base, prev, dtypes):
    slots = len(dtypes)
    depth, width = sources[0].shape
    rows = slots * depth
    return pl.pallas_call(
        functools.partial(
            forward_kernel, first=first, base=base, count=len(sources), slots=slots, has_prev=prev is not None),
        out_shape=[like((depth, width), dtype) for dtype in dtypes],
        in_specs=[WHOLE] * (1 + len(sources) + (slots if prev is not None else 0)),
        out_specs=[WHOLE] * slots,
        compiler_params=params(8),
        cost_estimate=pl.CostEstimate(
            flops=2 * len(sources) * rows * depth * width,
            bytes_accessed=2 * len(sources) * rows * depth + 4 * rows * width, transcendentals=0),
        name="forward",
    )(dense, *sources, *(prev or []))


def middle_kernel(*refs):
    pieces, (cot_ref, weight_ref, act_ref, agg_ref, pre_grad_ref, grad_ref) = refs[:-6], refs[-6:]
    agg = pieces[0][...]
    for piece in pieces[1:]:
        agg = agg + piece[...].astype(jnp.float32)
    agg = agg.astype(jnp.bfloat16)
    agg_ref[...] = agg
    weight = weight_ref[...]
    preact = bf16_dot(agg, weight)
    sigma = jax.nn.sigmoid(preact)
    act_ref[...] = (preact * sigma).astype(act_ref.dtype)
    slope = sigma * (1.0 + preact * (1.0 - sigma))
    pre_grad = (cot_ref[...].astype(jnp.float32) * slope).astype(jnp.bfloat16)
    pre_grad_ref[...] = pre_grad
    grad_ref[...] = lax.dot_general(
        pre_grad, weight, (((1,), (1,)), ((), ())), preferred_element_type=jnp.float32
    ).astype(jnp.bfloat16)


def middle(pieces, cotangent, weight):
    rows, width = cotangent.shape
    return pl.pallas_call(
        middle_kernel,
        out_shape=[like((rows, width), jnp.bfloat16)] * 4,
        in_specs=[WHOLE] * (2 + len(pieces)),
        out_specs=[WHOLE] * 4,
        compiler_params=params(8),
        cost_estimate=pl.CostEstimate(
            flops=4 * rows * width * width, bytes_accessed=10 * rows * width, transcendentals=rows * width),
        name="middle",
    )(*pieces, cotangent, weight)


def weight_kernel(place_ref, agg_ref, pre_grad_ref, *refs, groups):
    owns, send_ref, part_ref = refs[:groups], refs[groups], refs[groups + 1]
    core, member = place_ref[0] & 1, place_ref[1]
    rows = owns[0].shape[0]
    bits = bit_count(groups)
    part_ref[...] = lax.dot_general(
        agg_ref[...], pre_grad_ref[...], (((0,), (0,)), ((), ())), preferred_element_type=jnp.float32
    )

    def piece(k, side):
        start = (2 * (member ^ between(k, 1 - side, bits)) + side) * rows
        return part_ref[pl.ds(pl.multiple_of(start, rows), rows), :]

    for k in range(groups):
        owns[k][...] = piece(k, core)
        send_ref[k * rows:(k + 1) * rows, :] = piece(k, 1 - core).astype(send_ref.dtype)


def weight_part(agg, pre_grad, place, groups):
    rows, width = agg.shape
    part = width // (2 * groups)
    out = pl.pallas_call(
        functools.partial(weight_kernel, groups=groups),
        out_shape=[like((part, width), jnp.float32)] * groups + [like((groups * part, width), jnp.bfloat16)],
        in_specs=[SCALARS, WHOLE, WHOLE],
        out_specs=[WHOLE] * (groups + 1),
        scratch_shapes=[pltpu.VMEM((width, width), jnp.float32)],
        compiler_params=params(8),
        cost_estimate=pl.CostEstimate(
            flops=2 * rows * width * width, bytes_accessed=4 * rows * width + 4 * width * width, transcendentals=0),
        name="weight_part",
    )(place, agg, pre_grad)
    return out[:-1], out[-1]


def place_kernel(place_ref, *refs, groups):
    owns, other_ref, out_ref = refs[:groups], refs[groups], refs[groups + 1]
    core, member = place_ref[0] & 1, place_ref[1]
    rows = owns[0].shape[0]
    bits = bit_count(groups)
    for k in range(groups):
        for side, value in ((core, owns[k][...]), (1 - core, other_ref[k * rows:(k + 1) * rows, :])):
            start = (2 * (member ^ between(k, 1 - side, bits)) + side) * rows
            out_ref[pl.ds(pl.multiple_of(start, rows), rows), :] = value


def place_slices(owns, other, place):
    groups = len(owns)
    rows, width = owns[0].shape
    return pl.pallas_call(
        functools.partial(place_kernel, groups=groups),
        out_shape=like((2 * groups * rows, width), jnp.float32),
        in_specs=[SCALARS] + [WHOLE] * (groups + 1),
        out_specs=WHOLE,
        compiler_params=params(8),
        cost_estimate=pl.CostEstimate(flops=0, bytes_accessed=16 * groups * rows * width, transcendentals=0),
        name="place_slices",
    )(place, *owns, other)


def backward_kernel(*refs, side, count, slots):
    blocks, grads, outs = refs[:count], refs[count:count + slots], refs[count + slots:]
    rows = blocks[0].shape[1]
    for i, block in enumerate(blocks):
        total, start = None, 0
        for grad in grads:
            stop = start + grad.shape[0]
            part = bf16_dot(block[side, :, start:stop], grad[...])
            total, start = part if total is None else total + part, stop
        if side:
            outs[0][i * rows:(i + 1) * rows, :] = total.astype(outs[0].dtype)
        else:
            outs[i][...] = total


def backward(blocks, grads, side):
    _, cols, rows = blocks[0].shape
    width = grads[0].shape[1]
    count = len(blocks)
    own = [like((cols, width), jnp.float32)] * count
    return pl.pallas_call(
        functools.partial(backward_kernel, side=side, count=count, slots=len(grads)),
        out_shape=[like((count * cols, width), jnp.bfloat16)] if side else own,
        in_specs=[WHOLE] * (count + len(grads)),
        out_specs=[WHOLE] * (1 if side else count),
        compiler_params=params(8),
        cost_estimate=pl.CostEstimate(
            flops=2 * count * cols * rows * width,
            bytes_accessed=2 * count * cols * rows + 2 * rows * width + 4 * count * cols * width, transcendentals=0),
        name="backward",
    )(*blocks, *grads)


def settle_kernel(*refs, slots, count):
    totals, arrived, outs = refs[:slots], refs[slots:slots + count], refs[slots + count:]
    rows = totals[0].shape[0]
    for k in range(slots):
        total = totals[k][...]
        for ref in arrived:
            total = total + ref[k * rows:(k + 1) * rows, :].astype(jnp.float32)
        outs[k][...] = total.astype(outs[k].dtype)


def settle(totals, arrived, dtypes):
    rows, width = totals[0].shape
    return pl.pallas_call(
        functools.partial(settle_kernel, slots=len(totals), count=len(arrived)),
        out_shape=[like((rows, width), dtype) for dtype in dtypes],
        in_specs=[WHOLE] * (len(totals) + len(arrived)),
        out_specs=[WHOLE] * len(totals),
        compiler_params=params(8),
        cost_estimate=pl.CostEstimate(flops=rows * width, bytes_accessed=8 * rows * width, transcendentals=0),
        name="settle",
    )(*totals, *arrived)


def top_bit(slot):
    return 1 << (slot.bit_length() - 1)


def halve(totals, swap):
    while True:
        half = len(totals) // 2
        send = [total.astype(jnp.bfloat16) for total in totals[half:]]
        got = swap(jnp.concatenate(send) if half > 1 else send[0], half)
        if half == 1:
            return [totals[0], got]
        totals = add_slots(totals[:half], got)


def add_slots(totals, got):
    rows = totals[0].shape[0]
    return [total + got[k * rows:(k + 1) * rows].astype(jnp.float32) for k, total in enumerate(totals)]


def collect(totals, swap):
    totals = list(totals)
    arrived = []
    for k in reversed(range(1, len(totals))):
        got = swap(totals[k].astype(jnp.bfloat16), top_bit(k))
        if k == top_bit(k):
            arrived.append(got)
        else:
            totals[k - top_bit(k)] = totals[k - top_bit(k)].astype(jnp.float32) + got.astype(jnp.float32)
    return [totals[0], *arrived]


def local(features, cotangent, weight, tiles, tile_rows, tile_cols, tile_counts):
    blocks = lax.axis_size("dom")
    groups = lax.axis_size("repl")
    chips = blocks // 2
    rows_local, width = features.shape
    scale = float(rows_local * blocks * groups) ** (-0.5)
    position, member = lax.axis_index("dom"), lax.axis_index("repl")
    place = jnp.stack([position, member]).astype(jnp.int32)

    col_tiles = rows_local // tiles.shape[-1]
    row = tile_rows[0, 0]
    row = between((row // col_tiles) ^ member, position & 1, bit_count(groups)) * col_tiles + row % col_tiles
    spots = jnp.concatenate([row * col_tiles + tile_cols[0, 0], tile_counts[0, 0][:, None]], axis=1)
    dense = densify(tiles[0, 0], spots, place, groups, rows_local)

    held = [features]
    for k in range(1, chips):
        given = after(features, held[k - 1]) if k == top_bit(k) > 1 else held[k - top_bit(k)]
        held.append(swap_chips(given, top_bit(k)))
        if k == 1:
            held[1] = after(held[1], spots)
    totals = None
    for first, stop in ((0, chips // 2), (chips // 2, chips)):
        sources = []
        for k in range(first, stop):
            own = held[k] if totals is None else after(held[k], held[-1], *totals)
            sources += [own, swap_cores(own)]
        if stop < chips:
            totals = forward(dense, 2 * first, sources, 0, None, [jnp.float32] * groups)
    upper = groups // 2
    high = forward(dense, 2 * first, sources, upper, totals[upper:], [jnp.bfloat16] * upper)
    low = forward(after(dense, *high), 2 * first, sources, 0, totals[:upper], [jnp.float32] * upper)
    totals = low + high

    pieces = collect(totals, swap_members)
    dense_t = transposed(after(dense, *totals, pieces[1]))
    pieces[-1] = after(pieces[-1], *dense_t)
    activated, agg, pre_grad, grad = middle(pieces, cotangent, weight)
    owns, send = weight_part(agg, pre_grad, place, groups)
    parts = add_slots(owns, swap_cores(send))

    grads = [grad]
    for k in range(1, groups):
        if k == top_bit(k):
            straight = grads[0]
        else:
            straight = after(grads[k - top_bit(k)], grads[top_bit(k)])
        grads.append(swap_members(straight, top_bit(k)))
    part = parts[0]
    for k in range(1, groups):
        part = part + swap_members(parts[k].astype(jnp.bfloat16), k, turn=1).astype(jnp.float32)
    part = part.astype(jnp.bfloat16)
    terms = [part] + [swap_chips(part, k) for k in range(1, chips)]
    grads[-1] = after(grads[-1], *terms[1:])
    terms = [term.astype(jnp.float32) for term in terms]
    while len(terms) > 1:
        terms = [terms[i] + terms[i + 1] for i in range(0, len(terms), 2)]
    part = terms[0] * scale

    half = chips // 2
    other = backward(dense_t[half:], grads, 1)
    own = backward([after(dense_t[half], *other), *dense_t[half + 1:]], grads, 0)
    high = jnp.concatenate(add_slots(own, swap_cores(other[0]))).astype(jnp.bfloat16)
    grads[0] = after(grads[0], high)
    other = backward(dense_t[:half], grads, 1)
    totals = backward(dense_t[:half], grads, 0)
    arrived = [swap_cores(other[0]), swap_chips(high, half)]
    while half > 1:
        half //= 2
        totals = settle(totals, arrived, [jnp.float32] * half + [jnp.bfloat16] * half)
        send = jnp.concatenate(totals[half:]) if half > 1 else totals[half]
        totals, arrived = totals[:half], [swap_chips(send, half)]
    (feature_grad,) = settle(totals, arrived, [jnp.bfloat16])

    parts = [part] + [swap_members(part, k, turn=1) for k in range(1, groups)]
    weight_grad = place_slices(parts, swap_cores(jnp.concatenate(parts)), place)
    return (activated, feature_grad, weight_grad)


def solution(mesh):
    in_specs = (
        P(("dom", "repl"), None),
        P(("dom", "repl"), None),
        P(),
        P("dom", "repl", None, None, None, None),
        P("dom", "repl", None, None),
        P("dom", "repl", None, None),
        P("dom", "repl", None),
    )
    out_specs = (P(("dom", "repl"), None), P(("dom", "repl"), None), P())
    return jax.shard_map(local, mesh=mesh, in_specs=in_specs, out_specs=out_specs, check_vma=False)
```

```python
import functools

import jax
import jax.numpy as jnp
from jax import lax
from jax.experimental import pallas as pl
from jax.experimental.pallas import tpu as pltpu
from jax.sharding import PartitionSpec as P

WHOLE = pl.BlockSpec(memory_space=pltpu.VMEM)
SCALARS = pl.BlockSpec(memory_space=pltpu.SMEM)


def bit_count(n):
    return n.bit_length() - 1


def between(index, core, bits):
    reverse = 0
    for i in range(bits):
        reverse = reverse | (((index >> i) & 1) << (bits - 1 - i))
    return core * index + (1 - core) * reverse


def swap_cores(x):
    return lax.ppermute(x, "dom", [(i, i ^ 1) for i in range(lax.axis_size("dom"))])


def swap_chips(x, held):
    blocks = lax.axis_size("dom")
    bits = bit_count(blocks // 2)
    return lax.ppermute(x, "dom", [(i, i ^ (2 * between(held, i % 2, bits))) for i in range(blocks)])


def swap_members(x, held, turn=0):
    blocks, groups = lax.axis_size("dom"), lax.axis_size("repl")
    bits = bit_count(groups)
    pairs = []
    for i in range(blocks):
        for j in range(groups):
            pairs.append((i * groups + j, i * groups + (j ^ between(held, (i % 2) ^ turn, bits))))
    return lax.ppermute(x, ("dom", "repl"), pairs)


def after(x, *others):
    return lax.optimization_barrier((x, *others))[0]


def params(mib):
    return pltpu.CompilerParams(vmem_limit_bytes=mib * 1024 * 1024)


def like(shape, dtype):
    return jax.ShapeDtypeStruct(shape, dtype)


def bf16_dot(a, b):
    return jnp.dot(a, b, preferred_element_type=jnp.float32)


def column_of(position, j, blocks):
    core = (position & 1) ^ (j & 1)
    return (((position >> 1) ^ between(j >> 1, core, bit_count(blocks // 2))) << 1) | core


def densify_kernel(spots_ref, place_ref, tiles_ref, a_ref, acc_ref, *, col_tiles):
    column = column_of(place_ref[0], pl.program_id(0), pl.num_programs(0))
    size = tiles_ref.shape[-1]
    count = tiles_ref.shape[1]
    acc_ref[...] = jnp.zeros_like(acc_ref)

    def add(tile, carry):
        acc_ref[spots_ref[column, tile]] += tiles_ref[0, tile].astype(jnp.float32)
        return carry

    lax.fori_loop(0, spots_ref[column, count], add, 0)
    for spot in range(acc_ref.shape[0]):
        row, col = spot // col_tiles, spot % col_tiles
        a_ref[0, row * size:(row + 1) * size, col * size:(col + 1) * size] = acc_ref[spot].astype(a_ref.dtype)


def densify(tiles, spots, place, group_count, rows_local):
    columns, count, size, _ = tiles.shape
    col_tiles = rows_local // size
    rows = group_count * rows_local
    return pl.pallas_call(
        functools.partial(densify_kernel, col_tiles=col_tiles),
        out_shape=like((columns, rows, rows_local), jnp.bfloat16),
        grid_spec=pltpu.PrefetchScalarGridSpec(
            num_scalar_prefetch=2,
            grid=(columns,),
            in_specs=[pl.BlockSpec((1, count, size, size), lambda j, s, p: (column_of(p[0], j, columns), 0, 0, 0))],
            out_specs=pl.BlockSpec((1, rows, rows_local), lambda j, *_: (j, 0, 0)),
            scratch_shapes=[pltpu.VMEM((group_count * col_tiles * col_tiles, size, size), jnp.float32)],
        ),
        compiler_params=params(12),
        cost_estimate=pl.CostEstimate(
            flops=columns * count * size * size, bytes_accessed=8 * rows * columns * rows_local, transcendentals=0),
        name="densify",
    )(spots, place, tiles)


def transpose_kernel(a_ref, *outs):
    for i, out_ref in enumerate(outs):
        for side in range(2):
            out_ref[side] = a_ref[2 * i + side].T


def transposed(dense):
    columns, rows, cols = dense.shape
    return pl.pallas_call(
        transpose_kernel,
        out_shape=[like((2, cols, rows), jnp.bfloat16)] * (columns // 2),
        in_specs=[WHOLE],
        out_specs=[WHOLE] * (columns // 2),
        compiler_params=params(8),
        cost_estimate=pl.CostEstimate(flops=0, bytes_accessed=4 * columns * rows * cols, transcendentals=0),
        name="transposed",
    )(dense)


def forward_kernel(*refs, first, base, count, slots, has_prev):
    dense_ref, sources = refs[0], refs[1:1 + count]
    rest = refs[1 + count:]
    prev, outs = (rest[:slots], rest[slots:]) if has_prev else (None, rest)
    rows = outs[0].shape[0]
    for k, out_ref in reversed(list(enumerate(outs))):
        total = prev[k][...] if has_prev else None
        for j, source in enumerate(sources):
            part = bf16_dot(dense_ref[first + j, (base + k) * rows:(base + k + 1) * rows, :], source[...])
            total = part if total is None else total + part
        out_ref[...] = total.astype(out_ref.dtype)


def forward(dense, first, sources, base, prev, dtypes):
    slots = len(dtypes)
    depth, width = sources[0].shape
    rows = slots * depth
    return pl.pallas_call(
        functools.partial(
            forward_kernel, first=first, base=base, count=len(sources), slots=slots, has_prev=prev is not None),
        out_shape=[like((depth, width), dtype) for dtype in dtypes],
        in_specs=[WHOLE] * (1 + len(sources) + (slots if prev is not None else 0)),
        out_specs=[WHOLE] * slots,
        compiler_params=params(8),
        cost_estimate=pl.CostEstimate(
            flops=2 * len(sources) * rows * depth * width,
            bytes_accessed=2 * len(sources) * rows * depth + 4 * rows * width, transcendentals=0),
        name="forward",
    )(dense, *sources, *(prev or []))


def middle_kernel(*refs):
    pieces, (cot_ref, weight_ref, act_ref, agg_ref, pre_grad_ref, grad_ref) = refs[:-6], refs[-6:]
    agg = pieces[0][...]
    for piece in pieces[1:]:
        agg = agg + piece[...].astype(jnp.float32)
    agg = agg.astype(jnp.bfloat16)
    agg_ref[...] = agg
    weight = weight_ref[...]
    preact = bf16_dot(agg, weight)
    sigma = jax.nn.sigmoid(preact)
    act_ref[...] = (preact * sigma).astype(act_ref.dtype)
    slope = sigma * (1.0 + preact * (1.0 - sigma))
    pre_grad = (cot_ref[...].astype(jnp.float32) * slope).astype(jnp.bfloat16)
    pre_grad_ref[...] = pre_grad
    grad_ref[...] = lax.dot_general(
        pre_grad, weight, (((1,), (1,)), ((), ())), preferred_element_type=jnp.float32
    ).astype(jnp.bfloat16)


def middle(pieces, cotangent, weight):
    rows, width = cotangent.shape
    return pl.pallas_call(
        middle_kernel,
        out_shape=[like((rows, width), jnp.bfloat16)] * 4,
        in_specs=[WHOLE] * (2 + len(pieces)),
        out_specs=[WHOLE] * 4,
        compiler_params=params(8),
        cost_estimate=pl.CostEstimate(
            flops=4 * rows * width * width, bytes_accessed=10 * rows * width, transcendentals=rows * width),
        name="middle",
    )(*pieces, cotangent, weight)


def weight_kernel(place_ref, agg_ref, pre_grad_ref, *refs, groups):
    owns, send_ref, part_ref = refs[:groups], refs[groups], refs[groups + 1]
    core, member = place_ref[0] & 1, place_ref[1]
    rows = owns[0].shape[0]
    bits = bit_count(groups)
    part_ref[...] = lax.dot_general(
        agg_ref[...], pre_grad_ref[...], (((0,), (0,)), ((), ())), preferred_element_type=jnp.float32
    )

    def piece(k, side):
        start = (2 * (member ^ between(k, 1 - side, bits)) + side) * rows
        return part_ref[pl.ds(pl.multiple_of(start, rows), rows), :]

    for k in range(groups):
        owns[k][...] = piece(k, core)
        send_ref[k * rows:(k + 1) * rows, :] = piece(k, 1 - core).astype(send_ref.dtype)


def weight_part(agg, pre_grad, place, groups):
    rows, width = agg.shape
    part = width // (2 * groups)
    out = pl.pallas_call(
        functools.partial(weight_kernel, groups=groups),
        out_shape=[like((part, width), jnp.float32)] * groups + [like((groups * part, width), jnp.bfloat16)],
        in_specs=[SCALARS, WHOLE, WHOLE],
        out_specs=[WHOLE] * (groups + 1),
        scratch_shapes=[pltpu.VMEM((width, width), jnp.float32)],
        compiler_params=params(8),
        cost_estimate=pl.CostEstimate(
            flops=2 * rows * width * width, bytes_accessed=4 * rows * width + 4 * width * width, transcendentals=0),
        name="weight_part",
    )(place, agg, pre_grad)
    return out[:-1], out[-1]


def place_kernel(place_ref, *refs, groups):
    owns, other_ref, out_ref = refs[:groups], refs[groups], refs[groups + 1]
    core, member = place_ref[0] & 1, place_ref[1]
    rows = owns[0].shape[0]
    bits = bit_count(groups)
    for k in range(groups):
        for side, value in ((core, owns[k][...]), (1 - core, other_ref[k * rows:(k + 1) * rows, :])):
            start = (2 * (member ^ between(k, 1 - side, bits)) + side) * rows
            out_ref[pl.ds(pl.multiple_of(start, rows), rows), :] = value


def place_slices(owns, other, place):
    groups = len(owns)
    rows, width = owns[0].shape
    return pl.pallas_call(
        functools.partial(place_kernel, groups=groups),
        out_shape=like((2 * groups * rows, width), jnp.float32),
        in_specs=[SCALARS] + [WHOLE] * (groups + 1),
        out_specs=WHOLE,
        compiler_params=params(8),
        cost_estimate=pl.CostEstimate(flops=0, bytes_accessed=16 * groups * rows * width, transcendentals=0),
        name="place_slices",
    )(place, *owns, other)


def backward_kernel(*refs, side, count, slots):
    blocks, grads, outs = refs[:count], refs[count:count + slots], refs[count + slots:]
    rows = blocks[0].shape[1]
    for i, block in enumerate(blocks):
        total, start = None, 0
        for grad in grads:
            stop = start + grad.shape[0]
            part = bf16_dot(block[side, :, start:stop], grad[...])
            total, start = part if total is None else total + part, stop
        if side:
            outs[0][i * rows:(i + 1) * rows, :] = total.astype(outs[0].dtype)
        else:
            outs[i][...] = total


def backward(blocks, grads, side):
    _, cols, rows = blocks[0].shape
    width = grads[0].shape[1]
    count = len(blocks)
    own = [like((cols, width), jnp.float32)] * count
    return pl.pallas_call(
        functools.partial(backward_kernel, side=side, count=count, slots=len(grads)),
        out_shape=[like((count * cols, width), jnp.bfloat16)] if side else own,
        in_specs=[WHOLE] * (count + len(grads)),
        out_specs=[WHOLE] * (1 if side else count),
        compiler_params=params(8),
        cost_estimate=pl.CostEstimate(
            flops=2 * count * cols * rows * width,
            bytes_accessed=2 * count * cols * rows + 2 * rows * width + 4 * count * cols * width, transcendentals=0),
        name="backward",
    )(*blocks, *grads)


def settle_kernel(*refs, slots, count):
    totals, arrived, outs = refs[:slots], refs[slots:slots + count], refs[slots + count:]
    rows = totals[0].shape[0]
    for k in range(slots):
        total = totals[k][...]
        for ref in arrived:
            total = total + ref[k * rows:(k + 1) * rows, :].astype(jnp.float32)
        outs[k][...] = total.astype(outs[k].dtype)


def settle(totals, arrived, dtypes):
    rows, width = totals[0].shape
    return pl.pallas_call(
        functools.partial(settle_kernel, slots=len(totals), count=len(arrived)),
        out_shape=[like((rows, width), dtype) for dtype in dtypes],
        in_specs=[WHOLE] * (len(totals) + len(arrived)),
        out_specs=[WHOLE] * len(totals),
        compiler_params=params(8),
        cost_estimate=pl.CostEstimate(flops=rows * width, bytes_accessed=8 * rows * width, transcendentals=0),
        name="settle",
    )(*totals, *arrived)


def top_bit(slot):
    return 1 << (slot.bit_length() - 1)


def halve(totals, swap):
    while True:
        half = len(totals) // 2
        send = [total.astype(jnp.bfloat16) for total in totals[half:]]
        got = swap(jnp.concatenate(send) if half > 1 else send[0], half)
        if half == 1:
            return [totals[0], got]
        totals = add_slots(totals[:half], got)


def add_slots(totals, got):
    rows = totals[0].shape[0]
    return [total + got[k * rows:(k + 1) * rows].astype(jnp.float32) for k, total in enumerate(totals)]


def collect(totals, swap):
    totals = list(totals)
    arrived = []
    for k in reversed(range(1, len(totals))):
        got = swap(totals[k].astype(jnp.bfloat16), top_bit(k))
        if k == top_bit(k):
            arrived.append(got)
        else:
            totals[k - top_bit(k)] = totals[k - top_bit(k)].astype(jnp.float32) + got.astype(jnp.float32)
    return [totals[0], *arrived]


def local(features, cotangent, weight, tiles, tile_rows, tile_cols, tile_counts):
    blocks = lax.axis_size("dom")
    groups = lax.axis_size("repl")
    chips = blocks // 2
    rows_local, width = features.shape
    scale = float(rows_local * blocks * groups) ** (-0.5)
    position, member = lax.axis_index("dom"), lax.axis_index("repl")
    place = jnp.stack([position, member]).astype(jnp.int32)

    col_tiles = rows_local // tiles.shape[-1]
    row = tile_rows[0, 0]
    row = between((row // col_tiles) ^ member, position & 1, bit_count(groups)) * col_tiles + row % col_tiles
    spots = jnp.concatenate([row * col_tiles + tile_cols[0, 0], tile_counts[0, 0][:, None]], axis=1)
    dense = densify(tiles[0, 0], spots, place, groups, rows_local)

    held, beside = [features], swap_cores(features)
    for k in range(1, chips):
        given = after(features, beside) if k == top_bit(k) > 1 else held[k - top_bit(k)]
        held.append(swap_chips(given, top_bit(k)))
        if k == 1:
            held[1] = after(held[1], spots)
    totals, half = None, chips // 2
    for first, stop in ((0, chips // 2), (chips // 2, chips)):
        sources = []
        for k in range(first, stop):
            own = held[k] if totals is None else after(held[k], held[-1], *totals)
            sources += [own, swap_cores(own) if k else beside]
        if stop < chips:
            totals = forward(after(dense, held[half]), 2 * first, sources, 0, None, [jnp.float32] * groups)
    upper = groups // 2
    high = forward(dense, 2 * first, sources, upper, totals[upper:], [jnp.bfloat16] * upper)
    low = forward(after(dense, *high), 2 * first, sources, 0, totals[:upper], [jnp.float32] * upper)
    totals = low + high

    pieces = collect(totals, swap_members)
    dense_t = transposed(after(dense, *totals, pieces[1]))
    pieces[-1] = after(pieces[-1], *dense_t)
    activated, agg, pre_grad, grad = middle(pieces, cotangent, weight)
    owns, send = weight_part(agg, pre_grad, place, groups)
    parts = add_slots(owns, swap_cores(send))

    grads = [grad]
    for k in range(1, groups):
        if k == top_bit(k):
            straight = grads[0]
        else:
            straight = after(grads[k - top_bit(k)], grads[top_bit(k)])
        grads.append(swap_members(straight, top_bit(k)))
    part = parts[0]
    for k in range(1, groups):
        part = part + swap_members(parts[k].astype(jnp.bfloat16), k, turn=1).astype(jnp.float32)
    part = part.astype(jnp.bfloat16)
    near = swap_chips(part, 1)
    part = part.astype(jnp.float32) + near.astype(jnp.float32)
    grads[-1] = after(grads[-1], near)

    half = chips // 2
    other = backward(dense_t[half:], grads, 1)
    own = backward([after(dense_t[half], *other), *dense_t[half + 1:]], grads, 0)
    high = jnp.concatenate(add_slots(own, swap_cores(other[0]))).astype(jnp.bfloat16)
    grads[0] = after(grads[0], high)
    other = backward(dense_t[:half], grads, 1)
    totals = backward(dense_t[:half], grads, 0)
    arrived = [swap_cores(other[0]), swap_chips(high, half)]
    while half > 1:
        half //= 2
        totals = settle(totals, arrived, [jnp.float32] * half + [jnp.bfloat16] * half)
        send = jnp.concatenate(totals[half:]) if half > 1 else totals[half]
        totals, arrived = totals[:half], [swap_chips(send, half)]
    (feature_grad,) = settle(totals, arrived, [jnp.bfloat16])

    bit = 2
    while bit < chips:
        part = part.astype(jnp.bfloat16)
        part = part.astype(jnp.float32) + swap_chips(part, bit).astype(jnp.float32)
        bit *= 2
    part = part * scale
    parts = [part] + [swap_members(part, k, turn=1) for k in range(1, groups)]
    weight_grad = place_slices(parts, swap_cores(jnp.concatenate(parts)), place)
    return (activated, feature_grad, weight_grad)


def solution(mesh):
    in_specs = (
        P(("dom", "repl"), None),
        P(("dom", "repl"), None),
        P(),
        P("dom", "repl", None, None, None, None),
        P("dom", "repl", None, None),
        P("dom", "repl", None, None),
        P("dom", "repl", None),
    )
    out_specs = (P(("dom", "repl"), None), P(("dom", "repl"), None), P())
    return jax.shard_map(local, mesh=mesh, in_specs=in_specs, out_specs=out_specs, check_vma=False)
```

```python
import functools

import jax
import jax.numpy as jnp
from jax import lax
from jax.experimental import pallas as pl
from jax.experimental.pallas import tpu as pltpu
from jax.sharding import PartitionSpec as P

WHOLE = pl.BlockSpec(memory_space=pltpu.VMEM)
SCALARS = pl.BlockSpec(memory_space=pltpu.SMEM)


def bit_count(n):
    return n.bit_length() - 1


def between(index, core, bits):
    reverse = 0
    for i in range(bits):
        reverse = reverse | (((index >> i) & 1) << (bits - 1 - i))
    return core * index + (1 - core) * reverse


def swap_cores(x):
    return lax.ppermute(x, "dom", [(i, i ^ 1) for i in range(lax.axis_size("dom"))])


def swap_chips(x, held):
    blocks = lax.axis_size("dom")
    bits = bit_count(blocks // 2)
    return lax.ppermute(x, "dom", [(i, i ^ (2 * between(held, i % 2, bits))) for i in range(blocks)])


def swap_members(x, held, turn=0):
    blocks, groups = lax.axis_size("dom"), lax.axis_size("repl")
    bits = bit_count(groups)
    pairs = []
    for i in range(blocks):
        for j in range(groups):
            pairs.append((i * groups + j, i * groups + (j ^ between(held, (i % 2) ^ turn, bits))))
    return lax.ppermute(x, ("dom", "repl"), pairs)


def after(x, *others):
    return lax.optimization_barrier((x, *others))[0]


def params(mib):
    return pltpu.CompilerParams(vmem_limit_bytes=mib * 1024 * 1024)


def like(shape, dtype):
    return jax.ShapeDtypeStruct(shape, dtype)


def bf16_dot(a, b):
    return jnp.dot(a, b, preferred_element_type=jnp.float32)


def column_of(position, j, blocks):
    core = (position & 1) ^ (j & 1)
    return (((position >> 1) ^ between(j >> 1, core, bit_count(blocks // 2))) << 1) | core


def densify_kernel(spots_ref, place_ref, tiles_ref, a_ref, acc_ref, *, col_tiles):
    column = column_of(place_ref[0], pl.program_id(0), pl.num_programs(0))
    size = tiles_ref.shape[-1]
    count = tiles_ref.shape[1]
    acc_ref[...] = jnp.zeros_like(acc_ref)

    def add(tile, carry):
        acc_ref[spots_ref[column, tile]] += tiles_ref[0, tile].astype(jnp.float32)
        return carry

    lax.fori_loop(0, spots_ref[column, count], add, 0)
    for spot in range(acc_ref.shape[0]):
        row, col = spot // col_tiles, spot % col_tiles
        a_ref[0, row * size:(row + 1) * size, col * size:(col + 1) * size] = acc_ref[spot].astype(a_ref.dtype)


def densify(tiles, spots, place, group_count, rows_local):
    columns, count, size, _ = tiles.shape
    col_tiles = rows_local // size
    rows = group_count * rows_local
    return pl.pallas_call(
        functools.partial(densify_kernel, col_tiles=col_tiles),
        out_shape=like((columns, rows, rows_local), jnp.bfloat16),
        grid_spec=pltpu.PrefetchScalarGridSpec(
            num_scalar_prefetch=2,
            grid=(columns,),
            in_specs=[pl.BlockSpec((1, count, size, size), lambda j, s, p: (column_of(p[0], j, columns), 0, 0, 0))],
            out_specs=pl.BlockSpec((1, rows, rows_local), lambda j, *_: (j, 0, 0)),
            scratch_shapes=[pltpu.VMEM((group_count * col_tiles * col_tiles, size, size), jnp.float32)],
        ),
        compiler_params=params(12),
        cost_estimate=pl.CostEstimate(
            flops=columns * count * size * size, bytes_accessed=8 * rows * columns * rows_local, transcendentals=0),
        name="densify",
    )(spots, place, tiles)


def transpose_kernel(a_ref, *outs):
    for i, out_ref in enumerate(outs):
        for side in range(2):
            out_ref[side] = a_ref[2 * i + side].T


def transposed(dense):
    columns, rows, cols = dense.shape
    return pl.pallas_call(
        transpose_kernel,
        out_shape=[like((2, cols, rows), jnp.bfloat16)] * (columns // 2),
        in_specs=[WHOLE],
        out_specs=[WHOLE] * (columns // 2),
        compiler_params=params(8),
        cost_estimate=pl.CostEstimate(flops=0, bytes_accessed=4 * columns * rows * cols, transcendentals=0),
        name="transposed",
    )(dense)


def forward_kernel(*refs, which, base, slots, has_prev):
    count = len(which)
    dense_ref, sources = refs[0], refs[1:1 + count]
    rest = refs[1 + count:]
    prev, outs = (rest[:slots], rest[slots:]) if has_prev else (None, rest)
    rows = outs[0].shape[0]
    for k, out_ref in reversed(list(enumerate(outs))):
        total = prev[k][...] if has_prev else None
        for j, source in zip(which, sources):
            part = bf16_dot(dense_ref[j, (base + k) * rows:(base + k + 1) * rows, :], source[...])
            total = part if total is None else total + part
        out_ref[...] = total.astype(out_ref.dtype)


def forward(dense, which, sources, base, prev, dtypes):
    slots = len(dtypes)
    depth, width = sources[0].shape
    rows = slots * depth
    return pl.pallas_call(
        functools.partial(
            forward_kernel, which=which, base=base, slots=slots, has_prev=prev is not None),
        out_shape=[like((depth, width), dtype) for dtype in dtypes],
        in_specs=[WHOLE] * (1 + len(sources) + (slots if prev is not None else 0)),
        out_specs=[WHOLE] * slots,
        compiler_params=params(8),
        cost_estimate=pl.CostEstimate(
            flops=2 * len(sources) * rows * depth * width,
            bytes_accessed=2 * len(sources) * rows * depth + 4 * rows * width, transcendentals=0),
        name="forward",
    )(dense, *sources, *(prev or []))


def middle_kernel(*refs):
    pieces, (cot_ref, weight_ref, act_ref, agg_ref, pre_grad_ref, grad_ref) = refs[:-6], refs[-6:]
    agg = pieces[0][...]
    for piece in pieces[1:]:
        agg = agg + piece[...].astype(jnp.float32)
    agg = agg.astype(jnp.bfloat16)
    agg_ref[...] = agg
    weight = weight_ref[...]
    preact = bf16_dot(agg, weight)
    sigma = jax.nn.sigmoid(preact)
    act_ref[...] = (preact * sigma).astype(act_ref.dtype)
    slope = sigma * (1.0 + preact * (1.0 - sigma))
    pre_grad = (cot_ref[...].astype(jnp.float32) * slope).astype(jnp.bfloat16)
    pre_grad_ref[...] = pre_grad
    grad_ref[...] = lax.dot_general(
        pre_grad, weight, (((1,), (1,)), ((), ())), preferred_element_type=jnp.float32
    ).astype(jnp.bfloat16)


def middle(pieces, cotangent, weight):
    rows, width = cotangent.shape
    return pl.pallas_call(
        middle_kernel,
        out_shape=[like((rows, width), jnp.bfloat16)] * 4,
        in_specs=[WHOLE] * (2 + len(pieces)),
        out_specs=[WHOLE] * 4,
        compiler_params=params(8),
        cost_estimate=pl.CostEstimate(
            flops=4 * rows * width * width, bytes_accessed=10 * rows * width, transcendentals=rows * width),
        name="middle",
    )(*pieces, cotangent, weight)


def weight_kernel(place_ref, agg_ref, pre_grad_ref, *refs, groups):
    owns, send_ref, part_ref = refs[:groups], refs[groups], refs[groups + 1]
    core, member = place_ref[0] & 1, place_ref[1]
    rows = owns[0].shape[0]
    bits = bit_count(groups)
    part_ref[...] = lax.dot_general(
        agg_ref[...], pre_grad_ref[...], (((0,), (0,)), ((), ())), preferred_element_type=jnp.float32
    )

    def piece(k, side):
        start = (2 * (member ^ between(k, 1 - side, bits)) + side) * rows
        return part_ref[pl.ds(pl.multiple_of(start, rows), rows), :]

    for k in range(groups):
        owns[k][...] = piece(k, core)
        send_ref[k * rows:(k + 1) * rows, :] = piece(k, 1 - core).astype(send_ref.dtype)


def weight_part(agg, pre_grad, place, groups):
    rows, width = agg.shape
    part = width // (2 * groups)
    out = pl.pallas_call(
        functools.partial(weight_kernel, groups=groups),
        out_shape=[like((part, width), jnp.float32)] * groups + [like((groups * part, width), jnp.bfloat16)],
        in_specs=[SCALARS, WHOLE, WHOLE],
        out_specs=[WHOLE] * (groups + 1),
        scratch_shapes=[pltpu.VMEM((width, width), jnp.float32)],
        compiler_params=params(8),
        cost_estimate=pl.CostEstimate(
            flops=2 * rows * width * width, bytes_accessed=4 * rows * width + 4 * width * width, transcendentals=0),
        name="weight_part",
    )(place, agg, pre_grad)
    return out[:-1], out[-1]


def place_kernel(place_ref, *refs, groups):
    owns, other_ref, out_ref = refs[:groups], refs[groups], refs[groups + 1]
    core, member = place_ref[0] & 1, place_ref[1]
    rows = owns[0].shape[0]
    bits = bit_count(groups)
    for k in range(groups):
        for side, value in ((core, owns[k][...]), (1 - core, other_ref[k * rows:(k + 1) * rows, :])):
            start = (2 * (member ^ between(k, 1 - side, bits)) + side) * rows
            out_ref[pl.ds(pl.multiple_of(start, rows), rows), :] = value


def place_slices(owns, other, place):
    groups = len(owns)
    rows, width = owns[0].shape
    return pl.pallas_call(
        functools.partial(place_kernel, groups=groups),
        out_shape=like((2 * groups * rows, width), jnp.float32),
        in_specs=[SCALARS] + [WHOLE] * (groups + 1),
        out_specs=WHOLE,
        compiler_params=params(8),
        cost_estimate=pl.CostEstimate(flops=0, bytes_accessed=16 * groups * rows * width, transcendentals=0),
        name="place_slices",
    )(place, *owns, other)


def backward_kernel(*refs, side, count, slots):
    blocks, grads, outs = refs[:count], refs[count:count + slots], refs[count + slots:]
    rows = blocks[0].shape[1]
    for i, block in enumerate(blocks):
        total, start = None, 0
        for grad in grads:
            stop = start + grad.shape[0]
            part = bf16_dot(block[side, :, start:stop], grad[...])
            total, start = part if total is None else total + part, stop
        if side:
            outs[0][i * rows:(i + 1) * rows, :] = total.astype(outs[0].dtype)
        else:
            outs[i][...] = total


def backward(blocks, grads, side):
    _, cols, rows = blocks[0].shape
    width = grads[0].shape[1]
    count = len(blocks)
    own = [like((cols, width), jnp.float32)] * count
    return pl.pallas_call(
        functools.partial(backward_kernel, side=side, count=count, slots=len(grads)),
        out_shape=[like((count * cols, width), jnp.bfloat16)] if side else own,
        in_specs=[WHOLE] * (count + len(grads)),
        out_specs=[WHOLE] * (1 if side else count),
        compiler_params=params(8),
        cost_estimate=pl.CostEstimate(
            flops=2 * count * cols * rows * width,
            bytes_accessed=2 * count * cols * rows + 2 * rows * width + 4 * count * cols * width, transcendentals=0),
        name="backward",
    )(*blocks, *grads)


def settle_kernel(*refs, slots, count):
    totals, arrived, outs = refs[:slots], refs[slots:slots + count], refs[slots + count:]
    rows = totals[0].shape[0]
    for k in range(slots):
        total = totals[k][...]
        for ref in arrived:
            total = total + ref[k * rows:(k + 1) * rows, :].astype(jnp.float32)
        outs[k][...] = total.astype(outs[k].dtype)


def settle(totals, arrived, dtypes):
    rows, width = totals[0].shape
    return pl.pallas_call(
        functools.partial(settle_kernel, slots=len(totals), count=len(arrived)),
        out_shape=[like((rows, width), dtype) for dtype in dtypes],
        in_specs=[WHOLE] * (len(totals) + len(arrived)),
        out_specs=[WHOLE] * len(totals),
        compiler_params=params(8),
        cost_estimate=pl.CostEstimate(flops=rows * width, bytes_accessed=8 * rows * width, transcendentals=0),
        name="settle",
    )(*totals, *arrived)


def top_bit(slot):
    return 1 << (slot.bit_length() - 1)


def halve(totals, swap):
    while True:
        half = len(totals) // 2
        send = [total.astype(jnp.bfloat16) for total in totals[half:]]
        got = swap(jnp.concatenate(send) if half > 1 else send[0], half)
        if half == 1:
            return [totals[0], got]
        totals = add_slots(totals[:half], got)


def add_slots(totals, got):
    rows = totals[0].shape[0]
    return [total + got[k * rows:(k + 1) * rows].astype(jnp.float32) for k, total in enumerate(totals)]


def collect(totals, swap):
    totals = list(totals)
    arrived = []
    for k in reversed(range(1, len(totals))):
        got = swap(totals[k].astype(jnp.bfloat16), top_bit(k))
        if k == top_bit(k):
            arrived.append(got)
        else:
            totals[k - top_bit(k)] = totals[k - top_bit(k)].astype(jnp.float32) + got.astype(jnp.float32)
    return [totals[0], *arrived]


def local(features, cotangent, weight, tiles, tile_rows, tile_cols, tile_counts):
    blocks = lax.axis_size("dom")
    groups = lax.axis_size("repl")
    chips = blocks // 2
    rows_local, width = features.shape
    scale = float(rows_local * blocks * groups) ** (-0.5)
    position, member = lax.axis_index("dom"), lax.axis_index("repl")
    place = jnp.stack([position, member]).astype(jnp.int32)

    col_tiles = rows_local // tiles.shape[-1]
    row = tile_rows[0, 0]
    row = between((row // col_tiles) ^ member, position & 1, bit_count(groups)) * col_tiles + row % col_tiles
    spots = jnp.concatenate([row * col_tiles + tile_cols[0, 0], tile_counts[0, 0][:, None]], axis=1)
    dense = densify(tiles[0, 0], spots, place, groups, rows_local)

    held = [features]
    for k in range(1, chips):
        given = after(features, held[k - 1]) if k == top_bit(k) > 1 else held[k - top_bit(k)]
        held.append(swap_chips(given, top_bit(k)))
        if k == 1:
            held[1] = after(held[1], spots)
    half, upper = chips // 2, groups // 2
    sources = [x for own in held[:half] for x in (own, swap_cores(own))]
    totals = forward(dense, list(range(2 * half)), sources, 0, None, [jnp.float32] * groups)
    far = [after(own, *totals) for own in held[half:]]
    others = [swap_cores(own) for own in far]
    totals = forward(dense, list(range(2 * half, 2 * chips, 2)), far, 0, totals, [jnp.float32] * groups)
    odd = list(range(2 * half + 1, 2 * chips, 2))
    high = forward(dense, odd, others, upper, totals[upper:], [jnp.bfloat16] * upper)
    low = forward(after(dense, *high), odd, others, 0, totals[:upper], [jnp.float32] * upper)
    totals = low + high

    pieces = collect(totals, swap_members)
    dense_t = transposed(after(dense, *totals, pieces[1]))
    pieces[-1] = after(pieces[-1], *dense_t)
    activated, agg, pre_grad, grad = middle(pieces, cotangent, weight)
    owns, send = weight_part(agg, pre_grad, place, groups)
    parts = add_slots(owns, swap_cores(send))

    grads = [grad]
    for k in range(1, groups):
        if k == top_bit(k):
            straight = grads[0]
        else:
            straight = after(grads[k - top_bit(k)], grads[top_bit(k)])
        grads.append(swap_members(straight, top_bit(k)))
    part = parts[0]
    for k in range(1, groups):
        part = part + swap_members(parts[k].astype(jnp.bfloat16), k, turn=1).astype(jnp.float32)
    part = part.astype(jnp.bfloat16)
    near = swap_chips(part, 1)
    part = part.astype(jnp.float32) + near.astype(jnp.float32)
    grads[-1] = after(grads[-1], near)

    half = chips // 2
    other = backward(dense_t[half:], grads, 1)
    own = backward([after(dense_t[half], *other), *dense_t[half + 1:]], grads, 0)
    high = jnp.concatenate(add_slots(own, swap_cores(other[0]))).astype(jnp.bfloat16)
    grads[0] = after(grads[0], high)
    other = backward(dense_t[:half], grads, 1)
    totals = backward(dense_t[:half], grads, 0)
    arrived = [swap_cores(other[0]), swap_chips(high, half)]
    while half > 1:
        half //= 2
        totals = settle(totals, arrived, [jnp.float32] * half + [jnp.bfloat16] * half)
        send = jnp.concatenate(totals[half:]) if half > 1 else totals[half]
        totals, arrived = totals[:half], [swap_chips(send, half)]
    (feature_grad,) = settle(totals, arrived, [jnp.bfloat16])

    bit = 2
    while bit < chips:
        part = part.astype(jnp.bfloat16)
        part = part.astype(jnp.float32) + swap_chips(part, bit).astype(jnp.float32)
        bit *= 2
    part = part * scale
    parts = [part] + [swap_members(part, k, turn=1) for k in range(1, groups)]
    weight_grad = place_slices(parts, swap_cores(jnp.concatenate(parts)), place)
    return (activated, feature_grad, weight_grad)


def solution(mesh):
    in_specs = (
        P(("dom", "repl"), None),
        P(("dom", "repl"), None),
        P(),
        P("dom", "repl", None, None, None, None),
        P("dom", "repl", None, None),
        P("dom", "repl", None, None),
        P("dom", "repl", None),
    )
    out_specs = (P(("dom", "repl"), None), P(("dom", "repl"), None), P())
    return jax.shard_map(local, mesh=mesh, in_specs=in_specs, out_specs=out_specs, check_vma=False)
```

```python
import functools

import jax
import jax.numpy as jnp
from jax import lax
from jax.experimental import pallas as pl
from jax.experimental.pallas import tpu as pltpu
from jax.sharding import PartitionSpec as P

WHOLE = pl.BlockSpec(memory_space=pltpu.VMEM)
SCALARS = pl.BlockSpec(memory_space=pltpu.SMEM)


def bit_count(n):
    return n.bit_length() - 1


def between(index, core, bits):
    reverse = 0
    for i in range(bits):
        reverse = reverse | (((index >> i) & 1) << (bits - 1 - i))
    return core * index + (1 - core) * reverse


def swap_cores(x):
    return lax.ppermute(x, "dom", [(i, i ^ 1) for i in range(lax.axis_size("dom"))])


def swap_chips(x, held):
    blocks = lax.axis_size("dom")
    bits = bit_count(blocks // 2)
    return lax.ppermute(x, "dom", [(i, i ^ (2 * between(held, i % 2, bits))) for i in range(blocks)])


def swap_members(x, held, turn=0):
    blocks, groups = lax.axis_size("dom"), lax.axis_size("repl")
    bits = bit_count(groups)
    pairs = []
    for i in range(blocks):
        for j in range(groups):
            pairs.append((i * groups + j, i * groups + (j ^ between(held, (i % 2) ^ turn, bits))))
    return lax.ppermute(x, ("dom", "repl"), pairs)


def after(x, *others):
    return lax.optimization_barrier((x, *others))[0]


def params(mib):
    return pltpu.CompilerParams(vmem_limit_bytes=mib * 1024 * 1024)


def like(shape, dtype):
    return jax.ShapeDtypeStruct(shape, dtype)


def bf16_dot(a, b):
    return jnp.dot(a, b, preferred_element_type=jnp.float32)


def column_of(position, j, blocks):
    core = (position & 1) ^ (j & 1)
    return (((position >> 1) ^ between(j >> 1, core, bit_count(blocks // 2))) << 1) | core


def densify_kernel(spots_ref, place_ref, tiles_ref, a_ref, acc_ref, *, col_tiles):
    column = column_of(place_ref[0], pl.program_id(0), pl.num_programs(0))
    size = tiles_ref.shape[-1]
    count = tiles_ref.shape[1]
    acc_ref[...] = jnp.zeros_like(acc_ref)

    def add(tile, carry):
        acc_ref[spots_ref[column, tile]] += tiles_ref[0, tile].astype(jnp.float32)
        return carry

    lax.fori_loop(0, spots_ref[column, count], add, 0)
    for spot in range(acc_ref.shape[0]):
        row, col = spot // col_tiles, spot % col_tiles
        a_ref[0, row * size:(row + 1) * size, col * size:(col + 1) * size] = acc_ref[spot].astype(a_ref.dtype)


def densify(tiles, spots, place, group_count, rows_local):
    columns, count, size, _ = tiles.shape
    col_tiles = rows_local // size
    rows = group_count * rows_local
    return pl.pallas_call(
        functools.partial(densify_kernel, col_tiles=col_tiles),
        out_shape=like((columns, rows, rows_local), jnp.bfloat16),
        grid_spec=pltpu.PrefetchScalarGridSpec(
            num_scalar_prefetch=2,
            grid=(columns,),
            in_specs=[pl.BlockSpec((1, count, size, size), lambda j, s, p: (column_of(p[0], j, columns), 0, 0, 0))],
            out_specs=pl.BlockSpec((1, rows, rows_local), lambda j, *_: (j, 0, 0)),
            scratch_shapes=[pltpu.VMEM((group_count * col_tiles * col_tiles, size, size), jnp.float32)],
        ),
        compiler_params=params(12),
        cost_estimate=pl.CostEstimate(
            flops=columns * count * size * size, bytes_accessed=8 * rows * columns * rows_local, transcendentals=0),
        name="densify",
    )(spots, place, tiles)


def transpose_kernel(a_ref, *outs):
    for i, out_ref in enumerate(outs):
        for side in range(2):
            out_ref[side] = a_ref[2 * i + side].T


def transposed(dense):
    columns, rows, cols = dense.shape
    return pl.pallas_call(
        transpose_kernel,
        out_shape=[like((2, cols, rows), jnp.bfloat16)] * (columns // 2),
        in_specs=[WHOLE],
        out_specs=[WHOLE] * (columns // 2),
        compiler_params=params(8),
        cost_estimate=pl.CostEstimate(flops=0, bytes_accessed=4 * columns * rows * cols, transcendentals=0),
        name="transposed",
    )(dense)


def forward_kernel(*refs, which, base, slots, has_prev):
    count = len(which)
    dense_ref, sources = refs[0], refs[1:1 + count]
    rest = refs[1 + count:]
    prev, outs = (rest[:slots], rest[slots:]) if has_prev else (None, rest)
    rows = outs[0].shape[0]
    for k, out_ref in reversed(list(enumerate(outs))):
        total = prev[k][...] if has_prev else None
        for j, source in zip(which, sources):
            part = bf16_dot(dense_ref[j, (base + k) * rows:(base + k + 1) * rows, :], source[...])
            total = part if total is None else total + part
        out_ref[...] = total.astype(out_ref.dtype)


def forward(dense, which, sources, base, prev, dtypes):
    slots = len(dtypes)
    depth, width = sources[0].shape
    rows = slots * depth
    return pl.pallas_call(
        functools.partial(
            forward_kernel, which=which, base=base, slots=slots, has_prev=prev is not None),
        out_shape=[like((depth, width), dtype) for dtype in dtypes],
        in_specs=[WHOLE] * (1 + len(sources) + (slots if prev is not None else 0)),
        out_specs=[WHOLE] * slots,
        compiler_params=params(8),
        cost_estimate=pl.CostEstimate(
            flops=2 * len(sources) * rows * depth * width,
            bytes_accessed=2 * len(sources) * rows * depth + 4 * rows * width, transcendentals=0),
        name="forward",
    )(dense, *sources, *(prev or []))


def middle_kernel(*refs):
    pieces, (cot_ref, weight_ref, act_ref, agg_ref, pre_grad_ref, grad_ref) = refs[:-6], refs[-6:]
    agg = pieces[0][...]
    for piece in pieces[1:]:
        agg = agg + piece[...].astype(jnp.float32)
    agg = agg.astype(jnp.bfloat16)
    agg_ref[...] = agg
    weight = weight_ref[...]
    preact = bf16_dot(agg, weight)
    sigma = jax.nn.sigmoid(preact)
    act_ref[...] = (preact * sigma).astype(act_ref.dtype)
    slope = sigma * (1.0 + preact * (1.0 - sigma))
    pre_grad = (cot_ref[...].astype(jnp.float32) * slope).astype(jnp.bfloat16)
    pre_grad_ref[...] = pre_grad
    grad_ref[...] = lax.dot_general(
        pre_grad, weight, (((1,), (1,)), ((), ())), preferred_element_type=jnp.float32
    ).astype(jnp.bfloat16)


def middle(pieces, cotangent, weight):
    rows, width = cotangent.shape
    return pl.pallas_call(
        middle_kernel,
        out_shape=[like((rows, width), jnp.bfloat16)] * 4,
        in_specs=[WHOLE] * (2 + len(pieces)),
        out_specs=[WHOLE] * 4,
        compiler_params=params(8),
        cost_estimate=pl.CostEstimate(
            flops=4 * rows * width * width, bytes_accessed=10 * rows * width, transcendentals=rows * width),
        name="middle",
    )(*pieces, cotangent, weight)


def weight_kernel(place_ref, agg_ref, pre_grad_ref, *refs, groups):
    owns, send_ref, part_ref = refs[:groups], refs[groups], refs[groups + 1]
    core, member = place_ref[0] & 1, place_ref[1]
    rows = owns[0].shape[0]
    bits = bit_count(groups)
    part_ref[...] = lax.dot_general(
        agg_ref[...], pre_grad_ref[...], (((0,), (0,)), ((), ())), preferred_element_type=jnp.float32
    )

    def piece(k, side):
        start = (2 * (member ^ between(k, 1 - side, bits)) + side) * rows
        return part_ref[pl.ds(pl.multiple_of(start, rows), rows), :]

    for k in range(groups):
        owns[k][...] = piece(k, core)
        send_ref[k * rows:(k + 1) * rows, :] = piece(k, 1 - core).astype(send_ref.dtype)


def weight_part(agg, pre_grad, place, groups):
    rows, width = agg.shape
    part = width // (2 * groups)
    out = pl.pallas_call(
        functools.partial(weight_kernel, groups=groups),
        out_shape=[like((part, width), jnp.float32)] * groups + [like((groups * part, width), jnp.bfloat16)],
        in_specs=[SCALARS, WHOLE, WHOLE],
        out_specs=[WHOLE] * (groups + 1),
        scratch_shapes=[pltpu.VMEM((width, width), jnp.float32)],
        compiler_params=params(8),
        cost_estimate=pl.CostEstimate(
            flops=2 * rows * width * width, bytes_accessed=4 * rows * width + 4 * width * width, transcendentals=0),
        name="weight_part",
    )(place, agg, pre_grad)
    return out[:-1], out[-1]


def place_kernel(place_ref, *refs, groups):
    owns, other_ref, out_ref = refs[:groups], refs[groups], refs[groups + 1]
    core, member = place_ref[0] & 1, place_ref[1]
    rows = owns[0].shape[0]
    bits = bit_count(groups)
    for k in range(groups):
        for side, value in ((core, owns[k][...]), (1 - core, other_ref[k * rows:(k + 1) * rows, :])):
            start = (2 * (member ^ between(k, 1 - side, bits)) + side) * rows
            out_ref[pl.ds(pl.multiple_of(start, rows), rows), :] = value


def place_slices(owns, other, place):
    groups = len(owns)
    rows, width = owns[0].shape
    return pl.pallas_call(
        functools.partial(place_kernel, groups=groups),
        out_shape=like((2 * groups * rows, width), jnp.float32),
        in_specs=[SCALARS] + [WHOLE] * (groups + 1),
        out_specs=WHOLE,
        compiler_params=params(8),
        cost_estimate=pl.CostEstimate(flops=0, bytes_accessed=16 * groups * rows * width, transcendentals=0),
        name="place_slices",
    )(place, *owns, other)


def backward_kernel(*refs, side, count, slots):
    blocks, grads, outs = refs[:count], refs[count:count + slots], refs[count + slots:]
    rows = blocks[0].shape[1]
    for i, block in enumerate(blocks):
        total, start = None, 0
        for grad in grads:
            stop = start + grad.shape[0]
            part = bf16_dot(block[side, :, start:stop], grad[...])
            total, start = part if total is None else total + part, stop
        if side:
            outs[0][i * rows:(i + 1) * rows, :] = total.astype(outs[0].dtype)
        else:
            outs[i][...] = total


def backward(blocks, grads, side):
    _, cols, rows = blocks[0].shape
    width = grads[0].shape[1]
    count = len(blocks)
    own = [like((cols, width), jnp.float32)] * count
    return pl.pallas_call(
        functools.partial(backward_kernel, side=side, count=count, slots=len(grads)),
        out_shape=[like((count * cols, width), jnp.bfloat16)] if side else own,
        in_specs=[WHOLE] * (count + len(grads)),
        out_specs=[WHOLE] * (1 if side else count),
        compiler_params=params(8),
        cost_estimate=pl.CostEstimate(
            flops=2 * count * cols * rows * width,
            bytes_accessed=2 * count * cols * rows + 2 * rows * width + 4 * count * cols * width, transcendentals=0),
        name="backward",
    )(*blocks, *grads)


def settle_kernel(*refs, slots, count):
    totals, arrived, outs = refs[:slots], refs[slots:slots + count], refs[slots + count:]
    rows = totals[0].shape[0]
    for k in range(slots):
        total = totals[k][...]
        for ref in arrived:
            total = total + ref[k * rows:(k + 1) * rows, :].astype(jnp.float32)
        outs[k][...] = total.astype(outs[k].dtype)


def settle(totals, arrived, dtypes):
    rows, width = totals[0].shape
    return pl.pallas_call(
        functools.partial(settle_kernel, slots=len(totals), count=len(arrived)),
        out_shape=[like((rows, width), dtype) for dtype in dtypes],
        in_specs=[WHOLE] * (len(totals) + len(arrived)),
        out_specs=[WHOLE] * len(totals),
        compiler_params=params(8),
        cost_estimate=pl.CostEstimate(flops=rows * width, bytes_accessed=8 * rows * width, transcendentals=0),
        name="settle",
    )(*totals, *arrived)


def top_bit(slot):
    return 1 << (slot.bit_length() - 1)


def halve(totals, swap):
    while True:
        half = len(totals) // 2
        send = [total.astype(jnp.bfloat16) for total in totals[half:]]
        got = swap(jnp.concatenate(send) if half > 1 else send[0], half)
        if half == 1:
            return [totals[0], got]
        totals = add_slots(totals[:half], got)


def add_slots(totals, got):
    rows = totals[0].shape[0]
    return [total + got[k * rows:(k + 1) * rows].astype(jnp.float32) for k, total in enumerate(totals)]


def collect(totals, swap):
    totals = list(totals)
    arrived = []
    for k in reversed(range(1, len(totals))):
        got = swap(totals[k].astype(jnp.bfloat16), top_bit(k))
        if k == top_bit(k):
            arrived.append(got)
        else:
            totals[k - top_bit(k)] = totals[k - top_bit(k)].astype(jnp.float32) + got.astype(jnp.float32)
    return [totals[0], *arrived]


def local(features, cotangent, weight, tiles, tile_rows, tile_cols, tile_counts):
    blocks = lax.axis_size("dom")
    groups = lax.axis_size("repl")
    chips = blocks // 2
    rows_local, width = features.shape
    scale = float(rows_local * blocks * groups) ** (-0.5)
    position, member = lax.axis_index("dom"), lax.axis_index("repl")
    place = jnp.stack([position, member]).astype(jnp.int32)

    col_tiles = rows_local // tiles.shape[-1]
    row = tile_rows[0, 0]
    row = between((row // col_tiles) ^ member, position & 1, bit_count(groups)) * col_tiles + row % col_tiles
    spots = jnp.concatenate([row * col_tiles + tile_cols[0, 0], tile_counts[0, 0][:, None]], axis=1)
    dense = densify(tiles[0, 0], spots, place, groups, rows_local)

    held = [features]
    for k in range(1, chips):
        given = after(features, held[k - 1]) if k == top_bit(k) > 1 else held[k - top_bit(k)]
        held.append(swap_chips(given, top_bit(k)))
        if k == 1:
            held[1] = after(held[1], spots)
    half, upper = chips // 2, groups // 2
    sources = [x for own in held[:half] for x in (own, swap_cores(own))]
    totals = forward(dense, list(range(2 * half)), sources, 0, None, [jnp.float32] * groups)
    far = [after(own, *totals) for own in held[half:]]
    others = [swap_cores(own) for own in far]
    totals = forward(dense, list(range(2 * half, 2 * chips, 2)), far, 0, totals, [jnp.float32] * groups)
    odd = list(range(2 * half + 1, 2 * chips, 2))
    high = forward(dense, odd, others, upper, totals[upper:], [jnp.bfloat16] * upper)
    low = forward(after(dense, *high), odd, others, 0, totals[:upper], [jnp.float32] * upper)
    totals = low + high

    pieces = collect(totals, swap_members)
    dense_t = transposed(after(dense, *totals, pieces[1]))
    pieces[-1] = after(pieces[-1], *dense_t)
    activated, agg, pre_grad, grad = middle(pieces, cotangent, weight)
    owns, send = weight_part(agg, pre_grad, place, groups)
    parts = add_slots(owns, swap_cores(send))

    grads = [grad]
    for k in range(1, groups):
        grads.append(swap_members(grads[k - top_bit(k)], top_bit(k)))
    part = parts[0]
    for k in range(1, groups):
        part = part + swap_members(parts[k].astype(jnp.bfloat16), k, turn=1).astype(jnp.float32)
    part = part.astype(jnp.bfloat16)
    near = swap_chips(part, 1)
    part = part.astype(jnp.float32) + near.astype(jnp.float32)
    grads[-1] = after(grads[-1], near)

    half = chips // 2
    other = backward(dense_t[half:], grads, 1)
    own = backward([after(dense_t[half], *other), *dense_t[half + 1:]], grads, 0)
    high = jnp.concatenate(add_slots(own, swap_cores(other[0]))).astype(jnp.bfloat16)
    grads[0] = after(grads[0], high)
    other = backward(dense_t[:half], grads, 1)
    totals = backward(dense_t[:half], grads, 0)
    arrived = [swap_cores(other[0]), swap_chips(high, half)]
    while half > 1:
        half //= 2
        totals = settle(totals, arrived, [jnp.float32] * half + [jnp.bfloat16] * half)
        send = jnp.concatenate(totals[half:]) if half > 1 else totals[half]
        totals, arrived = totals[:half], [swap_chips(send, half)]
    (feature_grad,) = settle(totals, arrived, [jnp.bfloat16])

    bit = 2
    while bit < chips:
        part = part.astype(jnp.bfloat16)
        part = part.astype(jnp.float32) + swap_chips(part, bit).astype(jnp.float32)
        bit *= 2
    part = part * scale
    parts = [part] + [swap_members(part, k, turn=1) for k in range(1, groups)]
    weight_grad = place_slices(parts, swap_cores(jnp.concatenate(parts)), place)
    return (activated, feature_grad, weight_grad)


def solution(mesh):
    in_specs = (
        P(("dom", "repl"), None),
        P(("dom", "repl"), None),
        P(),
        P("dom", "repl", None, None, None, None),
        P("dom", "repl", None, None),
        P("dom", "repl", None, None),
        P("dom", "repl", None),
    )
    out_specs = (P(("dom", "repl"), None), P(("dom", "repl"), None), P())
    return jax.shard_map(local, mesh=mesh, in_specs=in_specs, out_specs=out_specs, check_vma=False)
```

```python
import functools

import jax
import jax.numpy as jnp
from jax import lax
from jax.experimental import pallas as pl
from jax.experimental.pallas import tpu as pltpu
from jax.sharding import PartitionSpec as P

WHOLE = pl.BlockSpec(memory_space=pltpu.VMEM)
SCALARS = pl.BlockSpec(memory_space=pltpu.SMEM)


def bit_count(n):
    return n.bit_length() - 1


def between(index, core, bits):
    reverse = 0
    for i in range(bits):
        reverse = reverse | (((index >> i) & 1) << (bits - 1 - i))
    return core * index + (1 - core) * reverse


def swap_cores(x):
    return lax.ppermute(x, "dom", [(i, i ^ 1) for i in range(lax.axis_size("dom"))])


def swap_chips(x, held):
    blocks = lax.axis_size("dom")
    bits = bit_count(blocks // 2)
    return lax.ppermute(x, "dom", [(i, i ^ (2 * between(held, i % 2, bits))) for i in range(blocks)])


def swap_members(x, held, turn=0):
    blocks, groups = lax.axis_size("dom"), lax.axis_size("repl")
    bits = bit_count(groups)
    pairs = []
    for i in range(blocks):
        for j in range(groups):
            pairs.append((i * groups + j, i * groups + (j ^ between(held, (i % 2) ^ turn, bits))))
    return lax.ppermute(x, ("dom", "repl"), pairs)


def after(x, *others):
    return lax.optimization_barrier((x, *others))[0]


def params(mib):
    return pltpu.CompilerParams(vmem_limit_bytes=mib * 1024 * 1024)


def like(shape, dtype):
    return jax.ShapeDtypeStruct(shape, dtype)


def bf16_dot(a, b):
    return jnp.dot(a, b, preferred_element_type=jnp.float32)


def column_of(position, j, blocks):
    core = (position & 1) ^ (j & 1)
    return (((position >> 1) ^ between(j >> 1, core, bit_count(blocks // 2))) << 1) | core


def densify_kernel(spots_ref, place_ref, tiles_ref, a_ref, acc_ref, *, col_tiles):
    column = column_of(place_ref[0], pl.program_id(0), pl.num_programs(0))
    size = tiles_ref.shape[-1]
    count = tiles_ref.shape[1]
    acc_ref[...] = jnp.zeros_like(acc_ref)

    def add(tile, carry):
        acc_ref[spots_ref[column, tile]] += tiles_ref[0, tile].astype(jnp.float32)
        return carry

    lax.fori_loop(0, spots_ref[column, count], add, 0)
    for spot in range(acc_ref.shape[0]):
        row, col = spot // col_tiles, spot % col_tiles
        a_ref[0, row * size:(row + 1) * size, col * size:(col + 1) * size] = acc_ref[spot].astype(a_ref.dtype)


def densify(tiles, spots, place, group_count, rows_local):
    columns, count, size, _ = tiles.shape
    col_tiles = rows_local // size
    rows = group_count * rows_local
    return pl.pallas_call(
        functools.partial(densify_kernel, col_tiles=col_tiles),
        out_shape=like((columns, rows, rows_local), jnp.bfloat16),
        grid_spec=pltpu.PrefetchScalarGridSpec(
            num_scalar_prefetch=2,
            grid=(columns,),
            in_specs=[pl.BlockSpec((1, count, size, size), lambda j, s, p: (column_of(p[0], j, columns), 0, 0, 0))],
            out_specs=pl.BlockSpec((1, rows, rows_local), lambda j, *_: (j, 0, 0)),
            scratch_shapes=[pltpu.VMEM((group_count * col_tiles * col_tiles, size, size), jnp.float32)],
        ),
        compiler_params=params(12),
        cost_estimate=pl.CostEstimate(
            flops=columns * count * size * size, bytes_accessed=8 * rows * columns * rows_local, transcendentals=0),
        name="densify",
    )(spots, place, tiles)


def transpose_kernel(a_ref, *outs):
    for i, out_ref in enumerate(outs):
        for side in range(2):
            out_ref[side] = a_ref[2 * i + side].T


def transposed(dense):
    columns, rows, cols = dense.shape
    return pl.pallas_call(
        transpose_kernel,
        out_shape=[like((2, cols, rows), jnp.bfloat16)] * (columns // 2),
        in_specs=[WHOLE],
        out_specs=[WHOLE] * (columns // 2),
        compiler_params=params(8),
        cost_estimate=pl.CostEstimate(flops=0, bytes_accessed=4 * columns * rows * cols, transcendentals=0),
        name="transposed",
    )(dense)


def forward_kernel(*refs, which, base, slots, has_prev):
    count = len(which)
    dense_ref, sources = refs[0], refs[1:1 + count]
    rest = refs[1 + count:]
    prev, outs = (rest[:slots], rest[slots:]) if has_prev else (None, rest)
    rows = outs[0].shape[0]
    for k, out_ref in reversed(list(enumerate(outs))):
        total = prev[k][...] if has_prev else None
        for j, source in zip(which, sources):
            part = bf16_dot(dense_ref[j, (base + k) * rows:(base + k + 1) * rows, :], source[...])
            total = part if total is None else total + part
        out_ref[...] = total.astype(out_ref.dtype)


def forward(dense, which, sources, base, prev, dtypes):
    slots = len(dtypes)
    depth, width = sources[0].shape
    rows = slots * depth
    return pl.pallas_call(
        functools.partial(
            forward_kernel, which=which, base=base, slots=slots, has_prev=prev is not None),
        out_shape=[like((depth, width), dtype) for dtype in dtypes],
        in_specs=[WHOLE] * (1 + len(sources) + (slots if prev is not None else 0)),
        out_specs=[WHOLE] * slots,
        compiler_params=params(8),
        cost_estimate=pl.CostEstimate(
            flops=2 * len(sources) * rows * depth * width,
            bytes_accessed=2 * len(sources) * rows * depth + 4 * rows * width, transcendentals=0),
        name="forward",
    )(dense, *sources, *(prev or []))


def middle_kernel(*refs):
    pieces, (cot_ref, weight_ref, act_ref, agg_ref, pre_grad_ref, grad_ref) = refs[:-6], refs[-6:]
    agg = pieces[0][...]
    for piece in pieces[1:]:
        agg = agg + piece[...].astype(jnp.float32)
    agg = agg.astype(jnp.bfloat16)
    agg_ref[...] = agg
    weight = weight_ref[...]
    preact = bf16_dot(agg, weight)
    sigma = jax.nn.sigmoid(preact)
    act_ref[...] = (preact * sigma).astype(act_ref.dtype)
    slope = sigma * (1.0 + preact * (1.0 - sigma))
    pre_grad = (cot_ref[...].astype(jnp.float32) * slope).astype(jnp.bfloat16)
    pre_grad_ref[...] = pre_grad
    grad_ref[...] = lax.dot_general(
        pre_grad, weight, (((1,), (1,)), ((), ())), preferred_element_type=jnp.float32
    ).astype(jnp.bfloat16)


def middle(pieces, cotangent, weight):
    rows, width = cotangent.shape
    return pl.pallas_call(
        middle_kernel,
        out_shape=[like((rows, width), jnp.bfloat16)] * 4,
        in_specs=[WHOLE] * (2 + len(pieces)),
        out_specs=[WHOLE] * 4,
        compiler_params=params(8),
        cost_estimate=pl.CostEstimate(
            flops=4 * rows * width * width, bytes_accessed=10 * rows * width, transcendentals=rows * width),
        name="middle",
    )(*pieces, cotangent, weight)


def weight_kernel(place_ref, agg_ref, pre_grad_ref, *refs, groups, side):
    outs, part_ref = refs[:-1], refs[-1]
    core, member = (place_ref[0] & 1) ^ side, place_ref[1]
    half = part_ref.shape[0]
    rows = half // groups
    part_ref[...] = lax.dot_general(
        agg_ref[:, pl.ds(pl.multiple_of(core * half, half), half)], pre_grad_ref[...], (((0,), (0,)), ((), ())),
        preferred_element_type=jnp.float32,
    )
    for k in range(groups):
        start = (member ^ between(k, 1 - core, bit_count(groups))) * rows
        piece = part_ref[pl.ds(pl.multiple_of(start, rows), rows), :]
        if side:
            outs[0][k * rows:(k + 1) * rows, :] = piece.astype(outs[0].dtype)
        else:
            outs[k][...] = piece


def weight_part(agg, pre_grad, place, groups, side):
    rows, width = agg.shape
    half = width // 2
    own = [like((half // groups, width), jnp.float32)] * groups
    return pl.pallas_call(
        functools.partial(weight_kernel, groups=groups, side=side),
        out_shape=[like((half, width), jnp.bfloat16)] if side else own,
        in_specs=[SCALARS, WHOLE, WHOLE],
        out_specs=[WHOLE] * (1 if side else groups),
        scratch_shapes=[pltpu.VMEM((half, width), jnp.float32)],
        compiler_params=params(8),
        cost_estimate=pl.CostEstimate(
            flops=2 * rows * half * width, bytes_accessed=4 * rows * width + 2 * width * width, transcendentals=0),
        name="weight_part",
    )(place, agg, pre_grad)


def place_kernel(place_ref, *refs, groups):
    owns, other_ref, out_ref = refs[:groups], refs[groups], refs[groups + 1]
    core, member = place_ref[0] & 1, place_ref[1]
    rows = owns[0].shape[0]
    bits = bit_count(groups)
    for k in range(groups):
        for side, value in ((core, owns[k][...]), (1 - core, other_ref[k * rows:(k + 1) * rows, :])):
            start = (side * groups + (member ^ between(k, 1 - side, bits))) * rows
            out_ref[pl.ds(pl.multiple_of(start, rows), rows), :] = value


def place_slices(owns, other, place):
    groups = len(owns)
    rows, width = owns[0].shape
    return pl.pallas_call(
        functools.partial(place_kernel, groups=groups),
        out_shape=like((2 * groups * rows, width), jnp.float32),
        in_specs=[SCALARS] + [WHOLE] * (groups + 1),
        out_specs=WHOLE,
        compiler_params=params(8),
        cost_estimate=pl.CostEstimate(flops=0, bytes_accessed=16 * groups * rows * width, transcendentals=0),
        name="place_slices",
    )(place, *owns, other)


def backward_kernel(*refs, side, count, slots):
    blocks, grads, outs = refs[:count], refs[count:count + slots], refs[count + slots:]
    rows = blocks[0].shape[1]
    for i, block in enumerate(blocks):
        total, start = None, 0
        for grad in grads:
            stop = start + grad.shape[0]
            part = bf16_dot(block[side, :, start:stop], grad[...])
            total, start = part if total is None else total + part, stop
        if side:
            outs[0][i * rows:(i + 1) * rows, :] = total.astype(outs[0].dtype)
        else:
            outs[i][...] = total


def backward(blocks, grads, side):
    _, cols, rows = blocks[0].shape
    width = grads[0].shape[1]
    count = len(blocks)
    own = [like((cols, width), jnp.float32)] * count
    return pl.pallas_call(
        functools.partial(backward_kernel, side=side, count=count, slots=len(grads)),
        out_shape=[like((count * cols, width), jnp.bfloat16)] if side else own,
        in_specs=[WHOLE] * (count + len(grads)),
        out_specs=[WHOLE] * (1 if side else count),
        compiler_params=params(8),
        cost_estimate=pl.CostEstimate(
            flops=2 * count * cols * rows * width,
            bytes_accessed=2 * count * cols * rows + 2 * rows * width + 4 * count * cols * width, transcendentals=0),
        name="backward",
    )(*blocks, *grads)


def settle_kernel(*refs, slots, count):
    totals, arrived, outs = refs[:slots], refs[slots:slots + count], refs[slots + count:]
    rows = totals[0].shape[0]
    for k in range(slots):
        total = totals[k][...]
        for ref in arrived:
            total = total + ref[k * rows:(k + 1) * rows, :].astype(jnp.float32)
        outs[k][...] = total.astype(outs[k].dtype)


def settle(totals, arrived, dtypes):
    rows, width = totals[0].shape
    return pl.pallas_call(
        functools.partial(settle_kernel, slots=len(totals), count=len(arrived)),
        out_shape=[like((rows, width), dtype) for dtype in dtypes],
        in_specs=[WHOLE] * (len(totals) + len(arrived)),
        out_specs=[WHOLE] * len(totals),
        compiler_params=params(8),
        cost_estimate=pl.CostEstimate(flops=rows * width, bytes_accessed=8 * rows * width, transcendentals=0),
        name="settle",
    )(*totals, *arrived)


def top_bit(slot):
    return 1 << (slot.bit_length() - 1)


def halve(totals, swap):
    while True:
        half = len(totals) // 2
        send = [total.astype(jnp.bfloat16) for total in totals[half:]]
        got = swap(jnp.concatenate(send) if half > 1 else send[0], half)
        if half == 1:
            return [totals[0], got]
        totals = add_slots(totals[:half], got)


def add_slots(totals, got):
    rows = totals[0].shape[0]
    return [total + got[k * rows:(k + 1) * rows].astype(jnp.float32) for k, total in enumerate(totals)]


def collect(totals, swap):
    totals = list(totals)
    arrived = []
    for k in reversed(range(1, len(totals))):
        got = swap(totals[k].astype(jnp.bfloat16), top_bit(k))
        if k == top_bit(k):
            arrived.append(got)
        else:
            totals[k - top_bit(k)] = totals[k - top_bit(k)].astype(jnp.float32) + got.astype(jnp.float32)
    return [totals[0], *arrived]


def local(features, cotangent, weight, tiles, tile_rows, tile_cols, tile_counts):
    blocks = lax.axis_size("dom")
    groups = lax.axis_size("repl")
    chips = blocks // 2
    rows_local, width = features.shape
    scale = float(rows_local * blocks * groups) ** (-0.5)
    position, member = lax.axis_index("dom"), lax.axis_index("repl")
    place = jnp.stack([position, member]).astype(jnp.int32)

    col_tiles = rows_local // tiles.shape[-1]
    row = tile_rows[0, 0]
    row = between((row // col_tiles) ^ member, position & 1, bit_count(groups)) * col_tiles + row % col_tiles
    spots = jnp.concatenate([row * col_tiles + tile_cols[0, 0], tile_counts[0, 0][:, None]], axis=1)
    dense = densify(tiles[0, 0], spots, place, groups, rows_local)

    held = [features]
    for k in range(1, chips):
        given = after(features, held[k - 1]) if k == top_bit(k) > 1 else held[k - top_bit(k)]
        held.append(swap_chips(given, top_bit(k)))
        if k == 1:
            held[1] = after(held[1], spots)
    half, upper = chips // 2, groups // 2
    sources = [x for own in held[:half] for x in (own, swap_cores(own))]
    totals = forward(dense, list(range(2 * half)), sources, 0, None, [jnp.float32] * groups)
    far = [after(own, *totals) for own in held[half:]]
    others = [swap_cores(own) for own in far]
    totals = forward(dense, list(range(2 * half, 2 * chips, 2)), far, 0, totals, [jnp.float32] * groups)
    odd = list(range(2 * half + 1, 2 * chips, 2))
    high = forward(dense, odd, others, upper, totals[upper:], [jnp.bfloat16] * upper)
    low = forward(after(dense, *high), odd, others, 0, totals[:upper], [jnp.float32] * upper)
    totals = low + high

    pieces = collect(totals, swap_members)
    dense_t = transposed(after(dense, *totals, pieces[1]))
    pieces[-1] = after(pieces[-1], *dense_t)
    activated, agg, pre_grad, grad = middle(pieces, cotangent, weight)
    (send,) = weight_part(agg, pre_grad, place, groups, 1)
    owns = weight_part(after(agg, send), pre_grad, place, groups, 0)
    parts = add_slots(owns, swap_cores(send))

    grads = [grad]
    for k in range(1, groups):
        grads.append(swap_members(grads[k - top_bit(k)], top_bit(k)))
    part = parts[0]
    for k in range(1, groups):
        part = part + swap_members(parts[k].astype(jnp.bfloat16), k, turn=1).astype(jnp.float32)
    part = part.astype(jnp.bfloat16)
    near = swap_chips(part, 1)
    part = part.astype(jnp.float32) + near.astype(jnp.float32)
    grads[-1] = after(grads[-1], near)

    half = chips // 2
    other = backward(dense_t[half:], grads, 1)
    own = backward([after(dense_t[half], *other), *dense_t[half + 1:]], grads, 0)
    high = jnp.concatenate(add_slots(own, swap_cores(other[0]))).astype(jnp.bfloat16)
    grads[0] = after(grads[0], high)
    other = backward(dense_t[:half], grads, 1)
    totals = backward(dense_t[:half], grads, 0)
    arrived = [swap_cores(other[0]), swap_chips(high, half)]
    while half > 1:
        half //= 2
        totals = settle(totals, arrived, [jnp.float32] * half + [jnp.bfloat16] * half)
        send = jnp.concatenate(totals[half:]) if half > 1 else totals[half]
        totals, arrived = totals[:half], [swap_chips(send, half)]
    (feature_grad,) = settle(totals, arrived, [jnp.bfloat16])

    bit = 2
    while bit < chips:
        part = part.astype(jnp.bfloat16)
        part = part.astype(jnp.float32) + swap_chips(part, bit).astype(jnp.float32)
        bit *= 2
    part = part * scale
    parts = [part] + [swap_members(part, k, turn=1) for k in range(1, groups)]
    weight_grad = place_slices(parts, swap_cores(jnp.concatenate(parts)), place)
    return (activated, feature_grad, weight_grad)


def solution(mesh):
    in_specs = (
        P(("dom", "repl"), None),
        P(("dom", "repl"), None),
        P(),
        P("dom", "repl", None, None, None, None),
        P("dom", "repl", None, None),
        P("dom", "repl", None, None),
        P("dom", "repl", None),
    )
    out_specs = (P(("dom", "repl"), None), P(("dom", "repl"), None), P())
    return jax.shard_map(local, mesh=mesh, in_specs=in_specs, out_specs=out_specs, check_vma=False)
```

```python
import functools

import jax
import jax.numpy as jnp
from jax import lax
from jax.experimental import pallas as pl
from jax.experimental.pallas import tpu as pltpu
from jax.sharding import PartitionSpec as P

WHOLE = pl.BlockSpec(memory_space=pltpu.VMEM)
SCALARS = pl.BlockSpec(memory_space=pltpu.SMEM)
CHUNKS = 2


def bit_count(n):
    return n.bit_length() - 1


def between(index, core, bits):
    reverse = 0
    for i in range(bits):
        reverse = reverse | (((index >> i) & 1) << (bits - 1 - i))
    return core * index + (1 - core) * reverse


def swap_cores(x):
    return lax.ppermute(x, "dom", [(i, i ^ 1) for i in range(lax.axis_size("dom"))])


def swap_chips(x, held):
    blocks = lax.axis_size("dom")
    bits = bit_count(blocks // 2)
    return lax.ppermute(x, "dom", [(i, i ^ (2 * between(held, i % 2, bits))) for i in range(blocks)])


def swap_members(x, held, turn=0):
    blocks, groups = lax.axis_size("dom"), lax.axis_size("repl")
    bits = bit_count(groups)
    pairs = []
    for i in range(blocks):
        for j in range(groups):
            pairs.append((i * groups + j, i * groups + (j ^ between(held, (i % 2) ^ turn, bits))))
    return lax.ppermute(x, ("dom", "repl"), pairs)


def after(x, *others):
    return lax.optimization_barrier((x, *others))[0]


def params(mib):
    return pltpu.CompilerParams(vmem_limit_bytes=mib * 1024 * 1024)


def like(shape, dtype):
    return jax.ShapeDtypeStruct(shape, dtype)


def bf16_dot(a, b):
    return jnp.dot(a, b, preferred_element_type=jnp.float32)


def column_of(position, j, blocks):
    core = (position & 1) ^ (j & 1)
    return (((position >> 1) ^ between(j >> 1, core, bit_count(blocks // 2))) << 1) | core


def densify_kernel(spots_ref, place_ref, tiles_ref, a_ref, acc_ref, *, col_tiles):
    column = column_of(place_ref[0], pl.program_id(0), pl.num_programs(0))
    size = tiles_ref.shape[-1]
    count = tiles_ref.shape[1]
    acc_ref[...] = jnp.zeros_like(acc_ref)

    def add(tile, carry):
        acc_ref[spots_ref[column, tile]] += tiles_ref[0, tile].astype(jnp.float32)
        return carry

    lax.fori_loop(0, spots_ref[column, count], add, 0)
    for spot in range(acc_ref.shape[0]):
        row, col = spot // col_tiles, spot % col_tiles
        a_ref[0, row * size:(row + 1) * size, col * size:(col + 1) * size] = acc_ref[spot].astype(a_ref.dtype)


def densify(tiles, spots, place, group_count, rows_local):
    columns, count, size, _ = tiles.shape
    col_tiles = rows_local // size
    rows = group_count * rows_local
    return pl.pallas_call(
        functools.partial(densify_kernel, col_tiles=col_tiles),
        out_shape=like((columns, rows, rows_local), jnp.bfloat16),
        grid_spec=pltpu.PrefetchScalarGridSpec(
            num_scalar_prefetch=2,
            grid=(columns,),
            in_specs=[pl.BlockSpec((1, count, size, size), lambda j, s, p: (column_of(p[0], j, columns), 0, 0, 0))],
            out_specs=pl.BlockSpec((1, rows, rows_local), lambda j, *_: (j, 0, 0)),
            scratch_shapes=[pltpu.VMEM((group_count * col_tiles * col_tiles, size, size), jnp.float32)],
        ),
        compiler_params=params(12),
        cost_estimate=pl.CostEstimate(
            flops=columns * count * size * size, bytes_accessed=8 * rows * columns * rows_local, transcendentals=0),
        name="densify",
    )(spots, place, tiles)


def transpose_kernel(a_ref, *outs):
    for i, out_ref in enumerate(outs):
        for side in range(2):
            out_ref[side] = a_ref[2 * i + side].T


def transposed(dense):
    columns, rows, cols = dense.shape
    return pl.pallas_call(
        transpose_kernel,
        out_shape=[like((2, cols, rows), jnp.bfloat16)] * (columns // 2),
        in_specs=[WHOLE],
        out_specs=[WHOLE] * (columns // 2),
        compiler_params=params(8),
        cost_estimate=pl.CostEstimate(flops=0, bytes_accessed=4 * columns * rows * cols, transcendentals=0),
        name="transposed",
    )(dense)


def forward_kernel(*refs, which, base, slots, has_prev):
    count = len(which)
    dense_ref, sources = refs[0], refs[1:1 + count]
    rest = refs[1 + count:]
    prev, outs = (rest[:slots], rest[slots:]) if has_prev else (None, rest)
    rows, width = outs[0].shape
    for k in reversed(range(slots)):
        total = prev[k][...] if has_prev else None
        for j, source in zip(which, sources):
            part = bf16_dot(dense_ref[j, (base + k) * rows:(base + k + 1) * rows, :], source[...])
            total = part if total is None else total + part
        for c, out_ref in enumerate(outs[k::slots]):
            out_ref[...] = total[:, c * width:(c + 1) * width].astype(out_ref.dtype)


def forward(dense, which, sources, base, prev, dtypes, chunks=1):
    slots = len(dtypes)
    depth, width = sources[0].shape
    rows = slots * depth
    out = pl.pallas_call(
        functools.partial(
            forward_kernel, which=which, base=base, slots=slots, has_prev=prev is not None),
        out_shape=[like((depth, width // chunks), dtype) for dtype in dtypes] * chunks,
        in_specs=[WHOLE] * (1 + len(sources) + (slots if prev is not None else 0)),
        out_specs=[WHOLE] * (slots * chunks),
        compiler_params=params(8),
        cost_estimate=pl.CostEstimate(
            flops=2 * len(sources) * rows * depth * width,
            bytes_accessed=2 * len(sources) * rows * depth + 4 * rows * width, transcendentals=0),
        name="forward",
    )(dense, *sources, *(prev or []))
    return out if chunks == 1 else [out[c * slots:(c + 1) * slots] for c in range(chunks)]


def middle_kernel(*refs, counts):
    pieces, (cot_ref, weight_ref, act_ref, agg_ref, pre_grad_ref, grad_ref) = refs[:-6], refs[-6:]
    start = 0
    width = pieces[0].shape[1]
    for c, count in enumerate(counts):
        agg = pieces[start][...]
        for piece in pieces[start + 1:start + count]:
            agg = agg + piece[...].astype(jnp.float32)
        agg_ref[:, c * width:(c + 1) * width] = agg.astype(jnp.bfloat16)
        start += count
    weight = weight_ref[...]
    preact = bf16_dot(agg_ref[...], weight)
    sigma = jax.nn.sigmoid(preact)
    act_ref[...] = (preact * sigma).astype(act_ref.dtype)
    slope = sigma * (1.0 + preact * (1.0 - sigma))
    pre_grad = (cot_ref[...].astype(jnp.float32) * slope).astype(jnp.bfloat16)
    pre_grad_ref[...] = pre_grad
    grad_ref[...] = lax.dot_general(
        pre_grad, weight, (((1,), (1,)), ((), ())), preferred_element_type=jnp.float32
    ).astype(jnp.bfloat16)


def middle(chunks, cotangent, weight):
    rows, width = cotangent.shape
    pieces = [piece for chunk in chunks for piece in chunk]
    return pl.pallas_call(
        functools.partial(middle_kernel, counts=[len(chunk) for chunk in chunks]),
        out_shape=[like((rows, width), jnp.bfloat16)] * 4,
        in_specs=[WHOLE] * (2 + len(pieces)),
        out_specs=[WHOLE] * 4,
        compiler_params=params(8),
        cost_estimate=pl.CostEstimate(
            flops=4 * rows * width * width, bytes_accessed=10 * rows * width, transcendentals=rows * width),
        name="middle",
    )(*pieces, cotangent, weight)


def weight_kernel(place_ref, agg_ref, pre_grad_ref, *refs, groups):
    owns, send_ref, part_ref = refs[:groups], refs[groups], refs[groups + 1]
    core, member = place_ref[0] & 1, place_ref[1]
    rows = owns[0].shape[0]
    bits = bit_count(groups)
    part_ref[...] = lax.dot_general(
        agg_ref[...], pre_grad_ref[...], (((0,), (0,)), ((), ())), preferred_element_type=jnp.float32
    )

    def piece(k, side):
        start = (2 * (member ^ between(k, 1 - side, bits)) + side) * rows
        return part_ref[pl.ds(pl.multiple_of(start, rows), rows), :]

    for k in range(groups):
        owns[k][...] = piece(k, core)
        send_ref[k * rows:(k + 1) * rows, :] = piece(k, 1 - core).astype(send_ref.dtype)


def weight_part(agg, pre_grad, place, groups):
    rows, width = agg.shape
    part = width // (2 * groups)
    out = pl.pallas_call(
        functools.partial(weight_kernel, groups=groups),
        out_shape=[like((part, width), jnp.float32)] * groups + [like((groups * part, width), jnp.bfloat16)],
        in_specs=[SCALARS, WHOLE, WHOLE],
        out_specs=[WHOLE] * (groups + 1),
        scratch_shapes=[pltpu.VMEM((width, width), jnp.float32)],
        compiler_params=params(8),
        cost_estimate=pl.CostEstimate(
            flops=2 * rows * width * width, bytes_accessed=4 * rows * width + 4 * width * width, transcendentals=0),
        name="weight_part",
    )(place, agg, pre_grad)
    return out[:-1], out[-1]


def place_kernel(place_ref, *refs, groups):
    owns, other_ref, out_ref = refs[:groups], refs[groups], refs[groups + 1]
    core, member = place_ref[0] & 1, place_ref[1]
    rows = owns[0].shape[0]
    bits = bit_count(groups)
    for k in range(groups):
        for side, value in ((core, owns[k][...]), (1 - core, other_ref[k * rows:(k + 1) * rows, :])):
            start = (2 * (member ^ between(k, 1 - side, bits)) + side) * rows
            out_ref[pl.ds(pl.multiple_of(start, rows), rows), :] = value


def place_slices(owns, other, place):
    groups = len(owns)
    rows, width = owns[0].shape
    return pl.pallas_call(
        functools.partial(place_kernel, groups=groups),
        out_shape=like((2 * groups * rows, width), jnp.float32),
        in_specs=[SCALARS] + [WHOLE] * (groups + 1),
        out_specs=WHOLE,
        compiler_params=params(8),
        cost_estimate=pl.CostEstimate(flops=0, bytes_accessed=16 * groups * rows * width, transcendentals=0),
        name="place_slices",
    )(place, *owns, other)


def backward_kernel(*refs, side, count, slots):
    blocks, grads, outs = refs[:count], refs[count:count + slots], refs[count + slots:]
    rows = blocks[0].shape[1]
    for i, block in enumerate(blocks):
        total, start = None, 0
        for grad in grads:
            stop = start + grad.shape[0]
            part = bf16_dot(block[side, :, start:stop], grad[...])
            total, start = part if total is None else total + part, stop
        if side:
            outs[0][i * rows:(i + 1) * rows, :] = total.astype(outs[0].dtype)
        else:
            outs[i][...] = total


def backward(blocks, grads, side):
    _, cols, rows = blocks[0].shape
    width = grads[0].shape[1]
    count = len(blocks)
    own = [like((cols, width), jnp.float32)] * count
    return pl.pallas_call(
        functools.partial(backward_kernel, side=side, count=count, slots=len(grads)),
        out_shape=[like((count * cols, width), jnp.bfloat16)] if side else own,
        in_specs=[WHOLE] * (count + len(grads)),
        out_specs=[WHOLE] * (1 if side else count),
        compiler_params=params(8),
        cost_estimate=pl.CostEstimate(
            flops=2 * count * cols * rows * width,
            bytes_accessed=2 * count * cols * rows + 2 * rows * width + 4 * count * cols * width, transcendentals=0),
        name="backward",
    )(*blocks, *grads)


def settle_kernel(*refs, slots, count):
    totals, arrived, outs = refs[:slots], refs[slots:slots + count], refs[slots + count:]
    rows = totals[0].shape[0]
    for k in range(slots):
        total = totals[k][...]
        for ref in arrived:
            total = total + ref[k * rows:(k + 1) * rows, :].astype(jnp.float32)
        outs[k][...] = total.astype(outs[k].dtype)


def settle(totals, arrived, dtypes):
    rows, width = totals[0].shape
    return pl.pallas_call(
        functools.partial(settle_kernel, slots=len(totals), count=len(arrived)),
        out_shape=[like((rows, width), dtype) for dtype in dtypes],
        in_specs=[WHOLE] * (len(totals) + len(arrived)),
        out_specs=[WHOLE] * len(totals),
        compiler_params=params(8),
        cost_estimate=pl.CostEstimate(flops=rows * width, bytes_accessed=8 * rows * width, transcendentals=0),
        name="settle",
    )(*totals, *arrived)


def top_bit(slot):
    return 1 << (slot.bit_length() - 1)


def halve(totals, swap):
    while True:
        half = len(totals) // 2
        send = [total.astype(jnp.bfloat16) for total in totals[half:]]
        got = swap(jnp.concatenate(send) if half > 1 else send[0], half)
        if half == 1:
            return [totals[0], got]
        totals = add_slots(totals[:half], got)


def add_slots(totals, got):
    rows = totals[0].shape[0]
    return [total + got[k * rows:(k + 1) * rows].astype(jnp.float32) for k, total in enumerate(totals)]


def add_kernel(total_ref, got_ref, out_ref):
    out_ref[...] = (total_ref[...].astype(jnp.float32) + got_ref[...].astype(jnp.float32)).astype(out_ref.dtype)


def add_rounded(total, got):
    return pl.pallas_call(
        add_kernel,
        out_shape=like(total.shape, jnp.bfloat16),
        in_specs=[WHOLE] * 2,
        out_specs=WHOLE,
        compiler_params=params(4),
        cost_estimate=pl.CostEstimate(flops=total.size, bytes_accessed=8 * total.size, transcendentals=0),
        name="add_rounded",
    )(total, got)


def collect(totals, swap):
    totals = list(totals)
    arrived = []
    for k in reversed(range(1, len(totals))):
        got = swap(totals[k].astype(jnp.bfloat16), top_bit(k))
        if k == top_bit(k):
            arrived.append(got)
        else:
            totals[k - top_bit(k)] = add_rounded(totals[k - top_bit(k)], got)
    return [totals[0], *arrived]


def local(features, cotangent, weight, tiles, tile_rows, tile_cols, tile_counts):
    blocks = lax.axis_size("dom")
    groups = lax.axis_size("repl")
    chips = blocks // 2
    rows_local, width = features.shape
    scale = float(rows_local * blocks * groups) ** (-0.5)
    position, member = lax.axis_index("dom"), lax.axis_index("repl")
    place = jnp.stack([position, member]).astype(jnp.int32)

    col_tiles = rows_local // tiles.shape[-1]
    row = tile_rows[0, 0]
    row = between((row // col_tiles) ^ member, position & 1, bit_count(groups)) * col_tiles + row % col_tiles
    spots = jnp.concatenate([row * col_tiles + tile_cols[0, 0], tile_counts[0, 0][:, None]], axis=1)
    dense = densify(tiles[0, 0], spots, place, groups, rows_local)

    held = [features]
    for k in range(1, chips):
        given = after(features, held[k - 1]) if k == top_bit(k) > 1 else held[k - top_bit(k)]
        held.append(swap_chips(given, top_bit(k)))
        if k == 1:
            held[1] = after(held[1], spots)
    half, upper = chips // 2, groups // 2
    sources = [x for own in held[:half] for x in (own, swap_cores(own))]
    totals = forward(dense, list(range(2 * half)), sources, 0, None, [jnp.float32] * groups)
    far = [after(own, *totals) for own in held[half:]]
    others = [swap_cores(own) for own in far]
    totals = forward(dense, list(range(2 * half, 2 * chips, 2)), far, 0, totals, [jnp.float32] * groups)
    odd = list(range(2 * half + 1, 2 * chips, 2))
    high = forward(dense, odd, others, upper, totals[upper:], [jnp.bfloat16] * upper, CHUNKS)
    low = forward(after(dense, *high[0]), odd, others, 0, totals[:upper], [jnp.float32] * upper, CHUNKS)

    pieces = [collect([*x, *y], swap_members) for x, y in zip(low, high)]
    dense_t = transposed(after(dense, *high[0], *[piece[1] for piece in pieces]))
    pieces[-1][-1] = after(pieces[-1][-1], *dense_t)
    activated, agg, pre_grad, grad = middle(pieces, cotangent, weight)
    owns, send = weight_part(agg, pre_grad, place, groups)
    parts = add_slots(owns, swap_cores(send))

    grads = [grad]
    for k in range(1, groups):
        grads.append(swap_members(grads[k - top_bit(k)], top_bit(k)))
    part = parts[0]
    for k in range(1, groups):
        part = part + swap_members(parts[k].astype(jnp.bfloat16), k, turn=1).astype(jnp.float32)
    part = part.astype(jnp.bfloat16)
    near = swap_chips(part, 1)
    part = part.astype(jnp.float32) + near.astype(jnp.float32)
    grads[-1] = after(grads[-1], near)

    half = chips // 2
    other = backward(dense_t[half:], grads, 1)
    own = backward([after(dense_t[half], *other), *dense_t[half + 1:]], grads, 0)
    high = jnp.concatenate(add_slots(own, swap_cores(other[0]))).astype(jnp.bfloat16)
    grads[0] = after(grads[0], high)
    other = backward(dense_t[:half], grads, 1)
    totals = backward(dense_t[:half], grads, 0)
    arrived = [swap_cores(other[0]), swap_chips(high, half)]
    while half > 1:
        half //= 2
        totals = settle(totals, arrived, [jnp.float32] * half + [jnp.bfloat16] * half)
        send = jnp.concatenate(totals[half:]) if half > 1 else totals[half]
        totals, arrived = totals[:half], [swap_chips(send, half)]
    (feature_grad,) = settle(totals, arrived, [jnp.bfloat16])

    bit = 2
    while bit < chips:
        part = part.astype(jnp.bfloat16)
        part = part.astype(jnp.float32) + swap_chips(part, bit).astype(jnp.float32)
        bit *= 2
    part = part * scale
    parts = [part] + [swap_members(part, k, turn=1) for k in range(1, groups)]
    weight_grad = place_slices(parts, swap_cores(jnp.concatenate(parts)), place)
    return (activated, feature_grad, weight_grad)


def solution(mesh):
    in_specs = (
        P(("dom", "repl"), None),
        P(("dom", "repl"), None),
        P(),
        P("dom", "repl", None, None, None, None),
        P("dom", "repl", None, None),
        P("dom", "repl", None, None),
        P("dom", "repl", None),
    )
    out_specs = (P(("dom", "repl"), None), P(("dom", "repl"), None), P())
    return jax.shard_map(local, mesh=mesh, in_specs=in_specs, out_specs=out_specs, check_vma=False)
```

```python
import functools

import jax
import jax.numpy as jnp
from jax import lax
from jax.experimental import pallas as pl
from jax.experimental.pallas import tpu as pltpu
from jax.sharding import PartitionSpec as P

WHOLE = pl.BlockSpec(memory_space=pltpu.VMEM)
SCALARS = pl.BlockSpec(memory_space=pltpu.SMEM)
CHUNKS = 2


def bit_count(n):
    return n.bit_length() - 1


def between(index, core, bits):
    reverse = 0
    for i in range(bits):
        reverse = reverse | (((index >> i) & 1) << (bits - 1 - i))
    return core * index + (1 - core) * reverse


def swap_cores(x):
    return lax.ppermute(x, "dom", [(i, i ^ 1) for i in range(lax.axis_size("dom"))])


def swap_chips(x, held):
    blocks = lax.axis_size("dom")
    bits = bit_count(blocks // 2)
    return lax.ppermute(x, "dom", [(i, i ^ (2 * between(held, i % 2, bits))) for i in range(blocks)])


def swap_members(x, held, turn=0):
    blocks, groups = lax.axis_size("dom"), lax.axis_size("repl")
    bits = bit_count(groups)
    pairs = []
    for i in range(blocks):
        for j in range(groups):
            pairs.append((i * groups + j, i * groups + (j ^ between(held, (i % 2) ^ turn, bits))))
    return lax.ppermute(x, ("dom", "repl"), pairs)


def after(x, *others):
    return lax.optimization_barrier((x, *others))[0]


def params(mib):
    return pltpu.CompilerParams(vmem_limit_bytes=mib * 1024 * 1024)


def like(shape, dtype):
    return jax.ShapeDtypeStruct(shape, dtype)


def bf16_dot(a, b):
    return jnp.dot(a, b, preferred_element_type=jnp.float32)


def column_of(position, j, blocks):
    core = (position & 1) ^ (j & 1)
    return (((position >> 1) ^ between(j >> 1, core, bit_count(blocks // 2))) << 1) | core


def densify_kernel(spots_ref, place_ref, tiles_ref, a_ref, acc_ref, *, col_tiles):
    column = column_of(place_ref[0], pl.program_id(0), pl.num_programs(0))
    size = tiles_ref.shape[-1]
    count = tiles_ref.shape[1]
    acc_ref[...] = jnp.zeros_like(acc_ref)

    def add(tile, carry):
        acc_ref[spots_ref[column, tile]] += tiles_ref[0, tile].astype(jnp.float32)
        return carry

    lax.fori_loop(0, spots_ref[column, count], add, 0)
    for spot in range(acc_ref.shape[0]):
        row, col = spot // col_tiles, spot % col_tiles
        a_ref[0, row * size:(row + 1) * size, col * size:(col + 1) * size] = acc_ref[spot].astype(a_ref.dtype)


def densify(tiles, spots, place, group_count, rows_local):
    columns, count, size, _ = tiles.shape
    col_tiles = rows_local // size
    rows = group_count * rows_local
    return pl.pallas_call(
        functools.partial(densify_kernel, col_tiles=col_tiles),
        out_shape=like((columns, rows, rows_local), jnp.bfloat16),
        grid_spec=pltpu.PrefetchScalarGridSpec(
            num_scalar_prefetch=2,
            grid=(columns,),
            in_specs=[pl.BlockSpec((1, count, size, size), lambda j, s, p: (column_of(p[0], j, columns), 0, 0, 0))],
            out_specs=pl.BlockSpec((1, rows, rows_local), lambda j, *_: (j, 0, 0)),
            scratch_shapes=[pltpu.VMEM((group_count * col_tiles * col_tiles, size, size), jnp.float32)],
        ),
        compiler_params=params(12),
        cost_estimate=pl.CostEstimate(
            flops=columns * count * size * size, bytes_accessed=8 * rows * columns * rows_local, transcendentals=0),
        name="densify",
    )(spots, place, tiles)


def transpose_kernel(a_ref, *outs):
    for i, out_ref in enumerate(outs):
        for side in range(2):
            out_ref[side] = a_ref[2 * i + side].T


def transposed(dense):
    columns, rows, cols = dense.shape
    return pl.pallas_call(
        transpose_kernel,
        out_shape=[like((2, cols, rows), jnp.bfloat16)] * (columns // 2),
        in_specs=[WHOLE],
        out_specs=[WHOLE] * (columns // 2),
        compiler_params=params(8),
        cost_estimate=pl.CostEstimate(flops=0, bytes_accessed=4 * columns * rows * cols, transcendentals=0),
        name="transposed",
    )(dense)


def forward_kernel(*refs, which, base, slots, has_prev):
    count = len(which)
    dense_ref, sources = refs[0], refs[1:1 + count]
    rest = refs[1 + count:]
    prev, outs = (rest[:slots], rest[slots:]) if has_prev else (None, rest)
    rows, width = outs[0].shape
    for k in reversed(range(slots)):
        total = prev[k][...] if has_prev else None
        for j, source in zip(which, sources):
            part = bf16_dot(dense_ref[j, (base + k) * rows:(base + k + 1) * rows, :], source[...])
            total = part if total is None else total + part
        for c, out_ref in enumerate(outs[k::slots]):
            out_ref[...] = total[:, c * width:(c + 1) * width].astype(out_ref.dtype)


def forward(dense, which, sources, base, prev, dtypes, chunks=1):
    slots = len(dtypes)
    depth, width = sources[0].shape
    rows = slots * depth
    out = pl.pallas_call(
        functools.partial(
            forward_kernel, which=which, base=base, slots=slots, has_prev=prev is not None),
        out_shape=[like((depth, width // chunks), dtype) for dtype in dtypes] * chunks,
        in_specs=[WHOLE] * (1 + len(sources) + (slots if prev is not None else 0)),
        out_specs=[WHOLE] * (slots * chunks),
        compiler_params=params(8),
        cost_estimate=pl.CostEstimate(
            flops=2 * len(sources) * rows * depth * width,
            bytes_accessed=2 * len(sources) * rows * depth + 4 * rows * width, transcendentals=0),
        name="forward",
    )(dense, *sources, *(prev or []))
    return out if chunks == 1 else [out[c * slots:(c + 1) * slots] for c in range(chunks)]


def middle_kernel(*refs, counts):
    pieces, (cot_ref, weight_ref, act_ref, agg_ref, pre_grad_ref, grad_ref) = refs[:-6], refs[-6:]
    start = 0
    width = pieces[0].shape[1]
    for c, count in enumerate(counts):
        agg = pieces[start][...]
        for piece in pieces[start + 1:start + count]:
            agg = agg + piece[...].astype(jnp.float32)
        agg_ref[:, c * width:(c + 1) * width] = agg.astype(jnp.bfloat16)
        start += count
    weight = weight_ref[...]
    preact = bf16_dot(agg_ref[...], weight)
    sigma = jax.nn.sigmoid(preact)
    act_ref[...] = (preact * sigma).astype(act_ref.dtype)
    slope = sigma * (1.0 + preact * (1.0 - sigma))
    pre_grad = (cot_ref[...].astype(jnp.float32) * slope).astype(jnp.bfloat16)
    pre_grad_ref[...] = pre_grad
    grad_ref[...] = lax.dot_general(
        pre_grad, weight, (((1,), (1,)), ((), ())), preferred_element_type=jnp.float32
    ).astype(jnp.bfloat16)


def middle(chunks, cotangent, weight):
    rows, width = cotangent.shape
    pieces = [piece for chunk in chunks for piece in chunk]
    return pl.pallas_call(
        functools.partial(middle_kernel, counts=[len(chunk) for chunk in chunks]),
        out_shape=[like((rows, width), jnp.bfloat16)] * 4,
        in_specs=[WHOLE] * (2 + len(pieces)),
        out_specs=[WHOLE] * 4,
        compiler_params=params(8),
        cost_estimate=pl.CostEstimate(
            flops=4 * rows * width * width, bytes_accessed=10 * rows * width, transcendentals=rows * width),
        name="middle",
    )(*pieces, cotangent, weight)


def weight_kernel(place_ref, agg_ref, pre_grad_ref, *refs, groups):
    owns, send_ref, part_ref = refs[:groups], refs[groups], refs[groups + 1]
    core, member = place_ref[0] & 1, place_ref[1]
    rows = owns[0].shape[0]
    bits = bit_count(groups)
    part_ref[...] = lax.dot_general(
        agg_ref[...], pre_grad_ref[...], (((0,), (0,)), ((), ())), preferred_element_type=jnp.float32
    )

    def piece(k, side):
        start = (2 * (member ^ between(k, 1 - side, bits)) + side) * rows
        return part_ref[pl.ds(pl.multiple_of(start, rows), rows), :]

    for k in range(groups):
        owns[k][...] = piece(k, core)
        send_ref[k * rows:(k + 1) * rows, :] = piece(k, 1 - core).astype(send_ref.dtype)


def weight_part(agg, pre_grad, place, groups):
    rows, width = agg.shape
    part = width // (2 * groups)
    out = pl.pallas_call(
        functools.partial(weight_kernel, groups=groups),
        out_shape=[like((part, width), jnp.float32)] * groups + [like((groups * part, width), jnp.bfloat16)],
        in_specs=[SCALARS, WHOLE, WHOLE],
        out_specs=[WHOLE] * (groups + 1),
        scratch_shapes=[pltpu.VMEM((width, width), jnp.float32)],
        compiler_params=params(8),
        cost_estimate=pl.CostEstimate(
            flops=2 * rows * width * width, bytes_accessed=4 * rows * width + 4 * width * width, transcendentals=0),
        name="weight_part",
    )(place, agg, pre_grad)
    return out[:-1], out[-1]


def place_kernel(place_ref, *refs, groups):
    owns, other_ref, out_ref = refs[:groups], refs[groups], refs[groups + 1]
    core, member = place_ref[0] & 1, place_ref[1]
    rows = owns[0].shape[0]
    bits = bit_count(groups)
    for k in range(groups):
        for side, value in ((core, owns[k][...]), (1 - core, other_ref[k * rows:(k + 1) * rows, :])):
            start = (2 * (member ^ between(k, 1 - side, bits)) + side) * rows
            out_ref[pl.ds(pl.multiple_of(start, rows), rows), :] = value


def place_slices(owns, other, place):
    groups = len(owns)
    rows, width = owns[0].shape
    return pl.pallas_call(
        functools.partial(place_kernel, groups=groups),
        out_shape=like((2 * groups * rows, width), jnp.float32),
        in_specs=[SCALARS] + [WHOLE] * (groups + 1),
        out_specs=WHOLE,
        compiler_params=params(8),
        cost_estimate=pl.CostEstimate(flops=0, bytes_accessed=16 * groups * rows * width, transcendentals=0),
        name="place_slices",
    )(place, *owns, other)


def backward_kernel(*refs, side, count, slots):
    blocks, grads, outs = refs[:count], refs[count:count + slots], refs[count + slots:]
    rows = blocks[0].shape[1]
    for i, block in enumerate(blocks):
        total, start = None, 0
        for grad in grads:
            stop = start + grad.shape[0]
            part = bf16_dot(block[side, :, start:stop], grad[...])
            total, start = part if total is None else total + part, stop
        if side:
            outs[0][i * rows:(i + 1) * rows, :] = total.astype(outs[0].dtype)
        else:
            outs[i][...] = total


def backward(blocks, grads, side):
    _, cols, rows = blocks[0].shape
    width = grads[0].shape[1]
    count = len(blocks)
    own = [like((cols, width), jnp.float32)] * count
    return pl.pallas_call(
        functools.partial(backward_kernel, side=side, count=count, slots=len(grads)),
        out_shape=[like((count * cols, width), jnp.bfloat16)] if side else own,
        in_specs=[WHOLE] * (count + len(grads)),
        out_specs=[WHOLE] * (1 if side else count),
        compiler_params=params(8),
        cost_estimate=pl.CostEstimate(
            flops=2 * count * cols * rows * width,
            bytes_accessed=2 * count * cols * rows + 2 * rows * width + 4 * count * cols * width, transcendentals=0),
        name="backward",
    )(*blocks, *grads)


def settle_kernel(*refs, slots, count):
    totals, arrived, outs = refs[:slots], refs[slots:slots + count], refs[slots + count:]
    rows = totals[0].shape[0]
    for k in range(slots):
        total = totals[k][...]
        for ref in arrived:
            total = total + ref[k * rows:(k + 1) * rows, :].astype(jnp.float32)
        outs[k][...] = total.astype(outs[k].dtype)


def settle(totals, arrived, dtypes):
    rows, width = totals[0].shape
    return pl.pallas_call(
        functools.partial(settle_kernel, slots=len(totals), count=len(arrived)),
        out_shape=[like((rows, width), dtype) for dtype in dtypes],
        in_specs=[WHOLE] * (len(totals) + len(arrived)),
        out_specs=[WHOLE] * len(totals),
        compiler_params=params(8),
        cost_estimate=pl.CostEstimate(flops=rows * width, bytes_accessed=8 * rows * width, transcendentals=0),
        name="settle",
    )(*totals, *arrived)


def top_bit(slot):
    return 1 << (slot.bit_length() - 1)


def halve(totals, swap):
    while True:
        half = len(totals) // 2
        send = [total.astype(jnp.bfloat16) for total in totals[half:]]
        got = swap(jnp.concatenate(send) if half > 1 else send[0], half)
        if half == 1:
            return [totals[0], got]
        totals = add_slots(totals[:half], got)


def add_slots(totals, got):
    rows = totals[0].shape[0]
    return [total + got[k * rows:(k + 1) * rows].astype(jnp.float32) for k, total in enumerate(totals)]


def add_kernel(total_ref, got_ref, out_ref):
    out_ref[...] = (total_ref[...].astype(jnp.float32) + got_ref[...].astype(jnp.float32)).astype(out_ref.dtype)


def add_rounded(total, got):
    return pl.pallas_call(
        add_kernel,
        out_shape=like(total.shape, jnp.bfloat16),
        in_specs=[WHOLE] * 2,
        out_specs=WHOLE,
        compiler_params=params(4),
        cost_estimate=pl.CostEstimate(flops=total.size, bytes_accessed=8 * total.size, transcendentals=0),
        name="add_rounded",
    )(total, got)


def collect(totals, swap):
    totals = list(totals)
    arrived = []
    for k in reversed(range(1, len(totals))):
        got = swap(totals[k].astype(jnp.bfloat16), top_bit(k))
        if k == top_bit(k):
            arrived.append(got)
        else:
            totals[k - top_bit(k)] = add_rounded(totals[k - top_bit(k)], got)
    return [totals[0], *arrived]


def local(features, cotangent, weight, tiles, tile_rows, tile_cols, tile_counts):
    blocks = lax.axis_size("dom")
    groups = lax.axis_size("repl")
    chips = blocks // 2
    rows_local, width = features.shape
    scale = float(rows_local * blocks * groups) ** (-0.5)
    position, member = lax.axis_index("dom"), lax.axis_index("repl")
    place = jnp.stack([position, member]).astype(jnp.int32)

    col_tiles = rows_local // tiles.shape[-1]
    row = tile_rows[0, 0]
    row = between((row // col_tiles) ^ member, position & 1, bit_count(groups)) * col_tiles + row % col_tiles
    spots = jnp.concatenate([row * col_tiles + tile_cols[0, 0], tile_counts[0, 0][:, None]], axis=1)
    dense = densify(tiles[0, 0], spots, place, groups, rows_local)

    held = [features]
    for k in range(1, chips):
        given = after(features, held[k - 1]) if k == top_bit(k) > 1 else held[k - top_bit(k)]
        held.append(swap_chips(given, top_bit(k)))
        if k == 1:
            held[1] = after(held[1], spots)
    half, upper = chips // 2, groups // 2
    sources = [x for own in held[:half] for x in (own, swap_cores(own))]
    totals = forward(dense, list(range(2 * half)), sources, 0, None, [jnp.float32] * groups)
    far = [after(own, *totals) for own in held[half:]]
    others = [swap_cores(own) for own in far]
    totals = forward(dense, list(range(2 * half, 2 * chips, 2)), far, 0, totals, [jnp.float32] * groups)
    odd = list(range(2 * half + 1, 2 * chips, 2))
    high = forward(dense, odd, others, upper, totals[upper:], [jnp.bfloat16] * upper, CHUNKS)
    low = forward(after(dense, *high[0]), odd, others, 0, totals[:upper], [jnp.float32] * upper, CHUNKS)

    pieces = [collect([*x, *y], swap_members) for x, y in zip(low, high)]
    dense_t = transposed(after(dense, *high[0], pieces[0][1]))
    pieces[-1][-1] = after(pieces[-1][-1], *dense_t)
    activated, agg, pre_grad, grad = middle(pieces, cotangent, weight)
    owns, send = weight_part(agg, pre_grad, place, groups)
    parts = add_slots(owns, swap_cores(send))

    grads = [grad]
    for k in range(1, groups):
        grads.append(swap_members(grads[k - top_bit(k)], top_bit(k)))
    part = parts[0]
    for k in range(1, groups):
        part = part + swap_members(parts[k].astype(jnp.bfloat16), k, turn=1).astype(jnp.float32)
    part = part.astype(jnp.bfloat16)
    near = swap_chips(part, 1)
    part = part.astype(jnp.float32) + near.astype(jnp.float32)
    grads[-1] = after(grads[-1], near)

    half = chips // 2
    other = backward(dense_t[half:], grads, 1)
    own = backward([after(dense_t[half], *other), *dense_t[half + 1:]], grads, 0)
    high = jnp.concatenate(add_slots(own, swap_cores(other[0]))).astype(jnp.bfloat16)
    grads[0] = after(grads[0], high)
    other = backward(dense_t[:half], grads, 1)
    totals = backward(dense_t[:half], grads, 0)
    arrived = [swap_cores(other[0]), swap_chips(high, half)]
    while half > 1:
        half //= 2
        totals = settle(totals, arrived, [jnp.float32] * half + [jnp.bfloat16] * half)
        send = jnp.concatenate(totals[half:]) if half > 1 else totals[half]
        totals, arrived = totals[:half], [swap_chips(send, half)]
    (feature_grad,) = settle(totals, arrived, [jnp.bfloat16])

    bit = 2
    while bit < chips:
        part = part.astype(jnp.bfloat16)
        part = part.astype(jnp.float32) + swap_chips(part, bit).astype(jnp.float32)
        bit *= 2
    part = part * scale
    parts = [part] + [swap_members(part, k, turn=1) for k in range(1, groups)]
    weight_grad = place_slices(parts, swap_cores(jnp.concatenate(parts)), place)
    return (activated, feature_grad, weight_grad)


def solution(mesh):
    in_specs = (
        P(("dom", "repl"), None),
        P(("dom", "repl"), None),
        P(),
        P("dom", "repl", None, None, None, None),
        P("dom", "repl", None, None),
        P("dom", "repl", None, None),
        P("dom", "repl", None),
    )
    out_specs = (P(("dom", "repl"), None), P(("dom", "repl"), None), P())
    return jax.shard_map(local, mesh=mesh, in_specs=in_specs, out_specs=out_specs, check_vma=False)
```

```python
import functools

import jax
import jax.numpy as jnp
from jax import lax
from jax.experimental import pallas as pl
from jax.experimental.pallas import tpu as pltpu
from jax.sharding import PartitionSpec as P

WHOLE = pl.BlockSpec(memory_space=pltpu.VMEM)
SCALARS = pl.BlockSpec(memory_space=pltpu.SMEM)


def bit_count(n):
    return n.bit_length() - 1


def between(index, core, bits):
    reverse = 0
    for i in range(bits):
        reverse = reverse | (((index >> i) & 1) << (bits - 1 - i))
    return core * index + (1 - core) * reverse


def swap_cores(x):
    return lax.ppermute(x, "dom", [(i, i ^ 1) for i in range(lax.axis_size("dom"))])


def swap_chips(x, held):
    blocks = lax.axis_size("dom")
    bits = bit_count(blocks // 2)
    return lax.ppermute(x, "dom", [(i, i ^ (2 * between(held, i % 2, bits))) for i in range(blocks)])


def swap_members(x, held, turn=0):
    blocks, groups = lax.axis_size("dom"), lax.axis_size("repl")
    bits = bit_count(groups)
    pairs = []
    for i in range(blocks):
        for j in range(groups):
            pairs.append((i * groups + j, i * groups + (j ^ between(held, (i % 2) ^ turn, bits))))
    return lax.ppermute(x, ("dom", "repl"), pairs)


def after(x, *others):
    return lax.optimization_barrier((x, *others))[0]


def params(mib):
    return pltpu.CompilerParams(vmem_limit_bytes=mib * 1024 * 1024)


def like(shape, dtype):
    return jax.ShapeDtypeStruct(shape, dtype)


def bf16_dot(a, b):
    return jnp.dot(a, b, preferred_element_type=jnp.float32)


def column_of(position, j, blocks):
    core = (position & 1) ^ (j & 1)
    return (((position >> 1) ^ between(j >> 1, core, bit_count(blocks // 2))) << 1) | core


def densify_kernel(spots_ref, place_ref, tiles_ref, a_ref, acc_ref, *, col_tiles):
    column = column_of(place_ref[0], pl.program_id(0), pl.num_programs(0))
    size = tiles_ref.shape[-1]
    count = tiles_ref.shape[1]
    acc_ref[...] = jnp.zeros_like(acc_ref)

    def add(tile, carry):
        acc_ref[spots_ref[column, tile]] += tiles_ref[0, tile].astype(jnp.float32)
        return carry

    lax.fori_loop(0, spots_ref[column, count], add, 0)
    for spot in range(acc_ref.shape[0]):
        row, col = spot // col_tiles, spot % col_tiles
        a_ref[0, row * size:(row + 1) * size, col * size:(col + 1) * size] = acc_ref[spot].astype(a_ref.dtype)


def densify(tiles, spots, place, group_count, rows_local):
    columns, count, size, _ = tiles.shape
    col_tiles = rows_local // size
    rows = group_count * rows_local
    return pl.pallas_call(
        functools.partial(densify_kernel, col_tiles=col_tiles),
        out_shape=like((columns, rows, rows_local), jnp.bfloat16),
        grid_spec=pltpu.PrefetchScalarGridSpec(
            num_scalar_prefetch=2,
            grid=(columns,),
            in_specs=[pl.BlockSpec((1, count, size, size), lambda j, s, p: (column_of(p[0], j, columns), 0, 0, 0))],
            out_specs=pl.BlockSpec((1, rows, rows_local), lambda j, *_: (j, 0, 0)),
            scratch_shapes=[pltpu.VMEM((group_count * col_tiles * col_tiles, size, size), jnp.float32)],
        ),
        compiler_params=params(12),
        cost_estimate=pl.CostEstimate(
            flops=columns * count * size * size, bytes_accessed=8 * rows * columns * rows_local, transcendentals=0),
        name="densify",
    )(spots, place, tiles)


def transpose_kernel(a_ref, *outs):
    for i, out_ref in enumerate(outs):
        for side in range(2):
            out_ref[side] = a_ref[2 * i + side].T


def transposed(dense):
    columns, rows, cols = dense.shape
    return pl.pallas_call(
        transpose_kernel,
        out_shape=[like((2, cols, rows), jnp.bfloat16)] * (columns // 2),
        in_specs=[WHOLE],
        out_specs=[WHOLE] * (columns // 2),
        compiler_params=params(8),
        cost_estimate=pl.CostEstimate(flops=0, bytes_accessed=4 * columns * rows * cols, transcendentals=0),
        name="transposed",
    )(dense)


def forward_kernel(*refs, which, base, slots, has_prev):
    count = len(which)
    dense_ref, sources = refs[0], refs[1:1 + count]
    rest = refs[1 + count:]
    prev, outs = (rest[:slots], rest[slots:]) if has_prev else (None, rest)
    rows = outs[0].shape[0]
    for k, out_ref in reversed(list(enumerate(outs))):
        total = prev[k][...] if has_prev else None
        for j, source in zip(which, sources):
            part = bf16_dot(dense_ref[j, (base + k) * rows:(base + k + 1) * rows, :], source[...])
            total = part if total is None else total + part
        out_ref[...] = total.astype(out_ref.dtype)


def forward(dense, which, sources, base, prev, dtypes):
    slots = len(dtypes)
    depth, width = sources[0].shape
    rows = slots * depth
    return pl.pallas_call(
        functools.partial(
            forward_kernel, which=which, base=base, slots=slots, has_prev=prev is not None),
        out_shape=[like((depth, width), dtype) for dtype in dtypes],
        in_specs=[WHOLE] * (1 + len(sources) + (slots if prev is not None else 0)),
        out_specs=[WHOLE] * slots,
        compiler_params=params(8),
        cost_estimate=pl.CostEstimate(
            flops=2 * len(sources) * rows * depth * width,
            bytes_accessed=2 * len(sources) * rows * depth + 4 * rows * width, transcendentals=0),
        name="forward",
    )(dense, *sources, *(prev or []))


def middle_kernel(*refs):
    pieces, (cot_ref, weight_ref, act_ref, agg_ref, pre_grad_ref, grad_ref) = refs[:-6], refs[-6:]
    agg = pieces[0][...]
    for piece in pieces[1:]:
        agg = agg + piece[...].astype(jnp.float32)
    agg = agg.astype(jnp.bfloat16)
    agg_ref[...] = agg
    weight = weight_ref[...]
    preact = bf16_dot(agg, weight)
    sigma = jax.nn.sigmoid(preact)
    act_ref[...] = (preact * sigma).astype(act_ref.dtype)
    slope = sigma * (1.0 + preact * (1.0 - sigma))
    pre_grad = (cot_ref[...].astype(jnp.float32) * slope).astype(jnp.bfloat16)
    pre_grad_ref[...] = pre_grad
    grad_ref[...] = lax.dot_general(
        pre_grad, weight, (((1,), (1,)), ((), ())), preferred_element_type=jnp.float32
    ).astype(jnp.bfloat16)


def middle(pieces, cotangent, weight):
    rows, width = cotangent.shape
    return pl.pallas_call(
        middle_kernel,
        out_shape=[like((rows, width), jnp.bfloat16)] * 4,
        in_specs=[WHOLE] * (2 + len(pieces)),
        out_specs=[WHOLE] * 4,
        compiler_params=params(8),
        cost_estimate=pl.CostEstimate(
            flops=4 * rows * width * width, bytes_accessed=10 * rows * width, transcendentals=rows * width),
        name="middle",
    )(*pieces, cotangent, weight)


def weight_kernel(place_ref, agg_ref, pre_grad_ref, *refs, groups):
    owns, send_ref, part_ref = refs[:groups], refs[groups], refs[groups + 1]
    core = place_ref[0] & 1
    rows = owns[0].shape[0]
    part_ref[...] = lax.dot_general(
        agg_ref[...], pre_grad_ref[...], (((0,), (0,)), ((), ())), preferred_element_type=jnp.float32
    )

    def piece(k, side):
        start = (2 * k + side) * rows
        return part_ref[pl.ds(pl.multiple_of(start, rows), rows), :]

    for k in range(groups):
        owns[k][...] = piece(k, core)
        send_ref[k * rows:(k + 1) * rows, :] = piece(k, 1 - core).astype(send_ref.dtype)


def weight_part(agg, pre_grad, place, groups):
    rows, width = agg.shape
    part = width // (2 * groups)
    out = pl.pallas_call(
        functools.partial(weight_kernel, groups=groups),
        out_shape=[like((part, width), jnp.float32)] * groups + [like((groups * part, width), jnp.bfloat16)],
        in_specs=[SCALARS, WHOLE, WHOLE],
        out_specs=[WHOLE] * (groups + 1),
        scratch_shapes=[pltpu.VMEM((width, width), jnp.float32)],
        compiler_params=params(8),
        cost_estimate=pl.CostEstimate(
            flops=2 * rows * width * width, bytes_accessed=4 * rows * width + 4 * width * width, transcendentals=0),
        name="weight_part",
    )(place, agg, pre_grad)
    return out[:-1], out[-1]


def place_kernel(place_ref, *refs, groups):
    owns, other_ref, out_ref = refs[:groups], refs[groups], refs[groups + 1]
    core, member = place_ref[0] & 1, place_ref[1]
    rows = owns[0].shape[0]
    bits = bit_count(groups)
    for k in range(groups):
        for side, value in ((core, owns[k][...]), (1 - core, other_ref[k * rows:(k + 1) * rows, :])):
            start = (2 * (member ^ between(k, 1 - side, bits)) + side) * rows
            out_ref[pl.ds(pl.multiple_of(start, rows), rows), :] = value


def place_slices(owns, other, place):
    groups = len(owns)
    rows, width = owns[0].shape
    return pl.pallas_call(
        functools.partial(place_kernel, groups=groups),
        out_shape=like((2 * groups * rows, width), jnp.float32),
        in_specs=[SCALARS] + [WHOLE] * (groups + 1),
        out_specs=WHOLE,
        compiler_params=params(8),
        cost_estimate=pl.CostEstimate(flops=0, bytes_accessed=16 * groups * rows * width, transcendentals=0),
        name="place_slices",
    )(place, *owns, other)


def backward_kernel(*refs, side, count, slots):
    blocks, grads, outs = refs[:count], refs[count:count + slots], refs[count + slots:]
    rows = blocks[0].shape[1]
    for i, block in enumerate(blocks):
        total, start = None, 0
        for grad in grads:
            stop = start + grad.shape[0]
            part = bf16_dot(block[side, :, start:stop], grad[...])
            total, start = part if total is None else total + part, stop
        if side:
            outs[0][i * rows:(i + 1) * rows, :] = total.astype(outs[0].dtype)
        else:
            outs[i][...] = total


def backward(blocks, grads, side):
    _, cols, rows = blocks[0].shape
    width = grads[0].shape[1]
    count = len(blocks)
    own = [like((cols, width), jnp.float32)] * count
    return pl.pallas_call(
        functools.partial(backward_kernel, side=side, count=count, slots=len(grads)),
        out_shape=[like((count * cols, width), jnp.bfloat16)] if side else own,
        in_specs=[WHOLE] * (count + len(grads)),
        out_specs=[WHOLE] * (1 if side else count),
        compiler_params=params(8),
        cost_estimate=pl.CostEstimate(
            flops=2 * count * cols * rows * width,
            bytes_accessed=2 * count * cols * rows + 2 * rows * width + 4 * count * cols * width, transcendentals=0),
        name="backward",
    )(*blocks, *grads)


def settle_kernel(*refs, slots, count):
    totals, arrived, outs = refs[:slots], refs[slots:slots + count], refs[slots + count:]
    rows = totals[0].shape[0]
    for k in range(slots):
        total = totals[k][...]
        for ref in arrived:
            total = total + ref[k * rows:(k + 1) * rows, :].astype(jnp.float32)
        outs[k][...] = total.astype(outs[k].dtype)


def settle(totals, arrived, dtypes):
    rows, width = totals[0].shape
    return pl.pallas_call(
        functools.partial(settle_kernel, slots=len(totals), count=len(arrived)),
        out_shape=[like((rows, width), dtype) for dtype in dtypes],
        in_specs=[WHOLE] * (len(totals) + len(arrived)),
        out_specs=[WHOLE] * len(totals),
        compiler_params=params(8),
        cost_estimate=pl.CostEstimate(flops=rows * width, bytes_accessed=8 * rows * width, transcendentals=0),
        name="settle",
    )(*totals, *arrived)


def top_bit(slot):
    return 1 << (slot.bit_length() - 1)


def halve(totals, swap):
    while True:
        half = len(totals) // 2
        send = [total.astype(jnp.bfloat16) for total in totals[half:]]
        got = swap(jnp.concatenate(send) if half > 1 else send[0], half)
        if half == 1:
            return [totals[0], got]
        totals = add_slots(totals[:half], got)


def add_slots(totals, got):
    rows = totals[0].shape[0]
    return [total + got[k * rows:(k + 1) * rows].astype(jnp.float32) for k, total in enumerate(totals)]


def collect(totals, swap):
    totals = list(totals)
    arrived = []
    for k in reversed(range(1, len(totals))):
        got = swap(totals[k].astype(jnp.bfloat16), top_bit(k))
        if k == top_bit(k):
            arrived.append(got)
        else:
            totals[k - top_bit(k)] = totals[k - top_bit(k)].astype(jnp.float32) + got.astype(jnp.float32)
    return [totals[0], *arrived]


def local(features, cotangent, weight, tiles, tile_rows, tile_cols, tile_counts):
    blocks = lax.axis_size("dom")
    groups = lax.axis_size("repl")
    chips = blocks // 2
    rows_local, width = features.shape
    scale = float(rows_local * blocks * groups) ** (-0.5)
    position, member = lax.axis_index("dom"), lax.axis_index("repl")
    place = jnp.stack([position, member]).astype(jnp.int32)

    col_tiles = rows_local // tiles.shape[-1]
    row = tile_rows[0, 0]
    row = between((row // col_tiles) ^ member, position & 1, bit_count(groups)) * col_tiles + row % col_tiles
    spots = jnp.concatenate([row * col_tiles + tile_cols[0, 0], tile_counts[0, 0][:, None]], axis=1)
    dense = densify(tiles[0, 0], spots, place, groups, rows_local)

    held = [features]
    for k in range(1, chips):
        given = after(features, held[k - 1]) if k == top_bit(k) > 1 else held[k - top_bit(k)]
        held.append(swap_chips(given, top_bit(k)))
        if k == 1:
            held[1] = after(held[1], spots)
    half, upper = chips // 2, groups // 2
    sources = [x for own in held[:half] for x in (own, swap_cores(own))]
    totals = forward(dense, list(range(2 * half)), sources, 0, None, [jnp.float32] * groups)
    far = [after(own, *totals) for own in held[half:]]
    others = [swap_cores(own) for own in far]
    totals = forward(dense, list(range(2 * half, 2 * chips, 2)), far, 0, totals, [jnp.float32] * groups)
    odd = list(range(2 * half + 1, 2 * chips, 2))
    high = forward(dense, odd, others, upper, totals[upper:], [jnp.bfloat16] * upper)
    low = forward(after(dense, *high), odd, others, 0, totals[:upper], [jnp.float32] * upper)
    totals = low + high

    pieces = collect(totals, swap_members)
    dense_t = transposed(after(dense, *totals, pieces[1]))
    pieces[-1] = after(pieces[-1], *dense_t)
    activated, agg, pre_grad, grad = middle(pieces, cotangent, weight)
    owns, send = weight_part(agg, pre_grad, place, groups)
    parts = add_slots(owns, swap_cores(send))

    grads = [grad]
    for k in range(1, groups):
        grads.append(swap_members(grads[k - top_bit(k)], top_bit(k)))
    parts = jnp.concatenate(parts).astype(jnp.bfloat16).reshape(groups, -1, width)
    parts = lax.all_to_all(parts, "repl", 0, 0).astype(jnp.float32)
    part = sum(parts[k] for k in range(groups)).astype(jnp.bfloat16)
    near = swap_chips(part, 1)
    part = part.astype(jnp.float32) + near.astype(jnp.float32)
    grads[-1] = after(grads[-1], near)

    half = chips // 2
    other = backward(dense_t[half:], grads, 1)
    own = backward([after(dense_t[half], *other), *dense_t[half + 1:]], grads, 0)
    high = jnp.concatenate(add_slots(own, swap_cores(other[0]))).astype(jnp.bfloat16)
    grads[0] = after(grads[0], high)
    other = backward(dense_t[:half], grads, 1)
    totals = backward(dense_t[:half], grads, 0)
    arrived = [swap_cores(other[0]), swap_chips(high, half)]
    while half > 1:
        half //= 2
        totals = settle(totals, arrived, [jnp.float32] * half + [jnp.bfloat16] * half)
        send = jnp.concatenate(totals[half:]) if half > 1 else totals[half]
        totals, arrived = totals[:half], [swap_chips(send, half)]
    (feature_grad,) = settle(totals, arrived, [jnp.bfloat16])

    bit = 2
    while bit < chips:
        part = part.astype(jnp.bfloat16)
        part = part.astype(jnp.float32) + swap_chips(part, bit).astype(jnp.float32)
        bit *= 2
    part = part * scale
    parts = [part] + [swap_members(part, k, turn=1) for k in range(1, groups)]
    weight_grad = place_slices(parts, swap_cores(jnp.concatenate(parts)), place)
    return (activated, feature_grad, weight_grad)


def solution(mesh):
    in_specs = (
        P(("dom", "repl"), None),
        P(("dom", "repl"), None),
        P(),
        P("dom", "repl", None, None, None, None),
        P("dom", "repl", None, None),
        P("dom", "repl", None, None),
        P("dom", "repl", None),
    )
    out_specs = (P(("dom", "repl"), None), P(("dom", "repl"), None), P())
    return jax.shard_map(local, mesh=mesh, in_specs=in_specs, out_specs=out_specs, check_vma=False)
```

```python
import functools

import jax
import jax.numpy as jnp
from jax import lax
from jax.experimental import pallas as pl
from jax.experimental.pallas import tpu as pltpu
from jax.sharding import PartitionSpec as P

WHOLE = pl.BlockSpec(memory_space=pltpu.VMEM)
SCALARS = pl.BlockSpec(memory_space=pltpu.SMEM)


def bit_count(n):
    return n.bit_length() - 1


def between(index, core, bits):
    reverse = 0
    for i in range(bits):
        reverse = reverse | (((index >> i) & 1) << (bits - 1 - i))
    return core * index + (1 - core) * reverse


def swap_cores(x):
    return lax.ppermute(x, "dom", [(i, i ^ 1) for i in range(lax.axis_size("dom"))])


def swap_chips(x, held):
    blocks = lax.axis_size("dom")
    bits = bit_count(blocks // 2)
    return lax.ppermute(x, "dom", [(i, i ^ (2 * between(held, i % 2, bits))) for i in range(blocks)])


def swap_line(x, mask):
    return lax.ppermute(x, "dom", [(i, i ^ (2 * mask)) for i in range(lax.axis_size("dom"))])


def swap_members(x, held, turn=0):
    blocks, groups = lax.axis_size("dom"), lax.axis_size("repl")
    bits = bit_count(groups)
    pairs = []
    for i in range(blocks):
        for j in range(groups):
            pairs.append((i * groups + j, i * groups + (j ^ between(held, (i % 2) ^ turn, bits))))
    return lax.ppermute(x, ("dom", "repl"), pairs)


def after(x, *others):
    return lax.optimization_barrier((x, *others))[0]


def params(mib):
    return pltpu.CompilerParams(vmem_limit_bytes=mib * 1024 * 1024)


def like(shape, dtype):
    return jax.ShapeDtypeStruct(shape, dtype)


def bf16_dot(a, b):
    return jnp.dot(a, b, preferred_element_type=jnp.float32)


def column_of(position, j, blocks):
    core = (position & 1) ^ (j & 1)
    return (((position >> 1) ^ between(j >> 1, core, bit_count(blocks // 2))) << 1) | core


def densify_kernel(spots_ref, place_ref, tiles_ref, a_ref, acc_ref, *, col_tiles):
    column = column_of(place_ref[0], pl.program_id(0), pl.num_programs(0))
    size = tiles_ref.shape[-1]
    count = tiles_ref.shape[1]
    acc_ref[...] = jnp.zeros_like(acc_ref)

    def add(tile, carry):
        acc_ref[spots_ref[column, tile]] += tiles_ref[0, tile].astype(jnp.float32)
        return carry

    lax.fori_loop(0, spots_ref[column, count], add, 0)
    for spot in range(acc_ref.shape[0]):
        row, col = spot // col_tiles, spot % col_tiles
        a_ref[0, row * size:(row + 1) * size, col * size:(col + 1) * size] = acc_ref[spot].astype(a_ref.dtype)


def densify(tiles, spots, place, group_count, rows_local):
    columns, count, size, _ = tiles.shape
    col_tiles = rows_local // size
    rows = group_count * rows_local
    return pl.pallas_call(
        functools.partial(densify_kernel, col_tiles=col_tiles),
        out_shape=like((columns, rows, rows_local), jnp.bfloat16),
        grid_spec=pltpu.PrefetchScalarGridSpec(
            num_scalar_prefetch=2,
            grid=(columns,),
            in_specs=[pl.BlockSpec((1, count, size, size), lambda j, s, p: (column_of(p[0], j, columns), 0, 0, 0))],
            out_specs=pl.BlockSpec((1, rows, rows_local), lambda j, *_: (j, 0, 0)),
            scratch_shapes=[pltpu.VMEM((group_count * col_tiles * col_tiles, size, size), jnp.float32)],
        ),
        compiler_params=params(12),
        cost_estimate=pl.CostEstimate(
            flops=columns * count * size * size, bytes_accessed=8 * rows * columns * rows_local, transcendentals=0),
        name="densify",
    )(spots, place, tiles)


def transpose_kernel(a_ref, *outs):
    for i, out_ref in enumerate(outs):
        for side in range(2):
            out_ref[side] = a_ref[2 * i + side].T


def transposed(dense):
    columns, rows, cols = dense.shape
    return pl.pallas_call(
        transpose_kernel,
        out_shape=[like((2, cols, rows), jnp.bfloat16)] * (columns // 2),
        in_specs=[WHOLE],
        out_specs=[WHOLE] * (columns // 2),
        compiler_params=params(8),
        cost_estimate=pl.CostEstimate(flops=0, bytes_accessed=4 * columns * rows * cols, transcendentals=0),
        name="transposed",
    )(dense)


def forward_kernel(*refs, which, base, slots, has_prev):
    count = len(which)
    dense_ref, sources = refs[0], refs[1:1 + count]
    rest = refs[1 + count:]
    prev, outs = (rest[:slots], rest[slots:]) if has_prev else (None, rest)
    rows = outs[0].shape[0]
    for k, out_ref in reversed(list(enumerate(outs))):
        total = prev[k][...] if has_prev else None
        for j, source in zip(which, sources):
            part = bf16_dot(dense_ref[j, (base + k) * rows:(base + k + 1) * rows, :], source[...])
            total = part if total is None else total + part
        out_ref[...] = total.astype(out_ref.dtype)


def forward(dense, which, sources, base, prev, dtypes):
    slots = len(dtypes)
    depth, width = sources[0].shape
    rows = slots * depth
    return pl.pallas_call(
        functools.partial(
            forward_kernel, which=which, base=base, slots=slots, has_prev=prev is not None),
        out_shape=[like((depth, width), dtype) for dtype in dtypes],
        in_specs=[WHOLE] * (1 + len(sources) + (slots if prev is not None else 0)),
        out_specs=[WHOLE] * slots,
        compiler_params=params(8),
        cost_estimate=pl.CostEstimate(
            flops=2 * len(sources) * rows * depth * width,
            bytes_accessed=2 * len(sources) * rows * depth + 4 * rows * width, transcendentals=0),
        name="forward",
    )(dense, *sources, *(prev or []))


def middle_kernel(*refs):
    pieces, (cot_ref, weight_ref, act_ref, agg_ref, pre_grad_ref, grad_ref) = refs[:-6], refs[-6:]
    agg = pieces[0][...]
    for piece in pieces[1:]:
        agg = agg + piece[...].astype(jnp.float32)
    agg = agg.astype(jnp.bfloat16)
    agg_ref[...] = agg
    weight = weight_ref[...]
    preact = bf16_dot(agg, weight)
    sigma = jax.nn.sigmoid(preact)
    act_ref[...] = (preact * sigma).astype(act_ref.dtype)
    slope = sigma * (1.0 + preact * (1.0 - sigma))
    pre_grad = (cot_ref[...].astype(jnp.float32) * slope).astype(jnp.bfloat16)
    pre_grad_ref[...] = pre_grad
    grad_ref[...] = lax.dot_general(
        pre_grad, weight, (((1,), (1,)), ((), ())), preferred_element_type=jnp.float32
    ).astype(jnp.bfloat16)


def middle(pieces, cotangent, weight):
    rows, width = cotangent.shape
    return pl.pallas_call(
        middle_kernel,
        out_shape=[like((rows, width), jnp.bfloat16)] * 4,
        in_specs=[WHOLE] * (2 + len(pieces)),
        out_specs=[WHOLE] * 4,
        compiler_params=params(8),
        cost_estimate=pl.CostEstimate(
            flops=4 * rows * width * width, bytes_accessed=10 * rows * width, transcendentals=rows * width),
        name="middle",
    )(*pieces, cotangent, weight)


def weight_kernel(place_ref, agg_ref, pre_grad_ref, *refs, groups):
    owns, send_ref, part_ref = refs[:groups], refs[groups], refs[groups + 1]
    core, member = place_ref[0] & 1, place_ref[1]
    rows = owns[0].shape[0]
    bits = bit_count(groups)
    part_ref[...] = lax.dot_general(
        agg_ref[...], pre_grad_ref[...], (((0,), (0,)), ((), ())), preferred_element_type=jnp.float32
    )

    def piece(k, side):
        start = (2 * (member ^ between(k, 1 - side, bits)) + side) * rows
        return part_ref[pl.ds(pl.multiple_of(start, rows), rows), :]

    for k in range(groups):
        owns[k][...] = piece(k, core)
        send_ref[k * rows:(k + 1) * rows, :] = piece(k, 1 - core).astype(send_ref.dtype)


def weight_part(agg, pre_grad, place, groups):
    rows, width = agg.shape
    part = width // (2 * groups)
    out = pl.pallas_call(
        functools.partial(weight_kernel, groups=groups),
        out_shape=[like((part, width), jnp.float32)] * groups + [like((groups * part, width), jnp.bfloat16)],
        in_specs=[SCALARS, WHOLE, WHOLE],
        out_specs=[WHOLE] * (groups + 1),
        scratch_shapes=[pltpu.VMEM((width, width), jnp.float32)],
        compiler_params=params(8),
        cost_estimate=pl.CostEstimate(
            flops=2 * rows * width * width, bytes_accessed=4 * rows * width + 4 * width * width, transcendentals=0),
        name="weight_part",
    )(place, agg, pre_grad)
    return out[:-1], out[-1]


def place_kernel(place_ref, *refs, groups):
    owns, other_ref, out_ref = refs[:groups], refs[groups], refs[groups + 1]
    core, member = place_ref[0] & 1, place_ref[1]
    rows = owns[0].shape[0]
    bits = bit_count(groups)
    for k in range(groups):
        for side, value in ((core, owns[k][...]), (1 - core, other_ref[k * rows:(k + 1) * rows, :])):
            start = (2 * (member ^ between(k, 1 - side, bits)) + side) * rows
            out_ref[pl.ds(pl.multiple_of(start, rows), rows), :] = value


def place_slices(owns, other, place):
    groups = len(owns)
    rows, width = owns[0].shape
    return pl.pallas_call(
        functools.partial(place_kernel, groups=groups),
        out_shape=like((2 * groups * rows, width), jnp.float32),
        in_specs=[SCALARS] + [WHOLE] * (groups + 1),
        out_specs=WHOLE,
        compiler_params=params(8),
        cost_estimate=pl.CostEstimate(flops=0, bytes_accessed=16 * groups * rows * width, transcendentals=0),
        name="place_slices",
    )(place, *owns, other)


def backward_kernel(*refs, side, count, slots):
    blocks, grads, outs = refs[:count], refs[count:count + slots], refs[count + slots:]
    rows = blocks[0].shape[1]
    for i, block in enumerate(blocks):
        total, start = None, 0
        for grad in grads:
            stop = start + grad.shape[0]
            part = bf16_dot(block[side, :, start:stop], grad[...])
            total, start = part if total is None else total + part, stop
        if side:
            outs[0][i * rows:(i + 1) * rows, :] = total.astype(outs[0].dtype)
        else:
            outs[i][...] = total


def backward(blocks, grads, side):
    _, cols, rows = blocks[0].shape
    width = grads[0].shape[1]
    count = len(blocks)
    own = [like((cols, width), jnp.float32)] * count
    return pl.pallas_call(
        functools.partial(backward_kernel, side=side, count=count, slots=len(grads)),
        out_shape=[like((count * cols, width), jnp.bfloat16)] if side else own,
        in_specs=[WHOLE] * (count + len(grads)),
        out_specs=[WHOLE] * (1 if side else count),
        compiler_params=params(8),
        cost_estimate=pl.CostEstimate(
            flops=2 * count * cols * rows * width,
            bytes_accessed=2 * count * cols * rows + 2 * rows * width + 4 * count * cols * width, transcendentals=0),
        name="backward",
    )(*blocks, *grads)


def settle_kernel(*refs, slots, count):
    totals, arrived, outs = refs[:slots], refs[slots:slots + count], refs[slots + count:]
    rows = totals[0].shape[0]
    for k in range(slots):
        total = totals[k][...]
        for ref in arrived:
            total = total + ref[k * rows:(k + 1) * rows, :].astype(jnp.float32)
        outs[k][...] = total.astype(outs[k].dtype)


def settle(totals, arrived, dtypes):
    rows, width = totals[0].shape
    return pl.pallas_call(
        functools.partial(settle_kernel, slots=len(totals), count=len(arrived)),
        out_shape=[like((rows, width), dtype) for dtype in dtypes],
        in_specs=[WHOLE] * (len(totals) + len(arrived)),
        out_specs=[WHOLE] * len(totals),
        compiler_params=params(8),
        cost_estimate=pl.CostEstimate(flops=rows * width, bytes_accessed=8 * rows * width, transcendentals=0),
        name="settle",
    )(*totals, *arrived)


def top_bit(slot):
    return 1 << (slot.bit_length() - 1)


def halve(totals, swap):
    while True:
        half = len(totals) // 2
        send = [total.astype(jnp.bfloat16) for total in totals[half:]]
        got = swap(jnp.concatenate(send) if half > 1 else send[0], half)
        if half == 1:
            return [totals[0], got]
        totals = add_slots(totals[:half], got)


def add_slots(totals, got):
    rows = totals[0].shape[0]
    return [total + got[k * rows:(k + 1) * rows].astype(jnp.float32) for k, total in enumerate(totals)]


def collect(totals, swap):
    totals = list(totals)
    arrived = []
    for k in reversed(range(1, len(totals))):
        got = swap(totals[k].astype(jnp.bfloat16), top_bit(k))
        if k == top_bit(k):
            arrived.append(got)
        else:
            totals[k - top_bit(k)] = totals[k - top_bit(k)].astype(jnp.float32) + got.astype(jnp.float32)
    return [totals[0], *arrived]


def local(features, cotangent, weight, tiles, tile_rows, tile_cols, tile_counts):
    blocks = lax.axis_size("dom")
    groups = lax.axis_size("repl")
    chips = blocks // 2
    rows_local, width = features.shape
    scale = float(rows_local * blocks * groups) ** (-0.5)
    position, member = lax.axis_index("dom"), lax.axis_index("repl")
    place = jnp.stack([position, member]).astype(jnp.int32)

    col_tiles = rows_local // tiles.shape[-1]
    row = tile_rows[0, 0]
    row = between((row // col_tiles) ^ member, position & 1, bit_count(groups)) * col_tiles + row % col_tiles
    spots = jnp.concatenate([row * col_tiles + tile_cols[0, 0], tile_counts[0, 0][:, None]], axis=1)
    dense = densify(tiles[0, 0], spots, place, groups, rows_local)

    held = [features]
    for k in range(1, chips):
        given = after(features, held[k - 1]) if k == top_bit(k) > 1 else held[k - top_bit(k)]
        held.append(swap_chips(given, top_bit(k)))
        if k == 1:
            held[1] = after(held[1], spots)
    half, upper = chips // 2, groups // 2
    sources = [x for own in held[:half] for x in (own, swap_cores(own))]
    totals = forward(dense, list(range(2 * half)), sources, 0, None, [jnp.float32] * groups)
    far = [after(own, *totals) for own in held[half:]]
    others = [swap_cores(own) for own in far]
    totals = forward(dense, list(range(2 * half, 2 * chips, 2)), far, 0, totals, [jnp.float32] * groups)
    odd = list(range(2 * half + 1, 2 * chips, 2))
    high = forward(dense, odd, others, upper, totals[upper:], [jnp.bfloat16] * upper)
    low = forward(after(dense, *high), odd, others, 0, totals[:upper], [jnp.float32] * upper)
    totals = low + high

    pieces = collect(totals, swap_members)
    dense_t = transposed(after(dense, *totals, pieces[1]))
    pieces[-1] = after(pieces[-1], *dense_t)
    activated, agg, pre_grad, grad = middle(pieces, cotangent, weight)
    owns, send = weight_part(agg, pre_grad, place, groups)
    parts = add_slots(owns, swap_cores(send))

    grads = [grad]
    for k in range(1, groups):
        grads.append(swap_members(grads[k - top_bit(k)], top_bit(k)))
    part = parts[0]
    for k in range(1, groups):
        part = part + swap_members(parts[k].astype(jnp.bfloat16), k, turn=1).astype(jnp.float32)
    part = part.astype(jnp.bfloat16)
    near = swap_line(part, 1)
    part = part.astype(jnp.float32) + near.astype(jnp.float32)
    grads[-1] = after(grads[-1], near)

    half = chips // 2
    other = backward(dense_t[half:], grads, 1)
    own = backward([after(dense_t[half], *other), *dense_t[half + 1:]], grads, 0)
    high = jnp.concatenate(add_slots(own, swap_cores(other[0]))).astype(jnp.bfloat16)
    grads[0] = after(grads[0], high)
    other = backward(dense_t[:half], grads, 1)
    totals = backward(dense_t[:half], grads, 0)
    arrived = [swap_cores(other[0]), swap_chips(high, half)]
    while half > 1:
        half //= 2
        totals = settle(totals, arrived, [jnp.float32] * half + [jnp.bfloat16] * half)
        send = jnp.concatenate(totals[half:]) if half > 1 else totals[half]
        totals, arrived = totals[:half], [swap_chips(send, half)]
    (feature_grad,) = settle(totals, arrived, [jnp.bfloat16])

    bit = 2
    while bit < chips:
        part = part.astype(jnp.bfloat16)
        part = part.astype(jnp.float32) + swap_line(part, bit).astype(jnp.float32)
        bit *= 2
    part = part * scale
    parts = [part] + [swap_members(part, k, turn=1) for k in range(1, groups)]
    weight_grad = place_slices(parts, swap_cores(jnp.concatenate(parts)), place)
    return (activated, feature_grad, weight_grad)


def solution(mesh):
    in_specs = (
        P(("dom", "repl"), None),
        P(("dom", "repl"), None),
        P(),
        P("dom", "repl", None, None, None, None),
        P("dom", "repl", None, None),
        P("dom", "repl", None, None),
        P("dom", "repl", None),
    )
    out_specs = (P(("dom", "repl"), None), P(("dom", "repl"), None), P())
    return jax.shard_map(local, mesh=mesh, in_specs=in_specs, out_specs=out_specs, check_vma=False)
```
